32 devices in a mesh: section: 2 (over core), ctx: 4 (over z), fsdp: 4 (over y, x).
Axes of the slice: x: 2, y: 2, z: 4, core: 2. Of those that a mesh axis runs over, the one named last changes fastest.
Arguments:
- tokens: bfloat16 [2, 8, 1024, 1024], P(None, 'fsdp', 'ctx'), as said below
- segment_ids: int32 [2, 8, 1024], P(None, 'fsdp', 'ctx'), may hold values from 0 to 1023, as said below
- valid_mask: int32 [2, 8, 1024], P(None, 'fsdp', 'ctx'), may hold values from 0 to 1, as said below
- cotangent: bfloat16 [2, 8, 1024, 1024], P(None, 'fsdp', 'ctx'), may hold values from -6 to 6
- qkv_weight: bfloat16 [2, 3, 1024, 1024], P('section', None, ('ctx', 'fsdp')), may hold values from -0.1875 to 0.1875
- out_proj: bfloat16 [2, 1024, 1024], P('section', ('ctx', 'fsdp')), may hold values from -0.75 to 0.75
- in_weight: bfloat16 [2, 1024, 4096], P('section', ('ctx', 'fsdp')), may hold values from -0.1875 to 0.1875
- out_weight: bfloat16 [2, 4096, 1024], P('section', ('ctx', 'fsdp')), may hold values from -0.09375 to 0.09375
- norm_gain: float32 [2, 2, 1024], P('section'), may hold values from 0.5 to 1.5
- norm_shift: float32 [2, 2, 1024], P('section'), may hold values from -4 to 4
- proj_bias: float32 [2, 4, 1024], P('section'), may hold values from -4 to 4
- ff_bias: float32 [2, 4096], P('section'), may hold values from -6 to 6
Outputs:
- activations: bfloat16 [2, 2, 8, 1024, 1024], P('section', None, 'fsdp', 'ctx')
- input_grads: bfloat16 [2, 2, 8, 1024, 1024], P('section', None, 'fsdp', 'ctx')
- grad_qkv: float32 [2, 3, 1024, 1024], P('section', None, ('ctx', 'fsdp'))
- grad_out_proj: float32 [2, 1024, 1024], P('section', ('ctx', 'fsdp'))
- grad_in: float32 [2, 1024, 4096], P('section', ('ctx', 'fsdp'))
- grad_out: float32 [2, 4096, 1024], P('section', ('ctx', 'fsdp'))
- grad_gain: float32 [2, 2, 1024], P('section', None, ('ctx', 'fsdp'))
- grad_shift: float32 [2, 2, 1024], P('section', None, ('ctx', 'fsdp'))
- grad_proj_bias: float32 [2, 4, 1024], P('section', None, ('ctx', 'fsdp'))
- grad_ff_bias: float32 [2, 4096], P('section', ('ctx', 'fsdp'))
- rms: float32 [2, 4], P('section')
The draws below stay inside these ranges and needn't reach their ends.
Inputs may be any that keep to these rules, and one draw needn't show every extreme that they name: `tokens`: activations of order one. `segment_ids`: ids never fall along a sequence; a document is a run of equal ids; the last position of each sequence has 1023. Among the 4 sequences of one fsdp index one is a single document without padding. `valid_mask`: each sequence's real tokens are a leading run of at least 3 / 8 of its positions.
All inputs are finite; a program needn't handle non-finite values.
Results may differ from the reference program's by a relative error of at most 0.017.
Values may be sent and summed in bfloat16 or wider, within the bound.
No kernel may reach another device: no remote copies, remote signals or barrier semaphores. Data moves between devices by JAX's collectives and lax.ppermute only.
A program may use at most 384 MiB of HBM per device.

```python
import jax
import jax.numpy as jnp
from jax import lax

D = 1024
HEADS = 16
FF = 4096
LEN = 1024
MICRO = 2
SEQS = 2
NSEQ = 8


def packing(key):
    starts_key = jax.random.fold_in(key, 101)
    level_key = jax.random.fold_in(key, 102)
    pad_key = jax.random.fold_in(key, 103)
    whole_key = jax.random.fold_in(key, 104)
    start_level = jax.random.randint(level_key, (MICRO, NSEQ, 1), 2, 9)
    raw_draw = jax.random.randint(starts_key, (MICRO, NSEQ, LEN), 0, 512)
    document_starts = (raw_draw < jnp.left_shift(1, 9 - start_level)).astype(jnp.int32)
    padding = jax.random.randint(pad_key, (MICRO, NSEQ, 1), 0, 5 * LEN // 8 + 1)
    group_count = NSEQ // SEQS
    chosen_seq = jax.random.randint(whole_key, (group_count,), 0, MICRO * SEQS)
    micro_ids = jnp.arange(MICRO)[:, None]
    seq_ids = jnp.arange(NSEQ)[None, :]
    whole_seq = micro_ids * SEQS + seq_ids % SEQS == chosen_seq[seq_ids // SEQS]
    position = jnp.arange(LEN)[None, None, :]
    document_starts = jnp.where(whole_seq[..., None] | (position == 0), 0, document_starts)
    padding = jnp.where(whole_seq[..., None], 0, padding)
    running = jnp.cumsum(document_starts, axis=-1)
    seg_rows = LEN - 1 - (running[..., -1:] - running)
    valid_rows = (position < LEN - padding).astype(jnp.int32)
    return (seg_rows.astype(jnp.int32), valid_rows)


def draw_segment_ids(key, part):
    seg_rows, valid_rows = packing(key)
    return seg_rows


def draw_valid_mask(key, part):
    seg_rows, valid_rows = packing(key)
    return valid_rows


def draw_tokens(key, part):
    key = jax.random.fold_in(key, 11)
    noise_key = jax.random.fold_in(key, 1)
    shape = (MICRO, NSEQ, LEN, D)
    position = jnp.arange(LEN).astype(jnp.float32) / LEN
    ramp = (0.6 + 0.9 * position)[None, None, :, None]
    values = jax.random.normal(noise_key, shape, jnp.float32) * ramp
    return jnp.clip(values, -6.0, 6.0).astype(jnp.bfloat16)


def raised(values, key, source, target, shards_of, factor):
    def block_of(dim):
        return (jnp.arange(values.shape[dim]) // (values.shape[dim] // shards_of)).reshape((-1,) + (1,) * (values.ndim - 1 - dim))

    near = jax.random.permutation(key, shards_of)[block_of(target)]
    other_side = (block_of(target) + shards_of // 2) % shards_of
    return jnp.where((block_of(source) == near) | (block_of(source) == other_side), factor * values, values)


def steps_of(own_key, shape, split, low, top_value):
    level, own = 1.0, jax.random.fold_in(own_key, 6)
    for axis_at, parts in split:
        heights = jnp.exp(jax.random.uniform(jax.random.fold_in(own, axis_at), (parts,), jnp.float32, low / len(split), top_value / len(split)))
        level = level * jnp.repeat(heights, shape[axis_at] // parts).reshape([-1 if axis == axis_at else 1 for axis in range(len(shape))])
    return level


def gaussian(stream_key, extent, scale, limit, pieces=(), kind=jnp.bfloat16):
    drawn = jax.random.normal(stream_key, extent, jnp.float32) * scale
    if len(pieces) > 0:
        drawn = steps_of(stream_key, extent, pieces, -0.22, 0.18) * drawn
    return jnp.clip(drawn, min=-limit, max=limit).astype(kind)


def bell_draw_with(stream_key, dims, scale, bound, split, heavy, kind=jnp.bfloat16):
    entries = scale * jax.random.normal(stream_key, dims, jnp.float32)
    if split:
        entries = entries * steps_of(stream_key, dims, split, -0.22, 0.18)
    return jnp.clip(raised(entries, jax.random.fold_in(stream_key, 3), *heavy), -bound, bound).astype(kind)


def setup_inputs(seed: int = 0) -> dict:
    streams_of = jax.random.split(jax.random.key(seed), 13)
    return {
        "tokens": draw_tokens(jax.random.fold_in(streams_of[12], 71), 0),
        "segment_ids": draw_segment_ids(jax.random.fold_in(streams_of[12], 71), 0),
        "valid_mask": draw_valid_mask(jax.random.fold_in(streams_of[12], 71), 0),
        "cotangent": bell_draw_with(streams_of[3], (MICRO, NSEQ, LEN, D), 1.0, 6.0, ((1, 4), (2, 4)), (1, 3, 4, 2.0)),
        "qkv_weight": gaussian(streams_of[4], (2, 3, D, D), D ** -0.5, 0.1875, ((0, 2), (2, 16))),
        "out_proj": gaussian(streams_of[5], (2, D, D), (D // 16) ** -0.5, 0.75, ((0, 2), (1, 16))),
        "in_weight": gaussian(streams_of[6], (2, D, FF), D ** -0.5, 0.1875, ((0, 2), (1, 16))),
        "out_weight": gaussian(streams_of[7], (2, FF, D), FF ** -0.5, 0.09375, ((0, 2), (1, 16))),
        "norm_gain": jnp.clip(1.0 + 0.1 * jax.random.normal(streams_of[8], (2, 2, D), jnp.float32), 0.5, 1.5),
        "norm_shift": gaussian(streams_of[9], (2, 2, D), 0.3, 4.0, ((0, 2),), jnp.float32),
        "proj_bias": gaussian(streams_of[10], (2, 4, D), 0.3, 4.0, ((0, 2),), jnp.float32),
        "ff_bias": gaussian(streams_of[11], (2, FF), 0.5, 6.0, ((0, 2),), jnp.float32),
    }


highest_precision = lax.Precision.HIGHEST
norm_eps = 1e-05
masked_score = -1e+30
group_seqs = 4

@jax.custom_vjp
def low(v):
    return lax.optimization_barrier(v.astype(jnp.bfloat16)).astype(jnp.float32)

@jax.custom_vjp
def low_back(v):
    return v

def low_keep(v):
    return (low(v), None)

def low_pass(kept, grad):
    return (grad,)

def back_keep(v):
    return (v, None)

def back_low(kept, grad):
    return (low(grad),)
low.defvjp(low_keep, low_pass)
low_back.defvjp(back_keep, back_low)

def normalize(residual, gain_row, shift_row):
    average = lax.optimization_barrier(jnp.mean(residual, axis=-1, keepdims=True))
    centred = residual - average
    spread = lax.optimization_barrier(jnp.mean(centred * centred, axis=-1, keepdims=True))
    return centred * lax.rsqrt(spread + norm_eps) * gain_row + shift_row

def project(operand_array, matrix_value):
    return jnp.einsum('bzf,fc->bzc', operand_array, matrix_value, precision=highest_precision)

def attend_one(packed):
    queries, key_rows, value_rows, seg_row, row_valid_flag = packed
    length = queries.shape[0]
    head_dim = D // HEADS
    query_heads = queries.reshape(length, HEADS, head_dim)
    key_heads = key_rows.reshape(length, HEADS, head_dim)
    value_heads = value_rows.reshape(length, HEADS, head_dim)
    scores = low_back(jnp.einsum('qhd,khd->hqk', query_heads, key_heads, precision=highest_precision) * head_dim ** (-0.5))
    position = jnp.arange(length)
    allowed = (seg_row[:, None] == seg_row[None, :]) & (row_valid_flag[None, :] == 1) | (position[:, None] == position[None, :])
    scores = jnp.where(allowed[None], scores, masked_score)
    probs = low(jax.nn.softmax(scores, axis=-1))
    mixed = jnp.einsum('hqk,khd->qhd', probs, value_heads, precision=highest_precision)
    return mixed.reshape(length, D)

def layer(layer_input, params, seg_rows, valid_rows):
    qkv, proj, w_in, w_out, gains, shifts, biases, ff_row = params
    queries = low_back(low(project(layer_input, qkv[0]) + biases[0]))
    key_rows = low_back(low(project(layer_input, qkv[1])))
    value_rows = low_back(low(project(layer_input, qkv[2]) + biases[1]))
    mixed = lax.map(jax.checkpoint(attend_one), (queries, key_rows, value_rows, seg_rows, valid_rows))
    mixed = low_back(low(mixed))
    branch_attn = low_back(project(mixed, proj) + biases[2])
    normed = normalize(layer_input + branch_attn, gains[0], shifts[0])
    hidden = low_back(project(low(normed), w_in) + ff_row)
    branch_ff = low_back(project(low(jax.nn.gelu(hidden, approximate=False)), w_out) + biases[3])
    output = normalize(normed + branch_ff, gains[1], shifts[1])
    column_valid = valid_rows.astype(jnp.float32)[..., None]
    squares = jnp.stack([jnp.sum(column_valid * member * member) for member in (layer_input, branch_attn, branch_ff, output)])
    return (output, squares)

def forward(first_params, second_params, layer_input, probe, seg_rows, valid_rows):
    first_out, first_squares = layer(layer_input, first_params, seg_rows, valid_rows)
    sent = low_back(low(first_out))
    second_out, second_squares = layer(sent + probe, second_params, seg_rows, valid_rows)
    return (second_out, (sent, jnp.stack([first_squares, second_squares])))

def reference(tokens, segment_ids, valid_mask, cotangent, qkv_weight, out_proj, in_weight, out_weight, norm_gain, norm_shift, proj_bias, ff_bias):
    weights = (qkv_weight, out_proj, in_weight, out_weight, norm_gain, norm_shift, proj_bias, ff_bias)
    first_params = tuple((member[0].astype(jnp.float32) for member in weights))
    second_params = tuple((member[1].astype(jnp.float32) for member in weights))
    block_count = MICRO * NSEQ // group_seqs

    def blocks(array):
        return array.reshape((block_count, group_seqs) + array.shape[2:])
    packed_all = (blocks(tokens.astype(jnp.float32)), blocks(segment_ids), blocks(valid_mask), blocks(cotangent.astype(jnp.float32)))

    def one_block(carry, packed):
        first_acc, second_acc, square_acc = carry
        block_tokens, block_segs, block_valid, block_cot = packed

        def run(first_p, second_p, layer_input, probe):
            return forward(first_p, second_p, layer_input, probe, block_segs, block_valid)
        probe = jnp.zeros_like(block_tokens)
        final_out, pull, aux = jax.vjp(run, first_params, second_params, block_tokens, probe, has_aux=True)
        sent, squares = aux
        grad_first, grad_second, grad_tokens, grad_probe = pull(block_cot)
        first_acc = jax.tree.map(jnp.add, first_acc, grad_first)
        second_acc = jax.tree.map(jnp.add, second_acc, grad_second)
        outputs = (sent.astype(jnp.bfloat16), final_out.astype(jnp.bfloat16), grad_tokens.astype(jnp.bfloat16), grad_probe.astype(jnp.bfloat16))
        return ((first_acc, second_acc, square_acc + squares), outputs)
    init = (jax.tree.map(jnp.zeros_like, first_params), jax.tree.map(jnp.zeros_like, second_params), jnp.zeros((2, 4), jnp.float32))
    (first_acc, second_acc, square_acc), outputs = lax.scan(one_block, init, packed_all)
    shaped = [member.reshape(MICRO, NSEQ, LEN, D) for member in outputs]
    activations = jnp.stack([shaped[0], shaped[1]])
    input_grads = jnp.stack([shaped[2], shaped[3]])
    grads = [jnp.stack([first_acc[index], second_acc[index]]) for index in range(8)]
    token_count = jnp.sum(valid_mask.astype(jnp.float32))
    rms = jnp.sqrt(square_acc / (token_count * D))
    return (activations, input_grads, grads[0], grads[1], grads[2], grads[3], grads[4], grads[5], grads[6], grads[7], rms)
```

```python
import math

import jax
import jax.numpy as jnp
from jax import lax
from jax.experimental import pallas as pl
from jax.experimental.pallas import tpu as pltpu
from jax.sharding import PartitionSpec as P

HEADS = 16
NORM_EPS = 1e-05
MASKED = -1e30
BF = jnp.bfloat16
F32 = jnp.float32
VMEM_LIMIT = 48 * 1024 * 1024


def nt_dot(a, b):
    return lax.dot_general(a, b, (((1,), (1,)), ((), ())), preferred_element_type=F32)


def nn_dot(a, b):
    return lax.dot_general(a, b, (((1,), (0,)), ((), ())), preferred_element_type=F32)


def tn_dot(a, b):
    return lax.dot_general(a, b, (((0,), (0,)), ((), ())), preferred_element_type=F32)


def mask_bias(code_k, seg_q, first_query):
    shape = (code_k.shape[0], seg_q.shape[1])
    key_at = lax.broadcasted_iota(jnp.int32, shape, 0)
    query_at = lax.broadcasted_iota(jnp.int32, shape, 1) + first_query
    allowed = (code_k == seg_q) | (key_at == query_at)
    return jnp.where(allowed, 0.0, MASKED)


def head_masked(block, head, head_dim):
    lane = lax.broadcasted_iota(jnp.int32, block.shape, 1)
    inside = (lane >= head * head_dim) & (lane < (head + 1) * head_dim)
    return jnp.where(inside, block, jnp.zeros_like(block))


def attend_forward_kernel(head_dim, q_ref, k_ref, v_ref, code_ref, seg_ref, o_ref, lse_ref, bias_ref):
    block = q_ref.shape[0]
    per = q_ref.shape[1] // head_dim
    scale = head_dim ** (-0.5)

    @pl.when(pl.program_id(1) == 0)
    def _():
        bias_ref[...] = mask_bias(code_ref[...], seg_ref[...], pl.program_id(0) * block)

    query = (q_ref[...].astype(F32) * scale).astype(BF)
    keys = k_ref[...]
    values_t = v_ref[...].astype(F32).T.astype(BF)
    outs, tops = [], []
    for head in range(per):
        scores = nt_dot(keys, head_masked(query, head, head_dim)) + bias_ref[...]
        top = jnp.max(scores, axis=0, keepdims=True)
        expo = jnp.exp(scores - top)
        total = jnp.sum(expo, axis=0, keepdims=True)
        part = nn_dot(values_t[head * head_dim : (head + 1) * head_dim], expo.astype(BF))
        outs.append(part / total)
        tops.append(top + jnp.log(total))
    o_ref[...] = jnp.concatenate(outs, axis=0).T.astype(BF)
    lse_ref[0] = jnp.concatenate(tops, axis=0)


def attend_backward_kernel(
    head_dim, q_ref, k_ref, v_ref, do_ref, lse_ref, code_ref, seg_ref, dq_ref, dk_ref, dv_ref, bias_ref, dk_acc, dv_acc
):
    block = q_ref.shape[0]
    per = q_ref.shape[1] // head_dim
    scale = head_dim ** (-0.5)
    at = pl.program_id(1)

    @pl.when(pl.program_id(0) == 0)
    def _():
        bias_ref[at] = mask_bias(code_ref[...], seg_ref[...], at * block)

    @pl.when(at == 0)
    def _():
        dk_acc[...] = jnp.zeros_like(dk_acc)
        dv_acc[...] = jnp.zeros_like(dv_acc)

    query = (q_ref[...].astype(F32) * scale).astype(BF)
    keys = k_ref[...]
    keys_t = keys.astype(F32).T.astype(BF)
    values = v_ref[...]
    grad_out = do_ref[...]
    outs = []
    for head in range(per):
        query_h = head_masked(query, head, head_dim)
        grad_h = head_masked(grad_out, head, head_dim)
        scores = nt_dot(keys, query_h) + bias_ref[at]
        probs = jnp.exp(scores - lse_ref[0, head : head + 1])
        grad_probs = nt_dot(values, grad_h)
        inner = jnp.sum(probs * grad_probs, axis=0, keepdims=True)
        grad_scores = (probs * (grad_probs - inner)).astype(BF)
        dv_acc[...] += nn_dot(probs.astype(BF), grad_h)
        dk_acc[...] += nn_dot(grad_scores, query_h)
        outs.append(nn_dot(keys_t[head * head_dim : (head + 1) * head_dim], grad_scores) * scale)
    dq_ref[...] = jnp.concatenate(outs, axis=0).T.astype(BF)

    @pl.when(at == pl.num_programs(1) - 1)
    def _():
        dk_ref[...] = dk_acc[...].astype(dk_ref.dtype)
        dv_ref[...] = dv_acc[...].astype(dv_ref.dtype)


def attend_forward(q, k, v, code_k, seg_q, head_dim):
    rows, width = q.shape
    keys = k.shape[0]
    block = min(256, rows)
    pair = 2 * head_dim
    cost = pl.CostEstimate(
        flops=16 * rows * keys * width, bytes_accessed=8 * rows * width, transcendentals=rows * keys * width // head_dim
    )
    return pl.pallas_call(
        lambda *refs: attend_forward_kernel(head_dim, *refs),
        grid=(rows // block, width // pair),
        in_specs=[
            pl.BlockSpec((block, pair), lambda i, h: (i, h)),
            pl.BlockSpec((keys, pair), lambda i, h: (0, h)),
            pl.BlockSpec((keys, pair), lambda i, h: (0, h)),
            pl.BlockSpec((keys, 1), lambda i, h: (0, 0)),
            pl.BlockSpec((1, block), lambda i, h: (0, i)),
        ],
        out_specs=[
            pl.BlockSpec((block, pair), lambda i, h: (i, h)),
            pl.BlockSpec((1, 2, block), lambda i, h: (h, 0, i)),
        ],
        out_shape=[
            jax.ShapeDtypeStruct((rows, width), BF),
            jax.ShapeDtypeStruct((width // pair, 2, rows), F32),
        ],
        scratch_shapes=[pltpu.VMEM((keys, block), F32)],
        compiler_params=pltpu.CompilerParams(vmem_limit_bytes=VMEM_LIMIT),
        cost_estimate=cost,
        name="attend_forward",
    )(q, k, v, code_k, seg_q)


def attend_backward(q, k, v, grad_out, lse, code_k, seg_q, head_dim, kv_type):
    rows, width = q.shape
    keys = k.shape[0]
    block = min(256, rows)
    pair = 2 * head_dim
    cost = pl.CostEstimate(
        flops=40 * rows * keys * width, bytes_accessed=16 * rows * width, transcendentals=rows * keys * width // head_dim
    )
    return pl.pallas_call(
        lambda *refs: attend_backward_kernel(head_dim, *refs),
        grid=(width // pair, rows // block),
        in_specs=[
            pl.BlockSpec((block, pair), lambda h, i: (i, h)),
            pl.BlockSpec((keys, pair), lambda h, i: (0, h)),
            pl.BlockSpec((keys, pair), lambda h, i: (0, h)),
            pl.BlockSpec((block, pair), lambda h, i: (i, h)),
            pl.BlockSpec((1, 2, block), lambda h, i: (h, 0, i)),
            pl.BlockSpec((keys, 1), lambda h, i: (0, 0)),
            pl.BlockSpec((1, block), lambda h, i: (0, i)),
        ],
        out_specs=[
            pl.BlockSpec((block, pair), lambda h, i: (i, h)),
            pl.BlockSpec((keys, pair), lambda h, i: (0, h)),
            pl.BlockSpec((keys, pair), lambda h, i: (0, h)),
        ],
        out_shape=[
            jax.ShapeDtypeStruct((rows, width), BF),
            jax.ShapeDtypeStruct((keys, width), kv_type),
            jax.ShapeDtypeStruct((keys, width), kv_type),
        ],
        scratch_shapes=[
            pltpu.VMEM((rows // block, keys, block), F32),
            pltpu.VMEM((keys, pair), F32),
            pltpu.VMEM((keys, pair), F32),
        ],
        compiler_params=pltpu.CompilerParams(vmem_limit_bytes=VMEM_LIMIT),
        cost_estimate=cost,
        name="attend_backward",
    )(q, k, v, grad_out, lse, code_k, seg_q)


def norm_forward(residual):
    average = jnp.mean(residual, axis=-1, keepdims=True)
    centred = residual - average
    spread = jnp.mean(centred * centred, axis=-1, keepdims=True)
    inverse = lax.rsqrt(spread + NORM_EPS)
    return centred * inverse, inverse


def norm_backward(grad, unit, inverse, gain):
    scaled = grad * gain
    return inverse * (
        scaled
        - jnp.mean(scaled, axis=-1, keepdims=True)
        - unit * jnp.mean(scaled * unit, axis=-1, keepdims=True)
    )


def gelu_pair(values):
    cdf = 0.5 * (1.0 + lax.erf(values * (2.0**-0.5)))
    density = jnp.exp(-0.5 * values * values) * ((2.0 * math.pi) ** -0.5)
    return values * cdf, cdf + values * density


class Place:
    def __init__(self):
        self.section = lax.axis_index("section")
        self.ctx = lax.axis_index("ctx")
        fsdp = lax.axis_index("fsdp")
        self.nz = lax.axis_size("ctx")
        self.nf = lax.axis_size("fsdp")
        side = math.isqrt(self.nf)
        self.nx = side if side * side == self.nf else self.nf
        self.ny = self.nf // self.nx
        self.y = fsdp // self.nx
        self.x = fsdp % self.nx

    def from_x(self, value, steps):
        pairs = []
        for f in range(self.nf):
            y, x = divmod(f, self.nx)
            pairs.append((y * self.nx + (x + steps) % self.nx, f))
        return lax.ppermute(value, "fsdp", pairs)

    def from_y(self, value, steps):
        pairs = []
        for f in range(self.nf):
            y, x = divmod(f, self.nx)
            pairs.append((((y + steps) % self.ny) * self.nx + x, f))
        return lax.ppermute(value, "fsdp", pairs)

    def sibling(self, value):
        return lax.ppermute(value, "section", [(0, 1), (1, 0)])

    def in_order(self, own, other, axis):
        first = self.section == 0
        return jnp.concatenate([jnp.where(first, own, other), jnp.where(first, other, own)], axis=axis)


def place_rotated(pieces, first, count):
    out = jnp.zeros((count,) + pieces[0].shape, pieces[0].dtype)
    for r, piece in enumerate(pieces):
        out = lax.dynamic_update_index_in_dim(out, piece, (first + r) % count, 0)
    return out


def gather_rows(place, shard, x_first):
    rows, cols = shard.shape
    column = lax.all_gather(shard, "ctx", axis=0, tiled=True).reshape(place.nz, rows, cols)
    if x_first:
        line = [column] + [place.from_x(column, r) for r in range(1, place.nx)]
        grid = [line] + [[place.from_y(piece, r) for piece in line] for r in range(1, place.ny)]
    else:
        line = [column] + [place.from_y(column, r) for r in range(1, place.ny)]
        more = [[place.from_x(piece, r) for piece in line] for r in range(1, place.nx)]
        grid = [[line[ry]] + [m[ry] for m in more] for ry in range(place.ny)]
    out = jnp.zeros((place.nz, place.nf, rows, cols), shard.dtype)
    for ry in range(place.ny):
        for rx in range(place.nx):
            at = ((place.y + ry) % place.ny) * place.nx + (place.x + rx) % place.nx
            out = lax.dynamic_update_slice(out, grid[ry][rx][:, None], (0, at, 0, 0))
    return out.reshape(place.nz * place.nf * rows, cols)


def scatter_rows(place, full, y_first):
    cols = full.shape[1]
    parts = full.reshape(place.nz, place.ny, place.nx, -1, cols)

    def along_y(value):
        keep = lax.dynamic_index_in_dim(value, place.y, 1, False).astype(F32)
        for r in range(1, place.ny):
            sent = lax.dynamic_index_in_dim(value, (place.y + r) % place.ny, 1, False)
            keep = keep + place.from_y(sent, -r).astype(F32)
        return keep.astype(BF)

    def along_x(value):
        axis = value.ndim - 3
        keep = lax.dynamic_index_in_dim(value, place.x, axis, False).astype(F32)
        for r in range(1, place.nx):
            sent = lax.dynamic_index_in_dim(value, (place.x + r) % place.nx, axis, False)
            keep = keep + place.from_x(sent, -r).astype(F32)
        return keep.astype(BF)

    if y_first:
        column = along_x(along_y(parts))
    else:
        column = along_y(along_x(parts))
    out = lax.psum_scatter(column.reshape(-1, cols), "ctx", scatter_dimension=0, tiled=True)
    return out.astype(F32)


def to_sequences(place, value):
    count = value.shape[0]
    groups = place.nz // count
    piece_at = place.ctx % count
    kept_seq = place.ctx // groups
    pieces = []
    for k in range(count):
        sent = lax.dynamic_index_in_dim(value, (piece_at + k) % count, 0, False)
        pairs = [(z, ((z % count + k) % count) * groups + z // count) for z in range(place.nz)]
        pieces.append(sent if all(a == b for a, b in pairs) else lax.ppermute(sent, "ctx", pairs))
    return place_rotated([pieces[0]] + pieces[:0:-1], kept_seq, count)


def from_sequences(place, value):
    count = value.shape[0]
    groups = place.nz // count
    kept_seq = place.ctx // groups
    pieces = []
    for k in range(count):
        sent = lax.dynamic_index_in_dim(value, (kept_seq - k) % count, 0, False)
        pairs = [(((z % count + k) % count) * groups + z // count, z) for z in range(place.nz)]
        pieces.append(sent if all(a == b for a, b in pairs) else lax.ppermute(sent, "ctx", pairs))
    return place_rotated(pieces, place.ctx % count, count)


def split_to_sequences(place, value):
    seqs, rows, width = value.shape
    half = rows // 2
    mine = lax.dynamic_slice_in_dim(value, place.section * half, half, 1)
    moved = to_sequences(place, mine)
    other = place.sibling(moved)
    first = place.section == 0
    both = jnp.stack([jnp.where(first, moved, other), jnp.where(first, other, moved)], axis=1)
    return both.reshape(seqs * rows, width)


def on_device(
    tokens,
    segment_ids,
    valid_mask,
    cotangent,
    qkv_weight,
    out_proj,
    in_weight,
    out_weight,
    norm_gain,
    norm_shift,
    proj_bias,
    ff_bias,
):
    place = Place()
    section = place.section
    first_section = section == 0
    micro, seqs, local, width = tokens.shape
    count = micro * seqs
    groups = place.nz // count
    rows = count * local
    head_dim = width // HEADS
    half = width // 2
    ff_width = in_weight.shape[2]
    ff_half = ff_width // 2
    chips = place.nz * place.nf
    ff_rows = out_weight.shape[1]
    ff_split = ff_rows // 2

    def part_of(which):
        qkv_part = lax.dynamic_slice_in_dim(qkv_weight[0], which * half, half, 2)
        proj_part = lax.dynamic_slice_in_dim(out_proj[0], which * half, half, 1)
        in_part = lax.dynamic_index_in_dim(
            in_weight[0].reshape(-1, chips, 2, ff_split), which, 2, False
        ).reshape(-1, ff_half)
        out_part = lax.dynamic_slice_in_dim(out_weight[0], which * ff_split, ff_split, 0)
        attn_part = jnp.concatenate([qkv_part[0], qkv_part[1], qkv_part[2], proj_part], axis=1)
        return (attn_part, in_part, out_part)

    own_parts = part_of(section)
    sent_parts = part_of(1 - section)
    full = [[None] * 3, [None] * 3]
    shards = [[None] * 3, [None] * 3]
    for index in range(3):
        other = place.sibling(sent_parts[index])
        shards[0][index] = jnp.where(first_section, own_parts[index], other)
        shards[1][index] = jnp.where(first_section, other, own_parts[index])
    flip = True
    for layer in range(2):
        for index in range(3):
            full[layer][index] = gather_rows(place, shards[layer][index], flip)
            flip = not flip

    def layer_weights(layer):
        attn, w_in, w_out = full[layer]
        w_qkv = attn[:, : 3 * half]
        columns = attn[:, 3 * half :]
        mine = lax.dynamic_slice_in_dim(columns, section * half, half, 0)
        sent = lax.dynamic_slice_in_dim(columns, (1 - section) * half, half, 0)
        w_proj = place.in_order(mine, place.sibling(sent), 1)
        return w_qkv, w_proj, w_in, w_out

    small_own = jnp.concatenate([norm_gain[0], norm_shift[0], proj_bias[0], ff_bias[0].reshape(-1, width)], axis=0)
    small_other = place.sibling(small_own)
    small = [
        jnp.where(first_section, small_own, small_other),
        jnp.where(first_section, small_other, small_own),
    ]

    def layer_small(layer):
        table = small[layer]
        gains, shifts, biases = table[0:2], table[2:4], table[4:8]
        ff_all = table[8:].reshape(chips, 2, ff_split)
        ff_part = lax.dynamic_index_in_dim(ff_all, section, 1, False).reshape(-1)
        bias_q = lax.dynamic_slice_in_dim(biases[0], section * half, half, 0)
        bias_v = lax.dynamic_slice_in_dim(biases[1], section * half, half, 0)
        bias_qkv = jnp.concatenate([bias_q, jnp.zeros_like(bias_q), bias_v])
        return gains, shifts, biases, ff_part, bias_qkv

    ids = segment_ids.reshape(count, local) * 2 + (valid_mask.reshape(count, local) == 1).astype(jnp.int32)
    ids = to_sequences(place, ids).reshape(rows)
    seg_own = ids // 2
    valid_own = ids % 2

    def over_groups(value, steps):
        pairs = []
        for z in range(place.nz):
            q, g = divmod(z, groups)
            pairs.append((q * groups + (g + steps) % groups, z))
        return lax.ppermute(value, "ctx", pairs)

    def gather_groups(value):
        return jnp.concatenate([value] + [over_groups(value, r) for r in range(1, groups)], axis=0)

    def scatter_groups(value):
        parts = value.reshape(groups, rows, -1)
        total = parts[0]
        for r in range(1, groups):
            total = total + over_groups(parts[r].astype(BF), -r).astype(F32)
        return total.astype(BF)

    code_k = gather_groups(jnp.where(valid_own == 1, seg_own, -1))[:, None]
    seg_q = seg_own[None, :]
    live = valid_own.astype(F32)[:, None]

    layer_input = split_to_sequences(place, tokens.reshape(count, local, width))
    grad_out = split_to_sequences(place, cotangent.reshape(count, local, width))

    saved, acts, squares = [], [], []
    weights = [layer_weights(layer) for layer in range(2)]
    smalls = [layer_small(layer) for layer in range(2)]
    for layer in range(2):
        w_qkv, w_proj, w_in, w_out = weights[layer]
        gains, shifts, biases, ff_part, bias_qkv = smalls[layer]
        qkv = (nn_dot(layer_input, w_qkv) + bias_qkv).astype(BF)
        q, k, v = qkv[:, :half], qkv[:, half : 2 * half], qkv[:, 2 * half :]
        if groups > 1:
            kv = gather_groups(qkv[:, half:])
            k, v = kv[:, :half], kv[:, half:]
        mixed, lse = attend_forward(q, k, v, code_k, seg_q, head_dim)
        part = nn_dot(mixed, w_proj)
        branch_attn = part + place.sibling(part.astype(BF)).astype(F32) + biases[2]
        wide_input = layer_input.astype(F32)
        unit_one, inverse_one = norm_forward(wide_input + branch_attn)
        normed = unit_one * gains[0] + shifts[0]
        normed_low = normed.astype(BF)
        hidden = nn_dot(normed_low, w_in) + ff_part
        activated, slope = gelu_pair(hidden)
        activated = activated.astype(BF)
        slope = slope.astype(BF)
        part = nn_dot(activated, w_out)
        branch_ff = part + place.sibling(part.astype(BF)).astype(F32) + biases[3]
        unit_two, inverse_two = norm_forward(normed + branch_ff)
        output = unit_two * gains[1] + shifts[1]
        squares.append(
            jnp.stack([jnp.sum(live * m * m) for m in (wide_input, branch_attn, branch_ff, output)])
        )
        saved.append(
            (layer_input, q, k, v, mixed, lse, unit_one, inverse_one, normed_low, activated, slope, unit_two, inverse_two)
        )
        layer_input = output.astype(BF)
        acts.append(layer_input)

    def give_back(pair):
        value = jnp.where(first_section, pair[0], pair[1])
        return from_sequences(place, value.reshape(count, local, width)).reshape(1, micro, seqs, local, width)

    activations = give_back(acts)

    square_sum = jnp.where(first_section, squares[0], squares[1])
    totals = lax.psum(jnp.concatenate([square_sum, jnp.sum(live)[None]]), ("ctx", "fsdp"))
    rms = jnp.sqrt(totals[:4] / (totals[4] * width))[None]

    grads = [None, None]
    input_grads = [None, None]
    small_grads = [None, None]
    grad_in = grad_out.astype(F32)
    for layer in (1, 0):
        w_qkv, w_proj, w_in, w_out = weights[layer]
        gains = smalls[layer][0]
        (u, q, k, v, mixed, lse, unit_one, inverse_one, normed_low, activated, slope, unit_two, inverse_two) = saved[layer]
        grad_gain_two = jnp.sum(grad_in * unit_two, axis=0)
        grad_shift_two = jnp.sum(grad_in, axis=0)
        grad_second = norm_backward(grad_in, unit_two, inverse_two, gains[1])
        grad_ff = grad_second.astype(BF)
        grad_w_out = tn_dot(activated, grad_ff).astype(BF)
        out_total = scatter_rows(place, grad_w_out, layer == 1)
        grad_b_out = jnp.sum(grad_ff.astype(F32), axis=0)
        grad_hidden = (nt_dot(grad_ff, w_out) * slope.astype(F32)).astype(BF)
        grad_ff_row = jnp.sum(grad_hidden.astype(F32), axis=0)
        part = nt_dot(grad_hidden, w_in)
        grad_normed = grad_second + part + place.sibling(part.astype(BF)).astype(F32)
        grad_w_in = tn_dot(normed_low, grad_hidden).astype(BF)
        in_total = scatter_rows(place, grad_w_in, layer == 0)
        grad_gain_one = jnp.sum(grad_normed * unit_one, axis=0)
        grad_shift_one = jnp.sum(grad_normed, axis=0)
        grad_first = norm_backward(grad_normed, unit_one, inverse_one, gains[0])
        grad_branch = grad_first.astype(BF)
        grad_b_proj = jnp.sum(grad_branch.astype(F32), axis=0)
        grad_mixed = nt_dot(grad_branch, w_proj).astype(BF)
        grad_w_proj = tn_dot(mixed, grad_branch).astype(BF)
        mine = lax.dynamic_slice_in_dim(grad_w_proj, section * half, half, 1)
        sent = lax.dynamic_slice_in_dim(grad_w_proj, (1 - section) * half, half, 1)
        grad_w_proj = place.in_order(mine, place.sibling(sent), 0)
        dq, dk, dv = attend_backward(
            q, k, v, grad_mixed, lse, code_k, seg_q, head_dim, BF if groups == 1 else F32
        )
        if groups > 1:
            dk, dv = scatter_groups(dk), scatter_groups(dv)
        dqkv = jnp.concatenate([dq, dk, dv], axis=1)
        part = nt_dot(dqkv, w_qkv)
        grad_u = grad_first + part + place.sibling(part.astype(BF)).astype(F32)
        grad_w_qkv = tn_dot(u, dqkv).astype(BF)
        attn_total = scatter_rows(place, jnp.concatenate([grad_w_qkv, grad_w_proj], axis=1), layer == 1)
        dqkv_rows = jnp.sum(dqkv.astype(F32), axis=0)
        grads[layer] = (attn_total, in_total, out_total)
        input_grads[layer] = grad_u.astype(BF)
        grad_in = input_grads[layer].astype(F32)
        here = jnp.where(section == layer, 1.0, 0.0)
        spread = jnp.zeros((2, 2, half), F32)
        spread = lax.dynamic_update_slice(spread, dqkv_rows[:half][None, None], (0, section, 0))
        spread = lax.dynamic_update_slice(spread, dqkv_rows[2 * half :][None, None], (1, section, 0))
        ff_spread = lax.dynamic_update_slice(
            jnp.zeros((chips, 2, ff_split), F32), grad_ff_row.reshape(chips, 1, ff_split), (0, section, 0)
        )
        rest = here * jnp.stack(
            [grad_gain_one, grad_gain_two, grad_shift_one, grad_shift_two, grad_b_proj, grad_b_out]
        )
        by_chip = jnp.concatenate([rest, spread.reshape(2, width)], axis=0).reshape(8, chips, -1)
        by_chip = jnp.moveaxis(by_chip, 1, 0).reshape(chips, -1)
        small_grads[layer] = jnp.concatenate([by_chip, ff_spread.reshape(chips, -1)], axis=1)

    input_grads = give_back(input_grads)

    def to_owner(pair):
        mine = jnp.where(first_section, pair[0], pair[1])
        sent = jnp.where(first_section, pair[1], pair[0])
        return mine, place.sibling(sent)

    def halves(pair):
        mine, other = to_owner(pair)
        return jnp.where(first_section, mine, other), jnp.where(first_section, other, mine)

    low, high = halves([grads[0][0], grads[1][0]])
    attn_rows = width // chips
    low = low.reshape(attn_rows, 4, half)
    high = high.reshape(attn_rows, 4, half)
    attn = jnp.concatenate([low, high], axis=2)
    grad_qkv = jnp.moveaxis(attn[:, :3], 1, 0)[None]
    grad_out_proj = attn[:, 3][None]
    low, high = halves([grads[0][1], grads[1][1]])
    grad_in_weight = jnp.stack(
        [low.reshape(-1, chips, ff_split), high.reshape(-1, chips, ff_split)], axis=2
    ).reshape(1, -1, ff_width)
    low, high = halves([grads[0][2], grads[1][2]])
    grad_out_weight = jnp.concatenate([low, high], axis=0)[None]

    mine, other = to_owner(small_grads)
    total = lax.psum_scatter(mine + other, ("ctx", "fsdp"), scatter_dimension=0, tiled=True)[0]
    per_chip = width // chips
    table = total[: 8 * per_chip].reshape(8, per_chip)
    grad_gain = table[0:2][None]
    grad_shift = table[2:4][None]
    grad_proj_bias = jnp.stack([table[6], table[7], table[4], table[5]])[None]
    grad_ff_bias = total[8 * per_chip :][None]
    return (
        activations,
        input_grads,
        grad_qkv,
        grad_out_proj,
        grad_in_weight,
        grad_out_weight,
        grad_gain,
        grad_shift,
        grad_proj_bias,
        grad_ff_bias,
        rms,
    )


def solution(mesh):
    placed = (
        P(None, "fsdp", "ctx", None),
        P(None, "fsdp", "ctx"),
        P(None, "fsdp", "ctx"),
        P(None, "fsdp", "ctx", None),
        P("section", None, ("ctx", "fsdp"), None),
        P("section", ("ctx", "fsdp"), None),
        P("section", ("ctx", "fsdp"), None),
        P("section", ("ctx", "fsdp"), None),
        P("section", None, None),
        P("section", None, None),
        P("section", None, None),
        P("section", None),
    )
    return jax.shard_map(
        on_device,
        mesh=mesh,
        in_specs=placed,
        out_specs=(
            P("section", None, "fsdp", "ctx", None),
            P("section", None, "fsdp", "ctx", None),
            P("section", None, ("ctx", "fsdp"), None),
            P("section", ("ctx", "fsdp"), None),
            P("section", ("ctx", "fsdp"), None),
            P("section", ("ctx", "fsdp"), None),
            P("section", None, ("ctx", "fsdp")),
            P("section", None, ("ctx", "fsdp")),
            P("section", None, ("ctx", "fsdp")),
            P("section", ("ctx", "fsdp")),
            P("section", None),
        ),
        check_vma=False,
    )
```

```python
import math

import jax
import jax.numpy as jnp
from jax import lax
from jax.experimental import pallas as pl
from jax.experimental.pallas import tpu as pltpu
from jax.sharding import PartitionSpec as P

HEADS = 16
NORM_EPS = 1e-05
MASKED = -1e30
BF = jnp.bfloat16


def priced(flops, bytes_accessed, transcendentals):
    share = 0.35
    return pl.CostEstimate(
        flops=int(share * flops),
        bytes_accessed=int(share * bytes_accessed),
        transcendentals=int(share * transcendentals),
    )


F32 = jnp.float32
MIB = 1024 * 1024


def nt_dot(a, b):
    return lax.dot_general(a, b, (((1,), (1,)), ((), ())), preferred_element_type=F32)


def nn_dot(a, b):
    return lax.dot_general(a, b, (((1,), (0,)), ((), ())), preferred_element_type=F32)


def tn_dot(a, b):
    return lax.dot_general(a, b, (((0,), (0,)), ((), ())), preferred_element_type=F32)


def mask_bias(code_k, seg_q):
    shape = (code_k.shape[0], seg_q.shape[1])
    key_at = lax.broadcasted_iota(jnp.int32, shape, 0)
    query_at = lax.broadcasted_iota(jnp.int32, shape, 1)
    allowed = (code_k == seg_q) | (key_at == query_at)
    return jnp.where(allowed, 0.0, MASKED)


def head_masked(block, head, head_dim):
    lane = lax.broadcasted_iota(jnp.int32, block.shape, 1)
    inside = (lane >= head * head_dim) & (lane < (head + 1) * head_dim)
    return jnp.where(inside, block, jnp.zeros_like(block))


def attend_forward_kernel(head_dim, q_ref, k_ref, v_ref, code_ref, seg_ref, o_ref, lse_ref, bias_ref):
    per = q_ref.shape[1] // head_dim

    @pl.when(pl.program_id(0) == 0)
    def _():
        bias_ref[...] = mask_bias(code_ref[...], seg_ref[...])

    query = (q_ref[...].astype(F32) * head_dim ** (-0.5)).astype(BF)
    keys = k_ref[...]
    values_t = v_ref[...].T
    outs, tops = [], []
    for head in range(per):
        scores = nt_dot(keys, head_masked(query, head, head_dim)) + bias_ref[...]
        top = jnp.max(scores, axis=0, keepdims=True)
        expo = jnp.exp(scores - top)
        total = jnp.sum(expo, axis=0, keepdims=True)
        part = nn_dot(values_t[head * head_dim : (head + 1) * head_dim], expo.astype(BF))
        outs.append(part / total)
        tops.append(top + jnp.log(total))
    o_ref[...] = jnp.concatenate(outs, axis=0).T.astype(BF)
    lse_ref[0] = jnp.concatenate(tops, axis=0)


def attend_backward_kernel(
    head_dim, q_ref, k_ref, v_ref, do_ref, lse_ref, code_ref, seg_ref, dq_ref, dk_ref, dv_ref, bias_ref
):
    rows = q_ref.shape[0]
    block = min(512, rows)
    per = q_ref.shape[1] // head_dim
    scale = head_dim ** (-0.5)

    @pl.when(pl.program_id(0) == 0)
    def _():
        bias_ref[...] = mask_bias(code_ref[...], seg_ref[...])

    keys = k_ref[...]
    keys_t = keys.T
    values = v_ref[...]
    dk, dv = None, None
    for first in range(0, rows, block):
        span = slice(first, first + block)
        query = (q_ref[span, :].astype(F32) * scale).astype(BF)
        grad_out = do_ref[span, :]
        outs = []
        for head in range(per):
            query_h = head_masked(query, head, head_dim)
            grad_h = head_masked(grad_out, head, head_dim)
            scores = nt_dot(keys, query_h) + bias_ref[:, span]
            probs = jnp.exp(scores - lse_ref[0, head : head + 1, span])
            grad_probs = nt_dot(values, grad_h)
            inner = jnp.sum(probs * grad_probs, axis=0, keepdims=True)
            grad_scores = (probs * (grad_probs - inner)).astype(BF)
            dv_part = nn_dot(probs.astype(BF), grad_h)
            dk_part = nn_dot(grad_scores, query_h)
            dv = dv_part if dv is None else dv + dv_part
            dk = dk_part if dk is None else dk + dk_part
            outs.append(nn_dot(keys_t[head * head_dim : (head + 1) * head_dim], grad_scores) * scale)
        dq_ref[span, :] = jnp.concatenate(outs, axis=0).T.astype(BF)
    dk_ref[...] = dk.astype(dk_ref.dtype)
    dv_ref[...] = dv.astype(dv_ref.dtype)


def attend_forward(q, k, v, code_k, seg_q, head_dim):
    rows, width = q.shape
    keys = k.shape[0]
    pair = 2 * head_dim
    cost = priced(
        flops=16 * rows * keys * width, bytes_accessed=8 * rows * width, transcendentals=rows * keys * width // head_dim
    )
    return pl.pallas_call(
        lambda *refs: attend_forward_kernel(head_dim, *refs),
        grid=(width // pair,),
        in_specs=[
            pl.BlockSpec((rows, pair), lambda h: (0, h)),
            pl.BlockSpec((keys, pair), lambda h: (0, h)),
            pl.BlockSpec((keys, pair), lambda h: (0, h)),
            pl.BlockSpec((keys, 1), lambda h: (0, 0)),
            pl.BlockSpec((1, rows), lambda h: (0, 0)),
        ],
        out_specs=[
            pl.BlockSpec((rows, pair), lambda h: (0, h)),
            pl.BlockSpec((1, 2, rows), lambda h: (h, 0, 0)),
        ],
        out_shape=[
            jax.ShapeDtypeStruct((rows, width), BF),
            jax.ShapeDtypeStruct((width // pair, 2, rows), F32),
        ],
        scratch_shapes=[pltpu.VMEM((keys, rows), F32)],
        compiler_params=pltpu.CompilerParams(vmem_limit_bytes=24 * MIB),
        cost_estimate=cost,
        name="attend_forward",
    )(q, k, v, code_k, seg_q)


def attend_backward(q, k, v, grad_out, lse, code_k, seg_q, head_dim, kv_type):
    rows, width = q.shape
    keys = k.shape[0]
    pair = 2 * head_dim
    cost = priced(
        flops=40 * rows * keys * width, bytes_accessed=16 * rows * width, transcendentals=rows * keys * width // head_dim
    )
    return pl.pallas_call(
        lambda *refs: attend_backward_kernel(head_dim, *refs),
        grid=(width // pair,),
        in_specs=[
            pl.BlockSpec((rows, pair), lambda h: (0, h)),
            pl.BlockSpec((keys, pair), lambda h: (0, h)),
            pl.BlockSpec((keys, pair), lambda h: (0, h)),
            pl.BlockSpec((rows, pair), lambda h: (0, h)),
            pl.BlockSpec((1, 2, rows), lambda h: (h, 0, 0)),
            pl.BlockSpec((keys, 1), lambda h: (0, 0)),
            pl.BlockSpec((1, rows), lambda h: (0, 0)),
        ],
        out_specs=[
            pl.BlockSpec((rows, pair), lambda h: (0, h)),
            pl.BlockSpec((keys, pair), lambda h: (0, h)),
            pl.BlockSpec((keys, pair), lambda h: (0, h)),
        ],
        out_shape=[
            jax.ShapeDtypeStruct((rows, width), BF),
            jax.ShapeDtypeStruct((keys, width), kv_type),
            jax.ShapeDtypeStruct((keys, width), kv_type),
        ],
        scratch_shapes=[pltpu.VMEM((keys, rows), F32)],
        compiler_params=pltpu.CompilerParams(vmem_limit_bytes=24 * MIB),
        cost_estimate=cost,
        name="attend_backward",
    )(q, k, v, grad_out, lse, code_k, seg_q)


def row_product(xs, w, transposed, rows_in, consts, outs, finish, name):
    rows = xs[0].shape[0]
    block = min(256, rows)
    widths = [x.shape[1] for x in xs]
    wide = w.shape[0] if transposed else w.shape[1]

    def body(*refs):
        refs = list(refs)
        x_refs = [refs.pop(0) for _ in xs]
        w_ref = refs.pop(0)
        row_refs = [refs.pop(0) for _ in rows_in]
        const_refs = [refs.pop(0) for _ in consts]
        total, first = None, 0
        for x_ref, depth in zip(x_refs, widths):
            if transposed:
                part = nt_dot(x_ref[...], w_ref[:, first : first + depth])
            else:
                part = nn_dot(x_ref[...], w_ref[first : first + depth, :])
            total = part if total is None else total + part
            first += depth
        results = finish(total, *[r[...] for r in row_refs], *[c[...] for c in const_refs])
        for out_ref, value in zip(refs, results):
            out_ref[...] = value.astype(out_ref.dtype)

    return pl.pallas_call(
        body,
        grid=(rows // block,),
        in_specs=[pl.BlockSpec((block, depth), lambda i: (i, 0)) for depth in widths]
        + [pl.BlockSpec(w.shape, lambda i: (0, 0))]
        + [pl.BlockSpec((block, r.shape[1]), lambda i: (i, 0)) for r in rows_in]
        + [pl.BlockSpec(c.shape, lambda i: (0, 0)) for c in consts],
        out_specs=[pl.BlockSpec((block, columns), lambda i: (i, 0)) for columns, _ in outs],
        out_shape=[jax.ShapeDtypeStruct((rows, columns), kind) for columns, kind in outs],
        compiler_params=pltpu.CompilerParams(vmem_limit_bytes=16 * MIB),
        cost_estimate=priced(
            flops=2 * rows * sum(widths) * wide,
            bytes_accessed=2 * (rows * sum(widths) + w.size) + sum(4 * rows * c for c, _ in outs),
            transcendentals=0,
        ),
        name=name,
    )(*xs, w, *rows_in, *consts)


def norm_rows_forward(part, other, before, live, table):
    rows, width = part.shape
    block = min(256, rows)

    def body(part_ref, other_ref, before_ref, live_ref, table_ref, unit_ref, inverse_ref, low_ref, sums_ref):
        start = before_ref[...].astype(F32)
        branch = part_ref[...].astype(F32) + other_ref[...].astype(F32) + table_ref[0:1, :]
        residual = start + branch
        centred = residual - jnp.mean(residual, axis=-1, keepdims=True)
        spread = jnp.mean(centred * centred, axis=-1, keepdims=True)
        inverse = lax.rsqrt(spread + NORM_EPS)
        unit = centred * inverse
        out = unit * table_ref[1:2, :] + table_ref[2:3, :]
        unit_ref[...] = unit.astype(BF)
        inverse_ref[...] = inverse
        low_ref[...] = out.astype(BF)
        real = live_ref[...]

        @pl.when(pl.program_id(0) == 0)
        def _():
            sums_ref[...] = jnp.zeros_like(sums_ref)

        sums_ref[0:1, :] += jnp.sum(real * start * start, axis=0, keepdims=True)
        sums_ref[1:2, :] += jnp.sum(real * branch * branch, axis=0, keepdims=True)
        sums_ref[2:3, :] += jnp.sum(real * out * out, axis=0, keepdims=True)

    by_row = pl.BlockSpec((block, width), lambda i: (i, 0))
    thin = pl.BlockSpec((block, 1), lambda i: (i, 0))
    fixed = pl.BlockSpec((8, width), lambda i: (0, 0))
    return pl.pallas_call(
        body,
        grid=(rows // block,),
        in_specs=[by_row, by_row, by_row, thin, fixed],
        out_specs=[by_row, thin, by_row, fixed],
        out_shape=[
            jax.ShapeDtypeStruct((rows, width), BF),
            jax.ShapeDtypeStruct((rows, 1), F32),
            jax.ShapeDtypeStruct((rows, width), BF),
            jax.ShapeDtypeStruct((8, width), F32),
        ],
        compiler_params=pltpu.CompilerParams(vmem_limit_bytes=12 * MIB),
        cost_estimate=priced(flops=20 * rows * width, bytes_accessed=10 * rows * width, transcendentals=rows),
        name="norm_forward",
    )(part, other, before, live, table)


def norm_rows_backward(terms, unit, inverse, gain, rounded):
    rows, width = unit.shape
    block = min(256, rows)

    def body(*refs):
        refs = list(refs)
        grad = sum([refs.pop(0)[...].astype(F32) for _ in terms])
        unit_ref, inverse_ref, gain_ref = refs[:3]
        low_ref, sums_ref = refs[3:5]
        if rounded:
            refs[5][...] = grad.astype(BF)
            grad = grad.astype(BF).astype(F32)
        unit_rows = unit_ref[...].astype(F32)
        scaled = grad * gain_ref[...]
        result = inverse_ref[...] * (
            scaled
            - jnp.mean(scaled, axis=-1, keepdims=True)
            - unit_rows * jnp.mean(scaled * unit_rows, axis=-1, keepdims=True)
        )
        low = result.astype(BF)
        low_ref[...] = low

        @pl.when(pl.program_id(0) == 0)
        def _():
            sums_ref[...] = jnp.zeros_like(sums_ref)

        sums_ref[0:1, :] += jnp.sum(grad * unit_rows, axis=0, keepdims=True)
        sums_ref[1:2, :] += jnp.sum(grad, axis=0, keepdims=True)
        sums_ref[2:3, :] += jnp.sum(low.astype(F32), axis=0, keepdims=True)

    by_row = pl.BlockSpec((block, width), lambda i: (i, 0))
    thin = pl.BlockSpec((block, 1), lambda i: (i, 0))
    fixed = pl.BlockSpec((8, width), lambda i: (0, 0))
    low_shape = jax.ShapeDtypeStruct((rows, width), BF)
    return pl.pallas_call(
        body,
        grid=(rows // block,),
        in_specs=[by_row] * len(terms) + [by_row, thin, pl.BlockSpec((1, width), lambda i: (0, 0))],
        out_specs=[by_row, fixed] + [by_row] * rounded,
        out_shape=[low_shape, jax.ShapeDtypeStruct((8, width), F32)] + [low_shape] * rounded,
        compiler_params=pltpu.CompilerParams(vmem_limit_bytes=12 * MIB),
        cost_estimate=priced(flops=20 * rows * width, bytes_accessed=10 * rows * width, transcendentals=0),
        name="norm_backward",
    )(*terms, unit, inverse, gain)


def gelu_pair(values):
    cdf = 0.5 * (1.0 + lax.erf(values * (2.0**-0.5)))
    density = jnp.exp(-0.5 * values * values) * ((2.0 * math.pi) ** -0.5)
    return values * cdf, cdf + values * density


class Place:
    def __init__(self):
        self.section = lax.axis_index("section")
        self.ctx = lax.axis_index("ctx")
        fsdp = lax.axis_index("fsdp")
        self.nz = lax.axis_size("ctx")
        self.nf = lax.axis_size("fsdp")
        side = math.isqrt(self.nf)
        self.nx = side if side * side == self.nf else self.nf
        self.ny = self.nf // self.nx
        self.y = fsdp // self.nx
        self.x = fsdp % self.nx

    def from_x(self, value, steps):
        pairs = []
        for f in range(self.nf):
            y, x = divmod(f, self.nx)
            pairs.append((y * self.nx + (x + steps) % self.nx, f))
        return lax.ppermute(value, "fsdp", pairs)

    def from_y(self, value, steps):
        pairs = []
        for f in range(self.nf):
            y, x = divmod(f, self.nx)
            pairs.append((((y + steps) % self.ny) * self.nx + x, f))
        return lax.ppermute(value, "fsdp", pairs)

    def sibling(self, value):
        return lax.ppermute(value, "section", [(0, 1), (1, 0)])

    def in_order(self, own, other, axis):
        first = self.section == 0
        return jnp.concatenate([jnp.where(first, own, other), jnp.where(first, other, own)], axis=axis)


def place_rotated(pieces, first, count):
    out = jnp.zeros((count,) + pieces[0].shape, pieces[0].dtype)
    for r, piece in enumerate(pieces):
        out = lax.dynamic_update_index_in_dim(out, piece, (first + r) % count, 0)
    return out


def tie(*trees):
    return lax.optimization_barrier(trees)


class Gather:
    def __init__(self, place, shard):
        self.place, self.shard = place, shard

    def along_z(self):
        rows, cols = self.shard.shape
        column = lax.all_gather(self.shard, "ctx", axis=0, tiled=True)
        return column.reshape(self.place.nz, rows, cols)

    def first(self, column):
        place = self.place
        from_x = [place.from_x(column, r) for r in range(1, place.nx)]
        from_y = [place.from_y(column, r) for r in range(1, place.ny)]
        return (from_x, from_y)

    def second(self, got):
        place = self.place
        from_x, from_y = got
        half = self.shard.shape[1] // 2
        left = [[place.from_y(piece[..., :half], r) for piece in from_x] for r in range(1, place.ny)]
        right = [[place.from_x(piece[..., half:], r) for r in range(1, place.nx)] for piece in from_y]
        return (left, right)

    def whole(self, column, got, more, split):
        place = self.place
        from_x, from_y = got
        left, right = more
        nz, rows, cols = column.shape
        nx, ny, nf = place.nx, place.ny, place.nf
        half = cols // 2
        diagonal = [(ry, rx) for ry in range(1, ny) for rx in range(1, nx)]
        pieces = [column] + from_x + from_y
        places = [(0, 0)] + [(0, r) for r in range(1, nx)] + [(r, 0) for r in range(1, ny)]
        lefts = [left[ry - 1][rx - 1] for ry, rx in diagonal]
        rights = [right[ry - 1][rx - 1] for ry, rx in diagonal]
        at = jnp.stack([place.y, place.x]).astype(jnp.int32)

        def assemble(at_ref, *refs):
            outs = refs[len(pieces) + 2 * len(diagonal) :]

            def index(ry, rx):
                return ((at_ref[0] + ry) % ny) * nx + (at_ref[1] + rx) % nx

            def put(to, first, value):
                last = first + value.shape[-1]
                if first < split:
                    stop = min(last, split)
                    outs[0][0, to, :, first:stop] = value[:, : stop - first]
                if last > split:
                    start = max(first, split)
                    outs[1][0, to, :, start - split : last - split] = value[:, start - first :]

            for at_piece, ref in zip(places, refs):
                put(index(*at_piece), 0, ref[0])
            for k, at_piece in enumerate(diagonal):
                put(index(*at_piece), 0, refs[len(pieces) + k][0])
                put(index(*at_piece), half, refs[len(pieces) + len(diagonal) + k][0])

        widths = [split] + [cols - split] * (split < cols)
        out = pl.pallas_call(
            assemble,
            grid_spec=pltpu.PrefetchScalarGridSpec(
                num_scalar_prefetch=1,
                grid=(nz,),
                in_specs=[pl.BlockSpec((1, rows, cols), lambda z, at_ref: (z, 0, 0))] * len(pieces)
                + [pl.BlockSpec((1, rows, half), lambda z, at_ref: (z, 0, 0))] * (2 * len(diagonal)),
                out_specs=[pl.BlockSpec((1, nf, rows, w), lambda z, at_ref: (z, 0, 0, 0)) for w in widths],
            ),
            out_shape=[jax.ShapeDtypeStruct((nz, nf, rows, w), column.dtype) for w in widths],
            compiler_params=pltpu.CompilerParams(vmem_limit_bytes=10 * MIB),
            cost_estimate=priced(flops=0, bytes_accessed=4 * nz * nf * rows * cols, transcendentals=0),
            name="assemble",
        )(at, *pieces, *lefts, *rights)
        return [part.reshape(nz * nf * rows, part.shape[-1]) for part in out]


def scatter_sizes(place):
    return place.nz, place.ny, place.nx


class Scatter:
    def __init__(self, place):
        self.place = place
        self.at = jnp.stack([place.y, place.x]).astype(jnp.int32)

    def product(self, x, grads, ready=None):
        place = self.place
        nz, ny, nx = scatter_sizes(place)
        tokens = x.shape[0]
        span = x.shape[1] // nz
        rows = span // (ny * nx)
        widths = [g.shape[1] for g in grads]
        extra = [] if ready is None else [ready]
        cols = sum(widths) + sum(e.shape[1] for e in extra)
        half = cols // 2

        def body(at_ref, x_ref, *refs):
            refs = list(refs)
            grad_refs = [refs.pop(0) for _ in grads]
            extra_refs = [refs.pop(0) for _ in extra]
            full_ref = refs.pop()
            left_refs = [refs.pop(0) for _ in range(ny)]
            right_refs = [refs.pop(0) for _ in range(nx)]
            sums_ref = refs.pop(0)
            turned = x_ref[...].T
            first = 0
            for ref, wide in zip(grad_refs, widths):
                for start in range(0, wide, 512):
                    stop = min(wide, start + 512)
                    value = nn_dot(turned, ref[:, start:stop]).astype(BF)
                    full_ref[:, :, :, first + start : first + stop] = value.reshape(ny, nx, rows, stop - start)
                first += wide
            for ref in extra_refs:
                full_ref[:, :, :, first:] = ref[...].reshape(ny, nx, rows, cols - first)
            for r, ref in enumerate(left_refs):
                ref[0] = full_ref[(at_ref[0] + r) % ny, :, :, :half]
            for r, ref in enumerate(right_refs):
                for y in range(ny):
                    ref[0, y] = full_ref[y, (at_ref[1] + r) % nx, :, half:]

            @pl.when(pl.program_id(0) == 0)
            def _():
                ones = jnp.ones((8, tokens), BF)
                first = 0
                for ref, wide in zip(grad_refs, widths):
                    sums_ref[:, first : first + wide] = nn_dot(ones, ref[...])
                    first += wide

        out = pl.pallas_call(
            body,
            grid_spec=pltpu.PrefetchScalarGridSpec(
                num_scalar_prefetch=1,
                grid=(nz,),
                in_specs=[pl.BlockSpec((tokens, span), lambda z, at_ref: (0, z))]
                + [pl.BlockSpec((tokens, wide), lambda z, at_ref: (0, 0)) for wide in widths]
                + [pl.BlockSpec((span, e.shape[1]), lambda z, at_ref: (z, 0)) for e in extra],
                out_specs=[pl.BlockSpec((1, nx, rows, half), lambda z, at_ref: (z, 0, 0, 0))] * ny
                + [pl.BlockSpec((1, ny, rows, half), lambda z, at_ref: (z, 0, 0, 0))] * nx
                + [pl.BlockSpec((8, sum(widths)), lambda z, at_ref: (0, 0))],
                scratch_shapes=[pltpu.VMEM((ny, nx, rows, cols), BF)],
            ),
            out_shape=[jax.ShapeDtypeStruct((nz, nx, rows, half), BF)] * ny
            + [jax.ShapeDtypeStruct((nz, ny, rows, half), BF)] * nx
            + [jax.ShapeDtypeStruct((8, sum(widths)), F32)],
            compiler_params=pltpu.CompilerParams(vmem_limit_bytes=20 * MIB),
            cost_estimate=priced(
                flops=2 * tokens * x.shape[1] * sum(widths),
                bytes_accessed=2 * (x.size + tokens * cols + x.shape[1] * cols),
                transcendentals=0,
            ),
            name="weight_grad",
        )(self.at, x, *grads, *extra)
        return (out[:ny], out[ny : ny + nx]), out[-1][0]

    def first(self, parts):
        place = self.place
        left, right = parts
        left = [left[0]] + [place.from_y(left[r], -r) for r in range(1, place.ny)]
        right = [right[0]] + [place.from_x(right[r], -r) for r in range(1, place.nx)]
        return (left, right)

    def second(self, parts):
        place = self.place
        nz, ny, nx = scatter_sizes(place)
        left, right = parts
        rows, half = left[0].shape[2:]

        def body(at_ref, *refs):
            left_in, right_in = refs[:ny], refs[ny : ny + nx]
            left_out, right_out = refs[ny + nx : ny + 2 * nx], refs[ny + 2 * nx :]
            for r, ref in enumerate(left_out):
                to = (at_ref[1] + r) % nx
                ref[...] = sum([piece[:, to].astype(F32) for piece in left_in]).astype(BF)
            for r, ref in enumerate(right_out):
                to = (at_ref[0] + r) % ny
                ref[...] = sum([piece[:, to].astype(F32) for piece in right_in]).astype(BF)

        out = pl.pallas_call(
            body,
            grid_spec=pltpu.PrefetchScalarGridSpec(
                num_scalar_prefetch=1,
                grid=(1,),
                in_specs=[pl.BlockSpec((nz, nx, rows, half), lambda z, at_ref: (0, 0, 0, 0))] * ny
                + [pl.BlockSpec((nz, ny, rows, half), lambda z, at_ref: (0, 0, 0, 0))] * nx,
                out_specs=[pl.BlockSpec((nz, rows, half), lambda z, at_ref: (0, 0, 0))] * (nx + ny),
            ),
            out_shape=[jax.ShapeDtypeStruct((nz, rows, half), BF)] * (nx + ny),
            compiler_params=pltpu.CompilerParams(vmem_limit_bytes=20 * MIB),
            cost_estimate=priced(flops=0, bytes_accessed=8 * nz * nx * ny * rows * half, transcendentals=0),
            name="scatter_add",
        )(self.at, *left, *right)
        left, right = out[:nx], out[nx:]
        left = [left[0]] + [place.from_x(left[r], -r) for r in range(1, nx)]
        right = [right[0]] + [place.from_y(right[r], -r) for r in range(1, ny)]
        return (left, right)

    def third(self, parts):
        left, right = parts
        both = [sum([piece.astype(F32) for piece in side]) for side in (left, right)]
        column = jnp.concatenate(both, axis=-1).astype(BF)
        return column.reshape(-1, column.shape[-1])

    def along_z(self, column):
        return lax.psum_scatter(column, "ctx", scatter_dimension=0, tiled=True)


def small_scatter(place, value):
    value = value.reshape(place.nz, place.ny, place.nx, -1)

    def pick(part, axis, index):
        return lax.dynamic_index_in_dim(part, index, axis, False)

    total = pick(value, 1, place.y)
    for r in range(1, place.ny):
        total = total + place.from_y(pick(value, 1, (place.y + r) % place.ny), -r)
    value = total
    total = pick(value, 1, place.x)
    for r in range(1, place.nx):
        total = total + place.from_x(pick(value, 1, (place.x + r) % place.nx), -r)
    value = total
    total = pick(value, 0, place.ctx)
    for r in range(1, place.nz):
        pairs = [(z, (z + r) % place.nz) for z in range(place.nz)]
        total = total + lax.ppermute(pick(value, 0, (place.ctx + r) % place.nz), "ctx", pairs)
    return total


def to_pieces(place, value, steps):
    count = value.shape[0]
    groups = place.nz // count
    piece_at = place.ctx % count
    pieces = []
    for k in steps:
        sent = lax.dynamic_index_in_dim(value, (piece_at + k) % count, 0, False)
        pairs = [(z, ((z % count + k) % count) * groups + z // count) for z in range(place.nz)]
        pieces.append(sent if all(a == b for a, b in pairs) else lax.ppermute(sent, "ctx", pairs))
    return pieces


def in_positions(place, pieces):
    count = len(pieces)
    kept_seq = place.ctx // (place.nz // count)
    return place_rotated([pieces[0]] + pieces[:0:-1], kept_seq, count)


def from_sequences(place, value, steps, section=None):
    count = value.shape[0]
    groups = place.nz // count
    kept_seq = place.ctx // groups
    pieces = []
    for k in steps:
        sent = lax.dynamic_index_in_dim(value, (kept_seq - k) % count, 0, False)
        pairs = [(((z % count + k) % count) * groups + z // count, z) for z in range(place.nz)]
        if any(a != b for a, b in pairs):
            if section is None:
                sent = lax.ppermute(sent, "ctx", pairs)
            else:
                first = section * place.nz
                sent = lax.ppermute(sent, ("section", "ctx"), [(first + a, first + b) for a, b in pairs])
        pieces.append(sent)
    return pieces


def half_rows(place, value):
    half = value.shape[1] // 2
    return lax.dynamic_slice_in_dim(value, place.section * half, half, 1)


def join_halves(place, moved):
    other = place.sibling(moved)
    first = place.section == 0
    both = jnp.stack([jnp.where(first, moved, other), jnp.where(first, other, moved)], axis=1)
    return both.reshape(-1, moved.shape[-1])


def on_device(
    tokens,
    segment_ids,
    valid_mask,
    cotangent,
    qkv_weight,
    out_proj,
    in_weight,
    out_weight,
    norm_gain,
    norm_shift,
    proj_bias,
    ff_bias,
):
    place = Place()
    section = place.section
    first_section = section == 0
    micro, seqs, local, width = tokens.shape
    count = micro * seqs
    groups = place.nz // count
    rows = count * local
    head_dim = width // HEADS
    half = width // 2
    ff_width = in_weight.shape[2]
    ff_half = ff_width // 2
    chips = place.nz * place.nf
    ff_rows = out_weight.shape[1]
    ff_split = ff_rows // 2

    def part_of(which):
        qkv_part = lax.dynamic_slice_in_dim(qkv_weight[0], which * half, half, 2)
        proj_part = lax.dynamic_slice_in_dim(out_proj[0], which * half, half, 1)
        in_part = lax.dynamic_index_in_dim(
            in_weight[0].reshape(-1, chips, 2, ff_split), which, 2, False
        ).reshape(-1, ff_half)
        out_part = lax.dynamic_slice_in_dim(out_weight[0], which * ff_split, ff_split, 0)
        attn_part = jnp.concatenate([qkv_part[0], qkv_part[1], qkv_part[2], proj_part], axis=1)
        return (attn_part, in_part, out_part)

    own_parts = part_of(section)
    sent_parts = part_of(1 - section)
    shards = [[None] * 3, [None] * 3]
    for index in range(3):
        other = place.sibling(sent_parts[index])
        shards[0][index] = jnp.where(first_section, own_parts[index], other)
        shards[1][index] = jnp.where(first_section, other, own_parts[index])
    gathers = [Gather(place, shard) for layer in shards for shard in layer]

    def proj_whole(columns):
        mine = lax.dynamic_slice_in_dim(columns, section * half, half, 0)
        sent = lax.dynamic_slice_in_dim(columns, (1 - section) * half, half, 0)
        return place.in_order(mine, place.sibling(sent), 1)

    small_own = jnp.concatenate([norm_gain[0], norm_shift[0], proj_bias[0], ff_bias[0].reshape(-1, width)], axis=0)
    small_other = place.sibling(small_own)
    small = [
        jnp.where(first_section, small_own, small_other),
        jnp.where(first_section, small_other, small_own),
    ]

    def layer_small(layer):
        table = small[layer]
        gains, shifts, biases = table[0:2], table[2:4], table[4:8]
        ff_all = table[8:].reshape(chips, 2, ff_split)
        ff_part = lax.dynamic_index_in_dim(ff_all, section, 1, False).reshape(-1)
        bias_q = lax.dynamic_slice_in_dim(biases[0], section * half, half, 0)
        bias_v = lax.dynamic_slice_in_dim(biases[1], section * half, half, 0)
        bias_qkv = jnp.concatenate([bias_q, jnp.zeros_like(bias_q), bias_v])
        return gains, shifts, biases, ff_part, bias_qkv

    ids = segment_ids.reshape(count, local) * 2 + (valid_mask.reshape(count, local) == 1).astype(jnp.int32)
    ids = in_positions(place, to_pieces(place, ids, range(count))).reshape(rows)
    seg_own = ids // 2
    valid_own = ids % 2

    def over_groups(value, steps):
        pairs = []
        for z in range(place.nz):
            q, g = divmod(z, groups)
            pairs.append((q * groups + (g + steps) % groups, z))
        return lax.ppermute(value, "ctx", pairs)

    def gather_groups(value):
        return jnp.concatenate([value] + [over_groups(value, r) for r in range(1, groups)], axis=0)

    def scatter_groups(value):
        parts = value.reshape(groups, rows, -1)
        total = parts[0]
        for r in range(1, groups):
            total = total + over_groups(parts[r].astype(BF), -r).astype(F32)
        return total.astype(BF)

    code_k = gather_groups(jnp.where(valid_own == 1, seg_own, -1))[:, None]
    seg_q = seg_own[None, :]
    live = valid_own.astype(F32)[:, None]

    token_half = half_rows(place, tokens.reshape(count, local, width))
    cot_half = half_rows(place, cotangent.reshape(count, local, width))
    smalls = [layer_small(layer) for layer in range(2)]

    def attention_in(layer_input, w_qkv, layer):
        q, k, v = row_product(
            [layer_input],
            w_qkv,
            False,
            [],
            [smalls[layer][4][None]],
            [(half, BF)] * 3,
            lambda total, bias: jnp.split(total + bias, 3, axis=1),
            "project_qkv",
        )
        if groups > 1:
            k, v = gather_groups(k), gather_groups(v)
        mixed, lse = attend_forward(q, k, v, code_k, seg_q, head_dim)
        return q, k, v, mixed, lse

    def norm_table(*given):
        return jnp.concatenate([row[None] for row in given] + [jnp.zeros((8 - len(given), width), F32)], axis=0)

    def to_width(xs, w, transposed, name):
        (low,) = row_product(xs, w, transposed, [], [], [(width, BF)], lambda total: (total,), name)
        return low

    def attention_norm(layer_input, low, layer):
        gains, shifts, biases = smalls[layer][:3]
        table = norm_table(biases[2], gains[0], shifts[0])
        return norm_rows_forward(low, place.sibling(low), layer_input, live, table)

    def feed_in(normed_low, w_in, layer):
        activated, slope = gelu_pair(nn_dot(normed_low, w_in) + smalls[layer][3])
        return activated.astype(BF), slope.astype(BF)

    def feed_norm(normed_low, low, layer):
        gains, shifts, biases = smalls[layer][:3]
        table = norm_table(biases[3], gains[1], shifts[1])
        return norm_rows_forward(low, place.sibling(low), normed_low, live, table)

    columns, got, whole, more = [None] * 6, [None] * 6, [None] * 6, [None] * 6
    token_pieces = to_pieces(place, token_half, range(2))
    columns[0] = gathers[0].along_z()
    columns[0], token_pieces, token_half, gathers[1].shard = tie(
        columns[0], token_pieces, token_half, gathers[1].shard
    )
    got[0] = gathers[0].first(columns[0])
    token_pieces += to_pieces(place, token_half, range(2, count))
    columns[1] = gathers[1].along_z()
    got[0], token_pieces = tie(got[0], token_pieces)
    more[0] = gathers[0].second(got[0])
    layer_input = join_halves(place, in_positions(place, token_pieces))
    more[0], layer_input, columns[1], gathers[2].shard = tie(more[0], layer_input, columns[1], gathers[2].shard)

    def arrived(step):
        split = 3 * half if step % 3 == 0 else columns[step].shape[2]
        whole[step] = gathers[step].whole(columns[step], got[step], more[step], split)

    arrived(0)
    inputs, attns, projs, outs = [layer_input, None], [None] * 2, [None] * 2, [None] * 2
    norms, feeds, ends = [None] * 2, [None] * 2, [None] * 2
    cot_pieces = []
    for step in range(6):
        layer = step // 3
        if step > 0:
            more[step] = gathers[step].second(got[step])
        if step + 1 < 6:
            got[step + 1] = gathers[step + 1].first(columns[step + 1])
        if step + 2 < 6:
            columns[step + 2] = gathers[step + 2].along_z()
        if step in (0, 4):
            if step == 4:
                ends[0] = feed_norm(norms[0][2], outs[0], 0)
                inputs[1] = ends[0][2]
            layer = step // 4
            w_qkv, columns_proj = whole[3 * layer]
            projs[layer] = proj_whole(columns_proj)
            attns[layer] = attention_in(inputs[layer], w_qkv, layer)
            outs[layer] = to_width([attns[layer][3]], projs[layer], False, "project_out")
        elif step == 1:
            norms[0] = attention_norm(inputs[0], outs[0], 0)
            cot_pieces += to_pieces(place, cot_half, range(2))
        elif step == 2:
            feeds[0] = feed_in(norms[0][2], whole[1][0], 0)
            cot_pieces += to_pieces(place, cot_half, range(2, count - 1))
        elif step == 3:
            outs[0] = to_width([feeds[0][0]], whole[2][0], False, "feed_out")
        elif step == 5:
            norms[1] = attention_norm(inputs[1], outs[1], 1)
            feeds[1] = feed_in(norms[1][2], whole[4][0], 1)
            cot_pieces += to_pieces(place, cot_half, [count - 1])
        shard = gathers[step + 3].shard if step + 3 < 6 else ()
        state = (inputs, attns, projs, outs, norms, feeds, ends, cot_pieces)
        got, more, columns, shard, state, cot_half = tie(got, more, columns, shard, state, cot_half)
        inputs, attns, projs, outs, norms, feeds, ends, cot_pieces = state
        if step + 3 < 6:
            gathers[step + 3].shard = shard
        if step > 0:
            arrived(step)

    outs[1] = to_width([feeds[1][0]], whole[5][0], False, "feed_out")
    outs[1], cot_pieces, norms = tie(outs[1], cot_pieces, norms)
    ends[1] = feed_norm(norms[1][2], outs[1], 1)
    terms = [join_halves(place, in_positions(place, cot_pieces))]

    scatter = Scatter(place)
    columns = [[None] * 3, [None] * 3]
    totals = [[None] * 3, [None] * 3]
    small_grads = [None, None]
    act_value = jnp.where(first_section, ends[0][2], ends[1][2]).reshape(count, local, width)
    attn_parts = back_one = grad_one = None
    act_back = []
    for layer in (1, 0):
        gains = smalls[layer][0]
        u = inputs[layer]
        q, k, v, mixed, lse = attns[layer]
        unit_one, inverse_one, normed_low, sums_one = norms[layer]
        activated, slope = feeds[layer]
        unit_two, inverse_two, output, sums_two = ends[layer]
        w_qkv = whole[3 * layer][0]
        w_proj, w_in, w_out = projs[layer], whole[3 * layer + 1][0], whole[3 * layer + 2][0]

        if layer == 0:
            columns[1][1] = scatter.third(in_parts)
        second = norm_rows_backward(terms, unit_two, inverse_two, gains[1:2], layer == 0)
        grad_ff, second_sums = second[:2]
        out_parts, _ = scatter.product(activated, [grad_ff])
        if layer == 1:
            out_parts, grad_ff, act_value = tie(out_parts, grad_ff, act_value)
            act_back += from_sequences(place, act_value, range(count - 1))
        else:
            grad_one = second[2].reshape(count, local, width)
            out_parts, grad_ff, grad_one, columns = tie(out_parts, grad_ff, grad_one, columns)
            totals[1][1] = scatter.along_z(columns[1][1])
            back_one = from_sequences(place, grad_one, range(2), 1)

        out_parts = scatter.first(out_parts)
        (grad_hidden,) = row_product(
            [grad_ff],
            w_out,
            True,
            [slope],
            [],
            [(ff_half, BF)],
            lambda total, slope: (total * slope.astype(F32),),
            "feed_out_back",
        )
        low = to_width([grad_hidden], w_in, True, "feed_in_back")
        low, grad_hidden, attn_parts = tie(low, grad_hidden, attn_parts)

        if layer == 0:
            attn_parts = scatter.second(attn_parts)
        other = place.sibling(low)
        in_parts, hidden_sums = scatter.product(normed_low, [grad_hidden])
        attn_parts, out_parts, in_parts, low, other = tie(attn_parts, out_parts, in_parts, low, other)

        if layer == 0:
            columns[1][0] = scatter.third(attn_parts)
        out_parts = scatter.second(out_parts)
        in_parts = scatter.first(in_parts)
        grad_branch, first_sums = norm_rows_backward(
            [grad_ff, low, other], unit_one, inverse_one, gains[0:1], False
        )
        (grad_mixed,) = row_product(
            [grad_branch], w_proj, True, [], [], [(half, BF)], lambda total: (total,), "project_out_back"
        )
        grad_w_proj = tn_dot(mixed, grad_branch).astype(BF)
        mine = lax.dynamic_slice_in_dim(grad_w_proj, section * half, half, 1)
        sent = lax.dynamic_slice_in_dim(grad_w_proj, (1 - section) * half, half, 1)
        if layer == 0:
            grad_mixed, columns, sent = tie(grad_mixed, columns, sent)
            totals[1][0] = scatter.along_z(columns[1][0])

        grad_w_proj = place.in_order(mine, place.sibling(sent), 0)
        dq, dk, dv = attend_backward(
            q, k, v, grad_mixed, lse, code_k, seg_q, head_dim, BF if groups == 1 else F32
        )
        if groups > 1:
            dk, dv = scatter_groups(dk), scatter_groups(dv)
        if layer == 1:
            out_parts, in_parts, dq, dk, dv, grad_w_proj, act_back, act_value = tie(
                out_parts, in_parts, dq, dk, dv, grad_w_proj, act_back, act_value
            )
            act_back += from_sequences(place, act_value, [count - 1])
        else:
            out_parts, in_parts, dq, dk, dv, grad_w_proj, back_one, grad_one, totals = tie(
                out_parts, in_parts, dq, dk, dv, grad_w_proj, back_one, grad_one, totals
            )
            back_one += from_sequences(place, grad_one, range(2, count), 1)

        columns[layer][2] = scatter.third(out_parts)
        in_parts = scatter.second(in_parts)
        low = to_width([dq, dk, dv], w_qkv, True, "project_qkv_back")
        low, dq, dk, dv, columns = tie(low, dq, dk, dv, columns)
        totals[layer][2] = scatter.along_z(columns[layer][2])
        other = place.sibling(low)
        attn_parts, dqkv_rows = scatter.product(u, [dq, dk, dv], grad_w_proj)
        in_parts, attn_parts, low, other = tie(in_parts, attn_parts, low, other)
        attn_parts = scatter.first(attn_parts)
        terms = [grad_branch, low, other]

        here = jnp.where(section == layer, 1.0, 0.0)
        spread = jnp.zeros((2, 2, half), F32)
        spread = lax.dynamic_update_slice(spread, dqkv_rows[:half][None, None], (0, section, 0))
        spread = lax.dynamic_update_slice(spread, dqkv_rows[2 * half :][None, None], (1, section, 0))
        ff_spread = lax.dynamic_update_slice(
            jnp.zeros((chips, 2, ff_split), F32), hidden_sums.reshape(chips, 1, ff_split), (0, section, 0)
        )
        rest = jnp.stack(
            [first_sums[0], second_sums[0], first_sums[1], second_sums[1], first_sums[2], second_sums[2]]
        )
        by_chip = jnp.concatenate([here * rest, spread.reshape(2, width)], axis=0).reshape(8, chips, -1)
        by_chip = jnp.moveaxis(by_chip, 1, 0).reshape(chips, -1)
        squares = jnp.concatenate([jnp.sum(sums_one[:2], axis=1), jnp.sum(sums_two[1:3], axis=1)])
        squares = here * jnp.concatenate([squares, jnp.sum(live)[None], jnp.zeros((3,), F32)])
        small_grads[layer] = jnp.concatenate(
            [by_chip, ff_spread.reshape(chips, -1), jnp.broadcast_to(squares, (chips, 8))], axis=1
        )

    totals[0][1] = scatter.along_z(scatter.third(in_parts))
    grad_zero = sum([term.astype(F32) for term in terms]).astype(BF).reshape(count, local, width)
    back_zero = from_sequences(place, grad_zero, range(count), 0)
    mine = jnp.where(first_section, small_grads[0], small_grads[1])
    sent = jnp.where(first_section, small_grads[1], small_grads[0])
    small_rows = mine + place.sibling(sent)
    attn_parts, small_rows, back_one, act_back = tie(attn_parts, small_rows, back_one, act_back)
    attn_parts = scatter.second(attn_parts)
    small_total = small_scatter(place, small_rows)
    totals[0][0] = scatter.along_z(scatter.third(attn_parts))

    def give_back(pieces):
        return place_rotated(pieces, place.ctx % count, count).reshape(1, micro, seqs, local, width)

    activations = give_back(act_back)
    input_grads = give_back([jnp.where(first_section, a, b) for a, b in zip(back_zero, back_one)])

    def halves(index):
        a, b = totals[0][index], totals[1][index]
        mine = jnp.where(first_section, a, b)
        other = place.sibling(jnp.where(first_section, b, a))
        low, high = jnp.where(first_section, mine, other), jnp.where(first_section, other, mine)
        return low.astype(F32), high.astype(F32)

    attn_rows = width // chips
    low, high = halves(0)
    low = low.reshape(attn_rows, 4, half)
    high = high.reshape(attn_rows, 4, half)
    attn = jnp.concatenate([low, high], axis=2)
    grad_qkv = jnp.moveaxis(attn[:, :3], 1, 0)[None]
    grad_out_proj = attn[:, 3][None]
    low, high = halves(1)
    grad_in_weight = jnp.stack(
        [low.reshape(-1, chips, ff_split), high.reshape(-1, chips, ff_split)], axis=2
    ).reshape(1, -1, ff_width)
    low, high = halves(2)
    grad_out_weight = jnp.concatenate([low, high], axis=0)[None]

    per_chip = width // chips
    table = small_total[: 8 * per_chip].reshape(8, per_chip)
    grad_gain = table[0:2][None]
    grad_shift = table[2:4][None]
    grad_proj_bias = jnp.stack([table[6], table[7], table[4], table[5]])[None]
    grad_ff_bias = small_total[8 * per_chip : 8 * per_chip + ff_rows][None]
    sums = small_total[8 * per_chip + ff_rows :]
    rms = jnp.sqrt(sums[:4] / (sums[4] * width))[None]
    return (
        activations,
        input_grads,
        grad_qkv,
        grad_out_proj,
        grad_in_weight,
        grad_out_weight,
        grad_gain,
        grad_shift,
        grad_proj_bias,
        grad_ff_bias,
        rms,
    )


def solution(mesh):
    placed = (
        P(None, "fsdp", "ctx", None),
        P(None, "fsdp", "ctx"),
        P(None, "fsdp", "ctx"),
        P(None, "fsdp", "ctx", None),
        P("section", None, ("ctx", "fsdp"), None),
        P("section", ("ctx", "fsdp"), None),
        P("section", ("ctx", "fsdp"), None),
        P("section", ("ctx", "fsdp"), None),
        P("section", None, None),
        P("section", None, None),
        P("section", None, None),
        P("section", None),
    )
    return jax.shard_map(
        on_device,
        mesh=mesh,
        in_specs=placed,
        out_specs=(
            P("section", None, "fsdp", "ctx", None),
            P("section", None, "fsdp", "ctx", None),
            P("section", None, ("ctx", "fsdp"), None),
            P("section", ("ctx", "fsdp"), None),
            P("section", ("ctx", "fsdp"), None),
            P("section", ("ctx", "fsdp"), None),
            P("section", None, ("ctx", "fsdp")),
            P("section", None, ("ctx", "fsdp")),
            P("section", None, ("ctx", "fsdp")),
            P("section", ("ctx", "fsdp")),
            P("section", None),
        ),
        check_vma=False,
    )
```

```python
import math

import jax
import jax.numpy as jnp
from jax import lax
from jax.experimental import pallas as pl
from jax.experimental.pallas import tpu as pltpu
from jax.sharding import PartitionSpec as P

HEADS = 16
NORM_EPS = 1e-05
MASKED = -1e30
BF = jnp.bfloat16


def priced(flops, bytes_accessed, transcendentals):
    share = 0.35
    return pl.CostEstimate(
        flops=int(share * flops),
        bytes_accessed=int(share * bytes_accessed),
        transcendentals=int(share * transcendentals),
    )


F32 = jnp.float32
MIB = 1024 * 1024


def nt_dot(a, b):
    return lax.dot_general(a, b, (((1,), (1,)), ((), ())), preferred_element_type=F32)


def nn_dot(a, b):
    return lax.dot_general(a, b, (((1,), (0,)), ((), ())), preferred_element_type=F32)


def tn_dot(a, b):
    return lax.dot_general(a, b, (((0,), (0,)), ((), ())), preferred_element_type=F32)


def mask_bias(code_k, seg_q):
    shape = (code_k.shape[0], seg_q.shape[1])
    key_at = lax.broadcasted_iota(jnp.int32, shape, 0)
    query_at = lax.broadcasted_iota(jnp.int32, shape, 1)
    allowed = (code_k == seg_q) | (key_at == query_at)
    return jnp.where(allowed, 0.0, MASKED)


def head_masked(block, head, head_dim):
    lane = lax.broadcasted_iota(jnp.int32, block.shape, 1)
    inside = (lane >= head * head_dim) & (lane < (head + 1) * head_dim)
    return jnp.where(inside, block, jnp.zeros_like(block))


def attend_forward_kernel(head_dim, q_ref, k_ref, v_ref, code_ref, seg_ref, o_ref, lse_ref, bias_ref):
    per = q_ref.shape[1] // head_dim

    @pl.when(pl.program_id(0) == 0)
    def _():
        bias_ref[...] = mask_bias(code_ref[...], seg_ref[...])

    query = (q_ref[...].astype(F32) * head_dim ** (-0.5)).astype(BF)
    keys = k_ref[...]
    values_t = v_ref[...].T
    outs, tops = [], []
    for head in range(per):
        scores = nt_dot(keys, head_masked(query, head, head_dim)) + bias_ref[...]
        top = jnp.max(scores, axis=0, keepdims=True)
        expo = jnp.exp(scores - top)
        total = jnp.sum(expo, axis=0, keepdims=True)
        part = nn_dot(values_t[head * head_dim : (head + 1) * head_dim], expo.astype(BF))
        outs.append(part / total)
        tops.append(top + jnp.log(total))
    o_ref[...] = jnp.concatenate(outs, axis=0).T.astype(BF)
    lse_ref[0] = jnp.concatenate(tops, axis=0)


def attend_backward_kernel(
    head_dim, q_ref, k_ref, v_ref, do_ref, lse_ref, code_ref, seg_ref, dq_ref, dk_ref, dv_ref, bias_ref
):
    rows = q_ref.shape[0]
    block = min(512, rows)
    per = q_ref.shape[1] // head_dim
    scale = head_dim ** (-0.5)

    @pl.when(pl.program_id(0) == 0)
    def _():
        bias_ref[...] = mask_bias(code_ref[...], seg_ref[...])

    keys = k_ref[...]
    keys_t = keys.T
    values = v_ref[...]
    dk, dv = None, None
    for first in range(0, rows, block):
        span = slice(first, first + block)
        query = (q_ref[span, :].astype(F32) * scale).astype(BF)
        grad_out = do_ref[span, :]
        outs = []
        for head in range(per):
            query_h = head_masked(query, head, head_dim)
            grad_h = head_masked(grad_out, head, head_dim)
            scores = nt_dot(keys, query_h) + bias_ref[:, span]
            probs = jnp.exp(scores - lse_ref[0, head : head + 1, span])
            grad_probs = nt_dot(values, grad_h)
            inner = jnp.sum(probs * grad_probs, axis=0, keepdims=True)
            grad_scores = (probs * (grad_probs - inner)).astype(BF)
            dv_part = nn_dot(probs.astype(BF), grad_h)
            dk_part = nn_dot(grad_scores, query_h)
            dv = dv_part if dv is None else dv + dv_part
            dk = dk_part if dk is None else dk + dk_part
            outs.append(nn_dot(keys_t[head * head_dim : (head + 1) * head_dim], grad_scores) * scale)
        dq_ref[span, :] = jnp.concatenate(outs, axis=0).T.astype(BF)
    dk_ref[...] = dk.astype(dk_ref.dtype)
    dv_ref[...] = dv.astype(dv_ref.dtype)


def attend_forward(q, k, v, code_k, seg_q, head_dim):
    rows, width = q.shape
    keys = k.shape[0]
    pair = 2 * head_dim
    cost = priced(
        flops=16 * rows * keys * width, bytes_accessed=8 * rows * width, transcendentals=rows * keys * width // head_dim
    )
    return pl.pallas_call(
        lambda *refs: attend_forward_kernel(head_dim, *refs),
        grid=(width // pair,),
        in_specs=[
            pl.BlockSpec((rows, pair), lambda h: (0, h)),
            pl.BlockSpec((keys, pair), lambda h: (0, h)),
            pl.BlockSpec((keys, pair), lambda h: (0, h)),
            pl.BlockSpec((keys, 1), lambda h: (0, 0)),
            pl.BlockSpec((1, rows), lambda h: (0, 0)),
        ],
        out_specs=[
            pl.BlockSpec((rows, pair), lambda h: (0, h)),
            pl.BlockSpec((1, 2, rows), lambda h: (h, 0, 0)),
        ],
        out_shape=[
            jax.ShapeDtypeStruct((rows, width), BF),
            jax.ShapeDtypeStruct((width // pair, 2, rows), F32),
        ],
        scratch_shapes=[pltpu.VMEM((keys, rows), F32)],
        compiler_params=pltpu.CompilerParams(vmem_limit_bytes=24 * MIB),
        cost_estimate=cost,
        name="attend_forward",
    )(q, k, v, code_k, seg_q)


def attend_backward(q, k, v, grad_out, lse, code_k, seg_q, head_dim, kv_type):
    rows, width = q.shape
    keys = k.shape[0]
    pair = 2 * head_dim
    cost = priced(
        flops=40 * rows * keys * width, bytes_accessed=16 * rows * width, transcendentals=rows * keys * width // head_dim
    )
    return pl.pallas_call(
        lambda *refs: attend_backward_kernel(head_dim, *refs),
        grid=(width // pair,),
        in_specs=[
            pl.BlockSpec((rows, pair), lambda h: (0, h)),
            pl.BlockSpec((keys, pair), lambda h: (0, h)),
            pl.BlockSpec((keys, pair), lambda h: (0, h)),
            pl.BlockSpec((rows, pair), lambda h: (0, h)),
            pl.BlockSpec((1, 2, rows), lambda h: (h, 0, 0)),
            pl.BlockSpec((keys, 1), lambda h: (0, 0)),
            pl.BlockSpec((1, rows), lambda h: (0, 0)),
        ],
        out_specs=[
            pl.BlockSpec((rows, pair), lambda h: (0, h)),
            pl.BlockSpec((keys, pair), lambda h: (0, h)),
            pl.BlockSpec((keys, pair), lambda h: (0, h)),
        ],
        out_shape=[
            jax.ShapeDtypeStruct((rows, width), BF),
            jax.ShapeDtypeStruct((keys, width), kv_type),
            jax.ShapeDtypeStruct((keys, width), kv_type),
        ],
        scratch_shapes=[pltpu.VMEM((keys, rows), F32)],
        compiler_params=pltpu.CompilerParams(vmem_limit_bytes=24 * MIB),
        cost_estimate=cost,
        name="attend_backward",
    )(q, k, v, grad_out, lse, code_k, seg_q)


def row_product(xs, w, transposed, rows_in, consts, outs, finish, name):
    rows = xs[0].shape[0]
    block = min(256, rows)
    widths = [x.shape[1] for x in xs]
    wide = w.shape[0] if transposed else w.shape[1]

    def body(*refs):
        refs = list(refs)
        x_refs = [refs.pop(0) for _ in xs]
        w_ref = refs.pop(0)
        row_refs = [refs.pop(0) for _ in rows_in]
        const_refs = [refs.pop(0) for _ in consts]
        total, first = None, 0
        for x_ref, depth in zip(x_refs, widths):
            if transposed:
                part = nt_dot(x_ref[...], w_ref[:, first : first + depth])
            else:
                part = nn_dot(x_ref[...], w_ref[first : first + depth, :])
            total = part if total is None else total + part
            first += depth
        results = finish(total, *[r[...] for r in row_refs], *[c[...] for c in const_refs])
        for out_ref, value in zip(refs, results):
            out_ref[...] = value.astype(out_ref.dtype)

    return pl.pallas_call(
        body,
        grid=(rows // block,),
        in_specs=[pl.BlockSpec((block, depth), lambda i: (i, 0)) for depth in widths]
        + [pl.BlockSpec(w.shape, lambda i: (0, 0))]
        + [pl.BlockSpec((block, r.shape[1]), lambda i: (i, 0)) for r in rows_in]
        + [pl.BlockSpec(c.shape, lambda i: (0, 0)) for c in consts],
        out_specs=[pl.BlockSpec((block, columns), lambda i: (i, 0)) for columns, _ in outs],
        out_shape=[jax.ShapeDtypeStruct((rows, columns), kind) for columns, kind in outs],
        compiler_params=pltpu.CompilerParams(vmem_limit_bytes=16 * MIB),
        cost_estimate=priced(
            flops=2 * rows * sum(widths) * wide,
            bytes_accessed=2 * (rows * sum(widths) + w.size) + sum(4 * rows * c for c, _ in outs),
            transcendentals=0,
        ),
        name=name,
    )(*xs, w, *rows_in, *consts)


def norm_rows_forward(part, other, before, live, table):
    rows, width = part.shape
    block = min(256, rows)

    def body(part_ref, other_ref, before_ref, live_ref, table_ref, unit_ref, inverse_ref, low_ref, sums_ref):
        start = before_ref[...].astype(F32)
        branch = part_ref[...].astype(F32) + other_ref[...].astype(F32) + table_ref[0:1, :]
        residual = start + branch
        centred = residual - jnp.mean(residual, axis=-1, keepdims=True)
        spread = jnp.mean(centred * centred, axis=-1, keepdims=True)
        inverse = lax.rsqrt(spread + NORM_EPS)
        unit = centred * inverse
        out = unit * table_ref[1:2, :] + table_ref[2:3, :]
        unit_ref[...] = unit.astype(BF)
        inverse_ref[...] = inverse
        low_ref[...] = out.astype(BF)
        real = live_ref[...]

        @pl.when(pl.program_id(0) == 0)
        def _():
            sums_ref[...] = jnp.zeros_like(sums_ref)

        sums_ref[0:1, :] += jnp.sum(real * start * start, axis=0, keepdims=True)
        sums_ref[1:2, :] += jnp.sum(real * branch * branch, axis=0, keepdims=True)
        sums_ref[2:3, :] += jnp.sum(real * out * out, axis=0, keepdims=True)

    by_row = pl.BlockSpec((block, width), lambda i: (i, 0))
    thin = pl.BlockSpec((block, 1), lambda i: (i, 0))
    fixed = pl.BlockSpec((8, width), lambda i: (0, 0))
    return pl.pallas_call(
        body,
        grid=(rows // block,),
        in_specs=[by_row, by_row, by_row, thin, fixed],
        out_specs=[by_row, thin, by_row, fixed],
        out_shape=[
            jax.ShapeDtypeStruct((rows, width), BF),
            jax.ShapeDtypeStruct((rows, 1), F32),
            jax.ShapeDtypeStruct((rows, width), BF),
            jax.ShapeDtypeStruct((8, width), F32),
        ],
        compiler_params=pltpu.CompilerParams(vmem_limit_bytes=12 * MIB),
        cost_estimate=priced(flops=20 * rows * width, bytes_accessed=10 * rows * width, transcendentals=rows),
        name="norm_forward",
    )(part, other, before, live, table)


def norm_rows_backward(terms, unit, inverse, gain, rounded):
    rows, width = unit.shape
    block = min(256, rows)

    def body(*refs):
        refs = list(refs)
        grad = sum([refs.pop(0)[...].astype(F32) for _ in terms])
        unit_ref, inverse_ref, gain_ref = refs[:3]
        low_ref, sums_ref = refs[3:5]
        if rounded:
            refs[5][...] = grad.astype(BF)
            grad = grad.astype(BF).astype(F32)
        unit_rows = unit_ref[...].astype(F32)
        scaled = grad * gain_ref[...]
        result = inverse_ref[...] * (
            scaled
            - jnp.mean(scaled, axis=-1, keepdims=True)
            - unit_rows * jnp.mean(scaled * unit_rows, axis=-1, keepdims=True)
        )
        low = result.astype(BF)
        low_ref[...] = low

        @pl.when(pl.program_id(0) == 0)
        def _():
            sums_ref[...] = jnp.zeros_like(sums_ref)

        sums_ref[0:1, :] += jnp.sum(grad * unit_rows, axis=0, keepdims=True)
        sums_ref[1:2, :] += jnp.sum(grad, axis=0, keepdims=True)
        sums_ref[2:3, :] += jnp.sum(low.astype(F32), axis=0, keepdims=True)

    by_row = pl.BlockSpec((block, width), lambda i: (i, 0))
    thin = pl.BlockSpec((block, 1), lambda i: (i, 0))
    fixed = pl.BlockSpec((8, width), lambda i: (0, 0))
    low_shape = jax.ShapeDtypeStruct((rows, width), BF)
    return pl.pallas_call(
        body,
        grid=(rows // block,),
        in_specs=[by_row] * len(terms) + [by_row, thin, pl.BlockSpec((1, width), lambda i: (0, 0))],
        out_specs=[by_row, fixed] + [by_row] * rounded,
        out_shape=[low_shape, jax.ShapeDtypeStruct((8, width), F32)] + [low_shape] * rounded,
        compiler_params=pltpu.CompilerParams(vmem_limit_bytes=12 * MIB),
        cost_estimate=priced(flops=20 * rows * width, bytes_accessed=10 * rows * width, transcendentals=0),
        name="norm_backward",
    )(*terms, unit, inverse, gain)


def gelu_pair(values):
    cdf = 0.5 * (1.0 + lax.erf(values * (2.0**-0.5)))
    density = jnp.exp(-0.5 * values * values) * ((2.0 * math.pi) ** -0.5)
    return values * cdf, cdf + values * density


class Place:
    def __init__(self):
        self.section = lax.axis_index("section")
        self.ctx = lax.axis_index("ctx")
        fsdp = lax.axis_index("fsdp")
        self.nz = lax.axis_size("ctx")
        self.nf = lax.axis_size("fsdp")
        side = math.isqrt(self.nf)
        self.nx = side if side * side == self.nf else self.nf
        self.ny = self.nf // self.nx
        self.y = fsdp // self.nx
        self.x = fsdp % self.nx

    def from_x(self, value, steps):
        pairs = []
        for f in range(self.nf):
            y, x = divmod(f, self.nx)
            pairs.append((y * self.nx + (x + steps) % self.nx, f))
        return lax.ppermute(value, "fsdp", pairs)

    def from_y(self, value, steps):
        pairs = []
        for f in range(self.nf):
            y, x = divmod(f, self.nx)
            pairs.append((((y + steps) % self.ny) * self.nx + x, f))
        return lax.ppermute(value, "fsdp", pairs)

    def sibling(self, value):
        return lax.ppermute(value, "section", [(0, 1), (1, 0)])

    def in_order(self, own, other, axis):
        first = self.section == 0
        return jnp.concatenate([jnp.where(first, own, other), jnp.where(first, other, own)], axis=axis)


def place_rotated(pieces, first, count):
    out = jnp.zeros((count,) + pieces[0].shape, pieces[0].dtype)
    for r, piece in enumerate(pieces):
        out = lax.dynamic_update_index_in_dim(out, piece, (first + r) % count, 0)
    return out


def tie(*trees):
    return lax.optimization_barrier(trees)


class Gather:
    def __init__(self, place, shard):
        self.place, self.shard = place, shard

    def along_z(self):
        rows, cols = self.shard.shape
        column = lax.all_gather(self.shard, "ctx", axis=0, tiled=True)
        return column.reshape(self.place.nz, rows, cols)

    def first(self, column):
        place = self.place
        from_x = [place.from_x(column, r) for r in range(1, place.nx)]
        from_y = [place.from_y(column, r) for r in range(1, place.ny)]
        return (from_x, from_y)

    def second(self, got):
        place = self.place
        from_x, from_y = got
        half = self.shard.shape[1] // 2
        left = [[place.from_y(piece[..., :half], r) for piece in from_x] for r in range(1, place.ny)]
        right = [[place.from_x(piece[..., half:], r) for r in range(1, place.nx)] for piece in from_y]
        return (left, right)

    def whole(self, column, got, more, split):
        place = self.place
        from_x, from_y = got
        left, right = more
        nz, rows, cols = column.shape
        nx, ny, nf = place.nx, place.ny, place.nf
        half = cols // 2
        diagonal = [(ry, rx) for ry in range(1, ny) for rx in range(1, nx)]
        pieces = [column] + from_x + from_y
        places = [(0, 0)] + [(0, r) for r in range(1, nx)] + [(r, 0) for r in range(1, ny)]
        lefts = [left[ry - 1][rx - 1] for ry, rx in diagonal]
        rights = [right[ry - 1][rx - 1] for ry, rx in diagonal]
        at = jnp.stack([place.y, place.x]).astype(jnp.int32)

        def assemble(at_ref, *refs):
            outs = refs[len(pieces) + 2 * len(diagonal) :]

            def index(ry, rx):
                return ((at_ref[0] + ry) % ny) * nx + (at_ref[1] + rx) % nx

            def put(to, first, value):
                last = first + value.shape[-1]
                if first < split:
                    stop = min(last, split)
                    outs[0][0, to, :, first:stop] = value[:, : stop - first]
                if last > split:
                    start = max(first, split)
                    outs[1][0, to, :, start - split : last - split] = value[:, start - first :]

            for at_piece, ref in zip(places, refs):
                put(index(*at_piece), 0, ref[0])
            for k, at_piece in enumerate(diagonal):
                put(index(*at_piece), 0, refs[len(pieces) + k][0])
                put(index(*at_piece), half, refs[len(pieces) + len(diagonal) + k][0])

        widths = [split] + [cols - split] * (split < cols)
        out = pl.pallas_call(
            assemble,
            grid_spec=pltpu.PrefetchScalarGridSpec(
                num_scalar_prefetch=1,
                grid=(nz,),
                in_specs=[pl.BlockSpec((1, rows, cols), lambda z, at_ref: (z, 0, 0))] * len(pieces)
                + [pl.BlockSpec((1, rows, half), lambda z, at_ref: (z, 0, 0))] * (2 * len(diagonal)),
                out_specs=[pl.BlockSpec((1, nf, rows, w), lambda z, at_ref: (z, 0, 0, 0)) for w in widths],
            ),
            out_shape=[jax.ShapeDtypeStruct((nz, nf, rows, w), column.dtype) for w in widths],
            compiler_params=pltpu.CompilerParams(vmem_limit_bytes=10 * MIB),
            cost_estimate=priced(flops=0, bytes_accessed=4 * nz * nf * rows * cols, transcendentals=0),
            name="assemble",
        )(at, *pieces, *lefts, *rights)
        return [part.reshape(nz * nf * rows, part.shape[-1]) for part in out]


def scatter_sizes(place):
    return place.nz, place.ny, place.nx


class Scatter:
    def __init__(self, place):
        self.place = place
        self.at = jnp.stack([place.y, place.x, place.section]).astype(jnp.int32)

    def product(self, x, grads, ready=None):
        place = self.place
        nz, ny, nx = scatter_sizes(place)
        tokens = x.shape[0]
        span = x.shape[1] // nz
        rows = span // (ny * nx)
        widths = [g.shape[1] for g in grads]
        extra = [] if ready is None else list(ready)
        cols = sum(widths) + (extra[0].shape[1] if extra else 0)
        half = cols // 2

        def body(at_ref, x_ref, *refs):
            refs = list(refs)
            grad_refs = [refs.pop(0) for _ in grads]
            extra_refs = [refs.pop(0) for _ in extra]
            full_ref = refs.pop()
            left_refs = [refs.pop(0) for _ in range(ny)]
            right_refs = [refs.pop(0) for _ in range(nx)]
            sums_ref = refs.pop(0)
            turned = x_ref[...].T
            first = 0
            for ref, wide in zip(grad_refs, widths):
                for start in range(0, wide, 512):
                    stop = min(wide, start + 512)
                    value = nn_dot(turned, ref[:, start:stop]).astype(BF)
                    full_ref[:, :, :, first + start : first + stop] = value.reshape(ny, nx, rows, stop - start)
                first += wide
            if extra:
                here = (pl.program_id(0) < nz // 2) == (at_ref[2] == 0)
                value = jnp.where(here, extra_refs[0][...], extra_refs[1][...])
                full_ref[:, :, :, first:] = value.reshape(ny, nx, rows, cols - first)
            for r, ref in enumerate(left_refs):
                ref[0] = full_ref[(at_ref[0] + r) % ny, :, :, :half]
            for r, ref in enumerate(right_refs):
                for y in range(ny):
                    ref[0, y] = full_ref[y, (at_ref[1] + r) % nx, :, half:]

            @pl.when(pl.program_id(0) == 0)
            def _():
                ones = jnp.ones((8, tokens), BF)
                first = 0
                for ref, wide in zip(grad_refs, widths):
                    sums_ref[:, first : first + wide] = nn_dot(ones, ref[...])
                    first += wide

        out = pl.pallas_call(
            body,
            grid_spec=pltpu.PrefetchScalarGridSpec(
                num_scalar_prefetch=1,
                grid=(nz,),
                in_specs=[pl.BlockSpec((tokens, span), lambda z, at_ref: (0, z))]
                + [pl.BlockSpec((tokens, wide), lambda z, at_ref: (0, 0)) for wide in widths]
                + [pl.BlockSpec((span, e.shape[1]), lambda z, at_ref: (z % (nz // 2), 0)) for e in extra],
                out_specs=[pl.BlockSpec((1, nx, rows, half), lambda z, at_ref: (z, 0, 0, 0))] * ny
                + [pl.BlockSpec((1, ny, rows, half), lambda z, at_ref: (z, 0, 0, 0))] * nx
                + [pl.BlockSpec((8, sum(widths)), lambda z, at_ref: (0, 0))],
                scratch_shapes=[pltpu.VMEM((ny, nx, rows, cols), BF)],
            ),
            out_shape=[jax.ShapeDtypeStruct((nz, nx, rows, half), BF)] * ny
            + [jax.ShapeDtypeStruct((nz, ny, rows, half), BF)] * nx
            + [jax.ShapeDtypeStruct((8, sum(widths)), F32)],
            compiler_params=pltpu.CompilerParams(vmem_limit_bytes=20 * MIB),
            cost_estimate=priced(
                flops=2 * tokens * x.shape[1] * sum(widths),
                bytes_accessed=2 * (x.size + tokens * cols + x.shape[1] * cols),
                transcendentals=0,
            ),
            name="weight_grad",
        )(self.at, x, *grads, *extra)
        return (out[:ny], out[ny : ny + nx]), out[-1][0]

    def first(self, parts):
        place = self.place
        left, right = parts
        left = [left[0]] + [place.from_y(left[r], -r) for r in range(1, place.ny)]
        right = [right[0]] + [place.from_x(right[r], -r) for r in range(1, place.nx)]
        return (left, right)

    def second(self, parts):
        place = self.place
        nz, ny, nx = scatter_sizes(place)
        left, right = parts
        rows, half = left[0].shape[2:]

        def body(at_ref, *refs):
            left_in, right_in = refs[:ny], refs[ny : ny + nx]
            left_out, right_out = refs[ny + nx : ny + 2 * nx], refs[ny + 2 * nx :]
            for r, ref in enumerate(left_out):
                to = (at_ref[1] + r) % nx
                ref[...] = sum([piece[:, to].astype(F32) for piece in left_in]).astype(BF)
            for r, ref in enumerate(right_out):
                to = (at_ref[0] + r) % ny
                ref[...] = sum([piece[:, to].astype(F32) for piece in right_in]).astype(BF)

        out = pl.pallas_call(
            body,
            grid_spec=pltpu.PrefetchScalarGridSpec(
                num_scalar_prefetch=1,
                grid=(1,),
                in_specs=[pl.BlockSpec((nz, nx, rows, half), lambda z, at_ref: (0, 0, 0, 0))] * ny
                + [pl.BlockSpec((nz, ny, rows, half), lambda z, at_ref: (0, 0, 0, 0))] * nx,
                out_specs=[pl.BlockSpec((nz, rows, half), lambda z, at_ref: (0, 0, 0))] * (nx + ny),
            ),
            out_shape=[jax.ShapeDtypeStruct((nz, rows, half), BF)] * (nx + ny),
            compiler_params=pltpu.CompilerParams(vmem_limit_bytes=20 * MIB),
            cost_estimate=priced(flops=0, bytes_accessed=8 * nz * nx * ny * rows * half, transcendentals=0),
            name="scatter_add",
        )(self.at, *left, *right)
        left, right = out[:nx], out[nx:]
        left = [left[0]] + [place.from_x(left[r], -r) for r in range(1, nx)]
        right = [right[0]] + [place.from_y(right[r], -r) for r in range(1, ny)]
        return (left, right)

    def third(self, parts):
        left, right = parts
        both = [sum([piece.astype(F32) for piece in side]) for side in (left, right)]
        column = jnp.concatenate(both, axis=-1).astype(BF)
        return column.reshape(-1, column.shape[-1])

    def along_z(self, column):
        return lax.psum_scatter(column, "ctx", scatter_dimension=0, tiled=True)


def small_scatter(place, value):
    value = value.reshape(place.nz, place.ny, place.nx, -1)

    def pick(part, axis, index):
        return lax.dynamic_index_in_dim(part, index, axis, False)

    total = pick(value, 1, place.y)
    for r in range(1, place.ny):
        total = total + place.from_y(pick(value, 1, (place.y + r) % place.ny), -r)
    value = total
    total = pick(value, 1, place.x)
    for r in range(1, place.nx):
        total = total + place.from_x(pick(value, 1, (place.x + r) % place.nx), -r)
    value = total
    total = pick(value, 0, place.ctx)
    for r in range(1, place.nz):
        pairs = [(z, (z + r) % place.nz) for z in range(place.nz)]
        total = total + lax.ppermute(pick(value, 0, (place.ctx + r) % place.nz), "ctx", pairs)
    return total


def to_pieces(place, value, steps):
    count = value.shape[0]
    groups = place.nz // count
    piece_at = place.ctx % count
    pieces = []
    for k in steps:
        sent = lax.dynamic_index_in_dim(value, (piece_at + k) % count, 0, False)
        pairs = [(z, ((z % count + k) % count) * groups + z // count) for z in range(place.nz)]
        pieces.append(sent if all(a == b for a, b in pairs) else lax.ppermute(sent, "ctx", pairs))
    return pieces


def in_positions(place, pieces):
    count = len(pieces)
    kept_seq = place.ctx // (place.nz // count)
    return place_rotated([pieces[0]] + pieces[:0:-1], kept_seq, count)


def from_sequences(place, value, steps, section=None):
    count = value.shape[0]
    groups = place.nz // count
    kept_seq = place.ctx // groups
    pieces = []
    for k in steps:
        sent = lax.dynamic_index_in_dim(value, (kept_seq - k) % count, 0, False)
        pairs = [(((z % count + k) % count) * groups + z // count, z) for z in range(place.nz)]
        if any(a != b for a, b in pairs):
            if section is None:
                sent = lax.ppermute(sent, "ctx", pairs)
            else:
                first = section * place.nz
                sent = lax.ppermute(sent, ("section", "ctx"), [(first + a, first + b) for a, b in pairs])
        pieces.append(sent)
    return pieces


def half_rows(place, value):
    half = value.shape[1] // 2
    return lax.dynamic_slice_in_dim(value, place.section * half, half, 1)


def join_halves(place, moved):
    other = place.sibling(moved)
    first = place.section == 0
    both = jnp.stack([jnp.where(first, moved, other), jnp.where(first, other, moved)], axis=1)
    return both.reshape(-1, moved.shape[-1])


def on_device(
    tokens,
    segment_ids,
    valid_mask,
    cotangent,
    qkv_weight,
    out_proj,
    in_weight,
    out_weight,
    norm_gain,
    norm_shift,
    proj_bias,
    ff_bias,
):
    place = Place()
    section = place.section
    first_section = section == 0
    micro, seqs, local, width = tokens.shape
    count = micro * seqs
    groups = place.nz // count
    rows = count * local
    head_dim = width // HEADS
    half = width // 2
    ff_width = in_weight.shape[2]
    ff_half = ff_width // 2
    chips = place.nz * place.nf
    ff_rows = out_weight.shape[1]
    ff_split = ff_rows // 2

    def part_of(which):
        qkv_part = lax.dynamic_slice_in_dim(qkv_weight[0], which * half, half, 2)
        proj_part = lax.dynamic_slice_in_dim(out_proj[0], which * half, half, 1)
        in_part = lax.dynamic_index_in_dim(
            in_weight[0].reshape(-1, chips, 2, ff_split), which, 2, False
        ).reshape(-1, ff_half)
        out_part = lax.dynamic_slice_in_dim(out_weight[0], which * ff_split, ff_split, 0)
        attn_part = jnp.concatenate([qkv_part[0], qkv_part[1], qkv_part[2], proj_part], axis=1)
        return (attn_part, in_part, out_part)

    own_parts = part_of(section)
    sent_parts = part_of(1 - section)
    shards = [[None] * 3, [None] * 3]
    for index in range(3):
        other = place.sibling(sent_parts[index])
        shards[0][index] = jnp.where(first_section, own_parts[index], other)
        shards[1][index] = jnp.where(first_section, other, own_parts[index])
    gathers = [Gather(place, shard) for layer in shards for shard in layer]

    def proj_whole(columns):
        mine = lax.dynamic_slice_in_dim(columns, section * half, half, 0)
        sent = lax.dynamic_slice_in_dim(columns, (1 - section) * half, half, 0)
        return place.in_order(mine, place.sibling(sent), 1)

    small_own = jnp.concatenate([norm_gain[0], norm_shift[0], proj_bias[0], ff_bias[0].reshape(-1, width)], axis=0)
    small_other = place.sibling(small_own)
    small = [
        jnp.where(first_section, small_own, small_other),
        jnp.where(first_section, small_other, small_own),
    ]

    def layer_small(layer):
        table = small[layer]
        gains, shifts, biases = table[0:2], table[2:4], table[4:8]
        ff_all = table[8:].reshape(chips, 2, ff_split)
        ff_part = lax.dynamic_index_in_dim(ff_all, section, 1, False).reshape(-1)
        bias_q = lax.dynamic_slice_in_dim(biases[0], section * half, half, 0)
        bias_v = lax.dynamic_slice_in_dim(biases[1], section * half, half, 0)
        bias_qkv = jnp.concatenate([bias_q, jnp.zeros_like(bias_q), bias_v])
        return gains, shifts, biases, ff_part, bias_qkv

    ids = segment_ids.reshape(count, local) * 2 + (valid_mask.reshape(count, local) == 1).astype(jnp.int32)
    ids = in_positions(place, to_pieces(place, ids, range(count))).reshape(rows)
    seg_own = ids // 2
    valid_own = ids % 2

    def over_groups(value, steps):
        pairs = []
        for z in range(place.nz):
            q, g = divmod(z, groups)
            pairs.append((q * groups + (g + steps) % groups, z))
        return lax.ppermute(value, "ctx", pairs)

    def gather_groups(value):
        return jnp.concatenate([value] + [over_groups(value, r) for r in range(1, groups)], axis=0)

    def scatter_groups(value):
        parts = value.reshape(groups, rows, -1)
        total = parts[0]
        for r in range(1, groups):
            total = total + over_groups(parts[r].astype(BF), -r).astype(F32)
        return total.astype(BF)

    code_k = gather_groups(jnp.where(valid_own == 1, seg_own, -1))[:, None]
    seg_q = seg_own[None, :]
    live = valid_own.astype(F32)[:, None]

    token_half = half_rows(place, tokens.reshape(count, local, width))
    cot_half = half_rows(place, cotangent.reshape(count, local, width))
    smalls = [layer_small(layer) for layer in range(2)]

    def project_in(layer_input, w_qkv, layer):
        return row_product(
            [layer_input],
            w_qkv,
            False,
            [],
            [smalls[layer][4][None]],
            [(half, BF)] * 3,
            lambda total, bias: jnp.split(total + bias, 3, axis=1),
            "project_qkv",
        )

    def attention(q, k, v):
        if groups > 1:
            k, v = gather_groups(k), gather_groups(v)
        mixed, lse = attend_forward(q, k, v, code_k, seg_q, head_dim)
        return q, k, v, mixed, lse

    def norm_table(*given):
        return jnp.concatenate([row[None] for row in given] + [jnp.zeros((8 - len(given), width), F32)], axis=0)

    def to_width(xs, w, transposed, name):
        (low,) = row_product(xs, w, transposed, [], [], [(width, BF)], lambda total: (total,), name)
        return low

    def attention_norm(layer_input, low, layer):
        gains, shifts, biases = smalls[layer][:3]
        table = norm_table(biases[2], gains[0], shifts[0])
        return norm_rows_forward(low, place.sibling(low), layer_input, live, table)

    def feed_in(normed_low, w_in, layer):
        activated, slope = gelu_pair(nn_dot(normed_low, w_in) + smalls[layer][3])
        return activated.astype(BF), slope.astype(BF)

    def feed_norm(normed_low, low, layer):
        gains, shifts, biases = smalls[layer][:3]
        table = norm_table(biases[3], gains[1], shifts[1])
        return norm_rows_forward(low, place.sibling(low), normed_low, live, table)

    columns, got, whole, more = [None] * 6, [None] * 6, [None] * 6, [None] * 6

    def near(at):
        got[at] = gathers[at].first(columns[at])

    def far(at):
        more[at] = gathers[at].second(got[at])

    def along_z(at):
        columns[at] = gathers[at].along_z()

    def arrived(at):
        split = 3 * half if at % 3 == 0 else columns[at].shape[2]
        whole[at] = gathers[at].whole(columns[at], got[at], more[at], split)

    def step_end(state, known):
        later = [gathers[at].shard for at in range(3, 6)]
        held = (got, more, columns[:known], later, state)
        held = tie(*held)
        got[:], more[:], columns[:known] = held[0], held[1], held[2]
        for at in range(3, 6):
            gathers[at].shard = held[3][at - 3]
        return held[4]

    token_pieces = to_pieces(place, token_half, range(2))
    along_z(0)
    token_pieces, token_half, code_k, seg_q, live = step_end((token_pieces, token_half, code_k, seg_q, live), 1)

    near(0)
    along_z(1)
    token_pieces += to_pieces(place, token_half, range(2, count))
    token_pieces = step_end(token_pieces, 1)

    far(0)
    along_z(2)
    layer_input = join_halves(place, in_positions(place, token_pieces))
    layer_input = step_end(layer_input, 2)
    arrived(0)

    near(1)
    w_qkv, columns_proj = whole[0]
    projs = [proj_whole(columns_proj), None]
    q, k, v = project_in(layer_input, w_qkv, 0)
    along_z(3)
    columns[2], q, projs = tie(columns[2], q, projs)
    near(2)
    attns = [attention(q, k, v), None]
    outs = [to_width([attns[0][3]], projs[0], False, "project_out"), None]
    layer_input, attns, projs, outs = step_end((layer_input, attns, projs, outs), 4)
    inputs = [layer_input, None]

    far(1)
    far(2)
    along_z(4)
    norms = [attention_norm(inputs[0], outs[0], 0), None]
    norms, cot_half = step_end((norms, cot_half), 5)
    arrived(1)
    arrived(2)

    near(3)
    along_z(5)
    feeds = [feed_in(norms[0][2], whole[1][0], 0), None]
    outs[0] = to_width([feeds[0][0]], whole[2][0], False, "feed_out")
    cot_pieces = to_pieces(place, cot_half, range(count))
    feeds, outs, cot_pieces = step_end((feeds, outs, cot_pieces), 5)

    far(3)
    near(4)
    ends = [feed_norm(norms[0][2], outs[0], 0), None]
    ends = step_end(ends, 6)
    inputs[1] = ends[0][2]
    arrived(3)

    far(4)
    near(5)
    w_qkv, columns_proj = whole[3]
    projs[1] = proj_whole(columns_proj)
    q, k, v = project_in(inputs[1], w_qkv, 1)
    attns[1] = attention(q, k, v)
    outs[1] = to_width([attns[1][3]], projs[1], False, "project_out")
    attns, projs, outs, inputs = step_end((attns, projs, outs, inputs), 6)
    arrived(4)

    far(5)
    norms[1] = attention_norm(inputs[1], outs[1], 1)
    feeds[1] = feed_in(norms[1][2], whole[4][0], 1)
    first_back = from_sequences(place, inputs[1].reshape(count, local, width), range(count - 1), 0)
    norms, feeds, first_back, first_out = step_end((norms, feeds, first_back, inputs[1]), 6)
    arrived(5)

    outs[1] = to_width([feeds[1][0]], whole[5][0], False, "feed_out")
    first_back += from_sequences(place, first_out.reshape(count, local, width), [count - 1], 0)
    outs[1], cot_pieces, norms, first_back = tie(outs[1], cot_pieces, norms, first_back)
    ends[1] = feed_norm(norms[1][2], outs[1], 1)
    terms = [join_halves(place, in_positions(place, cot_pieces))]

    scatter = Scatter(place)
    totals = [[None] * 3, [None] * 3]
    small_grads = [None, None]
    last_out = ends[1][2].reshape(count, local, width)
    last_back = from_sequences(place, last_out, range(count), 1)
    attn_parts = back_one = grad_one = None
    for layer in (1, 0):
        gains = smalls[layer][0]
        u = inputs[layer]
        q, k, v, mixed, lse = attns[layer]
        unit_one, inverse_one, normed_low, sums_one = norms[layer]
        activated, slope = feeds[layer]
        unit_two, inverse_two, output, sums_two = ends[layer]
        w_qkv = whole[3 * layer][0]
        w_proj, w_in, w_out = projs[layer], whole[3 * layer + 1][0], whole[3 * layer + 2][0]

        second = norm_rows_backward(terms, unit_two, inverse_two, gains[1:2], layer == 0)
        grad_ff, second_sums = second[:2]
        out_parts, _ = scatter.product(activated, [grad_ff])
        if layer == 1:
            out_parts, grad_ff = tie(out_parts, grad_ff)
        else:
            grad_one = second[2].reshape(count, local, width)
            out_parts, grad_ff, grad_one = tie(out_parts, grad_ff, grad_one)
            back_one = from_sequences(place, grad_one, range(2), 1)

        out_parts = scatter.first(out_parts)
        (grad_hidden,) = row_product(
            [grad_ff],
            w_out,
            True,
            [slope],
            [],
            [(ff_half, BF)],
            lambda total, slope: (total * slope.astype(F32),),
            "feed_out_back",
        )
        low = to_width([grad_hidden], w_in, True, "feed_in_back")
        in_parts, hidden_sums = scatter.product(normed_low, [grad_hidden])
        low, in_parts, out_parts, attn_parts, last_back = tie(low, in_parts, out_parts, attn_parts, last_back)
        other = place.sibling(low)
        if layer == 0:
            attn_parts = scatter.second(attn_parts)

        out_parts = scatter.second(out_parts)
        in_parts = scatter.first(in_parts)
        grad_branch, first_sums = norm_rows_backward(
            [grad_ff, low, other], unit_one, inverse_one, gains[0:1], False
        )
        (grad_mixed,) = row_product(
            [grad_branch], w_proj, True, [], [], [(half, BF)], lambda total: (total,), "project_out_back"
        )
        grad_w_proj = tn_dot(mixed, grad_branch).astype(BF)
        mine = lax.dynamic_slice_in_dim(grad_w_proj, section * half, half, 1)
        sent = lax.dynamic_slice_in_dim(grad_w_proj, (1 - section) * half, half, 1)
        if layer == 0:
            attn_parts, grad_mixed, sent = tie(attn_parts, grad_mixed, sent)
            totals[1][0] = scatter.along_z(scatter.third(attn_parts))

        grad_w_proj = (mine, place.sibling(sent))
        dq, dk, dv = attend_backward(
            q, k, v, grad_mixed, lse, code_k, seg_q, head_dim, BF if groups == 1 else F32
        )
        if groups > 1:
            dk, dv = scatter_groups(dk), scatter_groups(dv)
        out_parts, in_parts, dq, dk, dv, grad_w_proj, back_one, grad_one, totals = tie(
            out_parts, in_parts, dq, dk, dv, grad_w_proj, back_one, grad_one, totals
        )

        totals[layer][2] = scatter.along_z(scatter.third(out_parts))
        in_parts = scatter.second(in_parts)
        if layer == 0:
            back_one += from_sequences(place, grad_one, range(2, count), 1)
        attn_parts, dqkv_rows = scatter.product(u, [dq, dk, dv], grad_w_proj)
        in_parts, attn_parts, dq, dk, dv = tie(in_parts, attn_parts, dq, dk, dv)
        attn_parts = scatter.first(attn_parts)
        in_column = scatter.third(in_parts)
        low = to_width([dq, dk, dv], w_qkv, True, "project_qkv_back")
        low, in_column = tie(low, in_column)
        totals[layer][1] = scatter.along_z(in_column)
        other = place.sibling(low)
        terms = [grad_branch, low, other]

        here = jnp.where(section == layer, 1.0, 0.0)
        spread = jnp.zeros((2, 2, half), F32)
        spread = lax.dynamic_update_slice(spread, dqkv_rows[:half][None, None], (0, section, 0))
        spread = lax.dynamic_update_slice(spread, dqkv_rows[2 * half :][None, None], (1, section, 0))
        ff_spread = lax.dynamic_update_slice(
            jnp.zeros((chips, 2, ff_split), F32), hidden_sums.reshape(chips, 1, ff_split), (0, section, 0)
        )
        rest = jnp.stack(
            [first_sums[0], second_sums[0], first_sums[1], second_sums[1], first_sums[2], second_sums[2]]
        )
        by_chip = jnp.concatenate([here * rest, spread.reshape(2, width)], axis=0).reshape(8, chips, -1)
        by_chip = jnp.moveaxis(by_chip, 1, 0).reshape(chips, -1)
        squares = jnp.concatenate([jnp.sum(sums_one[:2], axis=1), jnp.sum(sums_two[1:3], axis=1)])
        squares = here * jnp.concatenate([squares, jnp.sum(live)[None], jnp.zeros((3,), F32)])
        small_grads[layer] = jnp.concatenate(
            [by_chip, ff_spread.reshape(chips, -1), jnp.broadcast_to(squares, (chips, 8))], axis=1
        )

    grad_zero = sum([term.astype(F32) for term in terms]).astype(BF).reshape(count, local, width)
    back_zero = from_sequences(place, grad_zero, range(count), 0)
    mine = jnp.where(first_section, small_grads[0], small_grads[1])
    sent = jnp.where(first_section, small_grads[1], small_grads[0])
    small_rows = mine + place.sibling(sent)
    attn_parts, small_rows, first_back, last_back, back_one, grad_zero = tie(
        attn_parts, small_rows, first_back, last_back, back_one, grad_zero
    )
    attn_parts = scatter.second(attn_parts)
    small_total = small_scatter(place, small_rows)
    attn_parts, back_zero = tie(attn_parts, back_zero)
    totals[0][0] = scatter.along_z(scatter.third(attn_parts))

    def give_back(pieces):
        return place_rotated(pieces, place.ctx % count, count).reshape(1, micro, seqs, local, width)

    activations = give_back([jnp.where(first_section, a, b) for a, b in zip(first_back, last_back)])
    input_grads = give_back([jnp.where(first_section, a, b) for a, b in zip(back_zero, back_one)])

    def halves(index):
        a, b = totals[0][index], totals[1][index]
        mine = jnp.where(first_section, a, b)
        other = place.sibling(jnp.where(first_section, b, a))
        low, high = jnp.where(first_section, mine, other), jnp.where(first_section, other, mine)
        return low.astype(F32), high.astype(F32)

    attn_rows = width // chips
    low, high = halves(0)
    low = low.reshape(attn_rows, 4, half)
    high = high.reshape(attn_rows, 4, half)
    attn = jnp.concatenate([low, high], axis=2)
    grad_qkv = jnp.moveaxis(attn[:, :3], 1, 0)[None]
    grad_out_proj = attn[:, 3][None]
    low, high = halves(1)
    grad_in_weight = jnp.stack(
        [low.reshape(-1, chips, ff_split), high.reshape(-1, chips, ff_split)], axis=2
    ).reshape(1, -1, ff_width)
    low, high = halves(2)
    grad_out_weight = jnp.concatenate([low, high], axis=0)[None]

    per_chip = width // chips
    table = small_total[: 8 * per_chip].reshape(8, per_chip)
    grad_gain = table[0:2][None]
    grad_shift = table[2:4][None]
    grad_proj_bias = jnp.stack([table[6], table[7], table[4], table[5]])[None]
    grad_ff_bias = small_total[8 * per_chip : 8 * per_chip + ff_rows][None]
    sums = small_total[8 * per_chip + ff_rows :]
    rms = jnp.sqrt(sums[:4] / (sums[4] * width))[None]
    return (
        activations,
        input_grads,
        grad_qkv,
        grad_out_proj,
        grad_in_weight,
        grad_out_weight,
        grad_gain,
        grad_shift,
        grad_proj_bias,
        grad_ff_bias,
        rms,
    )


def solution(mesh):
    placed = (
        P(None, "fsdp", "ctx", None),
        P(None, "fsdp", "ctx"),
        P(None, "fsdp", "ctx"),
        P(None, "fsdp", "ctx", None),
        P("section", None, ("ctx", "fsdp"), None),
        P("section", ("ctx", "fsdp"), None),
        P("section", ("ctx", "fsdp"), None),
        P("section", ("ctx", "fsdp"), None),
        P("section", None, None),
        P("section", None, None),
        P("section", None, None),
        P("section", None),
    )
    return jax.shard_map(
        on_device,
        mesh=mesh,
        in_specs=placed,
        out_specs=(
            P("section", None, "fsdp", "ctx", None),
            P("section", None, "fsdp", "ctx", None),
            P("section", None, ("ctx", "fsdp"), None),
            P("section", ("ctx", "fsdp"), None),
            P("section", ("ctx", "fsdp"), None),
            P("section", ("ctx", "fsdp"), None),
            P("section", None, ("ctx", "fsdp")),
            P("section", None, ("ctx", "fsdp")),
            P("section", None, ("ctx", "fsdp")),
            P("section", ("ctx", "fsdp")),
            P("section", None),
        ),
        check_vma=False,
    )
```

```python
import math

import jax
import jax.numpy as jnp
from jax import lax
from jax.experimental import pallas as pl
from jax.experimental.pallas import tpu as pltpu
from jax.sharding import PartitionSpec as P

HEADS = 16
NORM_EPS = 1e-05
MASKED = -1e30
BF = jnp.bfloat16


def priced(flops, bytes_accessed, transcendentals):
    share = 0.35
    return pl.CostEstimate(
        flops=int(share * flops),
        bytes_accessed=int(share * bytes_accessed),
        transcendentals=int(share * transcendentals),
    )


F32 = jnp.float32
MIB = 1024 * 1024


def nt_dot(a, b):
    return lax.dot_general(a, b, (((1,), (1,)), ((), ())), preferred_element_type=F32)


def nn_dot(a, b):
    return lax.dot_general(a, b, (((1,), (0,)), ((), ())), preferred_element_type=F32)


def tn_dot(a, b):
    return lax.dot_general(a, b, (((0,), (0,)), ((), ())), preferred_element_type=F32)


def mask_bias(code_k, seg_q):
    shape = (code_k.shape[0], seg_q.shape[1])
    key_at = lax.broadcasted_iota(jnp.int32, shape, 0)
    query_at = lax.broadcasted_iota(jnp.int32, shape, 1)
    allowed = (code_k == seg_q) | (key_at == query_at)
    return jnp.where(allowed, 0.0, MASKED)


def head_masked(block, head, head_dim):
    lane = lax.broadcasted_iota(jnp.int32, block.shape, 1)
    inside = (lane >= head * head_dim) & (lane < (head + 1) * head_dim)
    return jnp.where(inside, block, jnp.zeros_like(block))


def attend_forward_kernel(head_dim, q_ref, k_ref, v_ref, code_ref, seg_ref, o_ref, lse_ref, bias_ref):
    per = q_ref.shape[1] // head_dim

    @pl.when(pl.program_id(0) == 0)
    def _():
        bias_ref[...] = mask_bias(code_ref[...], seg_ref[...])

    query = (q_ref[...].astype(F32) * head_dim ** (-0.5)).astype(BF)
    keys = k_ref[...]
    values_t = v_ref[...].T
    outs, tops = [], []
    for head in range(per):
        scores = nt_dot(keys, head_masked(query, head, head_dim)) + bias_ref[...]
        top = jnp.max(scores, axis=0, keepdims=True)
        expo = jnp.exp(scores - top)
        total = jnp.sum(expo, axis=0, keepdims=True)
        part = nn_dot(values_t[head * head_dim : (head + 1) * head_dim], expo.astype(BF))
        outs.append(part / total)
        tops.append(top + jnp.log(total))
    o_ref[...] = jnp.concatenate(outs, axis=0).T.astype(BF)
    lse_ref[0] = jnp.concatenate(tops, axis=0)


def attend_backward_kernel(
    head_dim, q_ref, k_ref, v_ref, do_ref, lse_ref, code_ref, seg_ref, dq_ref, dk_ref, dv_ref, bias_ref
):
    rows = q_ref.shape[0]
    block = min(512, rows)
    per = q_ref.shape[1] // head_dim
    scale = head_dim ** (-0.5)

    @pl.when(pl.program_id(0) == 0)
    def _():
        bias_ref[...] = mask_bias(code_ref[...], seg_ref[...])

    keys = k_ref[...]
    keys_t = keys.T
    values = v_ref[...]
    dk, dv = None, None
    for first in range(0, rows, block):
        span = slice(first, first + block)
        query = (q_ref[span, :].astype(F32) * scale).astype(BF)
        grad_out = do_ref[span, :]
        outs = []
        for head in range(per):
            query_h = head_masked(query, head, head_dim)
            grad_h = head_masked(grad_out, head, head_dim)
            scores = nt_dot(keys, query_h) + bias_ref[:, span]
            probs = jnp.exp(scores - lse_ref[0, head : head + 1, span])
            grad_probs = nt_dot(values, grad_h)
            inner = jnp.sum(probs * grad_probs, axis=0, keepdims=True)
            grad_scores = (probs * (grad_probs - inner)).astype(BF)
            dv_part = nn_dot(probs.astype(BF), grad_h)
            dk_part = nn_dot(grad_scores, query_h)
            dv = dv_part if dv is None else dv + dv_part
            dk = dk_part if dk is None else dk + dk_part
            outs.append(nn_dot(keys_t[head * head_dim : (head + 1) * head_dim], grad_scores) * scale)
        dq_ref[span, :] = jnp.concatenate(outs, axis=0).T.astype(BF)
    dk_ref[...] = dk.astype(dk_ref.dtype)
    dv_ref[...] = dv.astype(dv_ref.dtype)


def attend_forward(q, k, v, code_k, seg_q, head_dim):
    rows, width = q.shape
    keys = k.shape[0]
    pair = 2 * head_dim
    cost = priced(
        flops=16 * rows * keys * width, bytes_accessed=8 * rows * width, transcendentals=rows * keys * width // head_dim
    )
    return pl.pallas_call(
        lambda *refs: attend_forward_kernel(head_dim, *refs),
        grid=(width // pair,),
        in_specs=[
            pl.BlockSpec((rows, pair), lambda h: (0, h)),
            pl.BlockSpec((keys, pair), lambda h: (0, h)),
            pl.BlockSpec((keys, pair), lambda h: (0, h)),
            pl.BlockSpec((keys, 1), lambda h: (0, 0)),
            pl.BlockSpec((1, rows), lambda h: (0, 0)),
        ],
        out_specs=[
            pl.BlockSpec((rows, pair), lambda h: (0, h)),
            pl.BlockSpec((1, 2, rows), lambda h: (h, 0, 0)),
        ],
        out_shape=[
            jax.ShapeDtypeStruct((rows, width), BF),
            jax.ShapeDtypeStruct((width // pair, 2, rows), F32),
        ],
        scratch_shapes=[pltpu.VMEM((keys, rows), F32)],
        compiler_params=pltpu.CompilerParams(vmem_limit_bytes=24 * MIB),
        cost_estimate=cost,
        name="attend_forward",
    )(q, k, v, code_k, seg_q)


def attend_backward(q, k, v, grad_out, lse, code_k, seg_q, head_dim, kv_type):
    rows, width = q.shape
    keys = k.shape[0]
    pair = 2 * head_dim
    cost = priced(
        flops=40 * rows * keys * width, bytes_accessed=16 * rows * width, transcendentals=rows * keys * width // head_dim
    )
    return pl.pallas_call(
        lambda *refs: attend_backward_kernel(head_dim, *refs),
        grid=(width // pair,),
        in_specs=[
            pl.BlockSpec((rows, pair), lambda h: (0, h)),
            pl.BlockSpec((keys, pair), lambda h: (0, h)),
            pl.BlockSpec((keys, pair), lambda h: (0, h)),
            pl.BlockSpec((rows, pair), lambda h: (0, h)),
            pl.BlockSpec((1, 2, rows), lambda h: (h, 0, 0)),
            pl.BlockSpec((keys, 1), lambda h: (0, 0)),
            pl.BlockSpec((1, rows), lambda h: (0, 0)),
        ],
        out_specs=[
            pl.BlockSpec((rows, pair), lambda h: (0, h)),
            pl.BlockSpec((keys, pair), lambda h: (0, h)),
            pl.BlockSpec((keys, pair), lambda h: (0, h)),
        ],
        out_shape=[
            jax.ShapeDtypeStruct((rows, width), BF),
            jax.ShapeDtypeStruct((keys, width), kv_type),
            jax.ShapeDtypeStruct((keys, width), kv_type),
        ],
        scratch_shapes=[pltpu.VMEM((keys, rows), F32)],
        compiler_params=pltpu.CompilerParams(vmem_limit_bytes=24 * MIB),
        cost_estimate=cost,
        name="attend_backward",
    )(q, k, v, grad_out, lse, code_k, seg_q)


def row_product(xs, w, transposed, rows_in, consts, outs, finish, name):
    rows = xs[0].shape[0]
    block = min(256, rows)
    widths = [x.shape[1] for x in xs]
    wide = w.shape[0] if transposed else w.shape[1]

    def body(*refs):
        refs = list(refs)
        x_refs = [refs.pop(0) for _ in xs]
        w_ref = refs.pop(0)
        row_refs = [refs.pop(0) for _ in rows_in]
        const_refs = [refs.pop(0) for _ in consts]
        total, first = None, 0
        for x_ref, depth in zip(x_refs, widths):
            if transposed:
                part = nt_dot(x_ref[...], w_ref[:, first : first + depth])
            else:
                part = nn_dot(x_ref[...], w_ref[first : first + depth, :])
            total = part if total is None else total + part
            first += depth
        results = finish(total, *[r[...] for r in row_refs], *[c[...] for c in const_refs])
        for out_ref, value in zip(refs, results):
            out_ref[...] = value.astype(out_ref.dtype)

    return pl.pallas_call(
        body,
        grid=(rows // block,),
        in_specs=[pl.BlockSpec((block, depth), lambda i: (i, 0)) for depth in widths]
        + [pl.BlockSpec(w.shape, lambda i: (0, 0))]
        + [pl.BlockSpec((block, r.shape[1]), lambda i: (i, 0)) for r in rows_in]
        + [pl.BlockSpec(c.shape, lambda i: (0, 0)) for c in consts],
        out_specs=[pl.BlockSpec((block, columns), lambda i: (i, 0)) for columns, _ in outs],
        out_shape=[jax.ShapeDtypeStruct((rows, columns), kind) for columns, kind in outs],
        compiler_params=pltpu.CompilerParams(vmem_limit_bytes=16 * MIB),
        cost_estimate=priced(
            flops=2 * rows * sum(widths) * wide,
            bytes_accessed=2 * (rows * sum(widths) + w.size) + sum(4 * rows * c for c, _ in outs),
            transcendentals=0,
        ),
        name=name,
    )(*xs, w, *rows_in, *consts)


def norm_rows_forward(part, other, before, live, table):
    rows, width = part.shape
    block = min(256, rows)

    def body(part_ref, other_ref, before_ref, live_ref, table_ref, unit_ref, inverse_ref, low_ref, sums_ref):
        start = before_ref[...].astype(F32)
        branch = part_ref[...].astype(F32) + other_ref[...].astype(F32) + table_ref[0:1, :]
        residual = start + branch
        centred = residual - jnp.mean(residual, axis=-1, keepdims=True)
        spread = jnp.mean(centred * centred, axis=-1, keepdims=True)
        inverse = lax.rsqrt(spread + NORM_EPS)
        unit = centred * inverse
        out = unit * table_ref[1:2, :] + table_ref[2:3, :]
        unit_ref[...] = unit.astype(BF)
        inverse_ref[...] = inverse
        low_ref[...] = out.astype(BF)
        real = live_ref[...]

        @pl.when(pl.program_id(0) == 0)
        def _():
            sums_ref[...] = jnp.zeros_like(sums_ref)

        sums_ref[0:1, :] += jnp.sum(real * start * start, axis=0, keepdims=True)
        sums_ref[1:2, :] += jnp.sum(real * branch * branch, axis=0, keepdims=True)
        sums_ref[2:3, :] += jnp.sum(real * out * out, axis=0, keepdims=True)

    by_row = pl.BlockSpec((block, width), lambda i: (i, 0))
    thin = pl.BlockSpec((block, 1), lambda i: (i, 0))
    fixed = pl.BlockSpec((8, width), lambda i: (0, 0))
    return pl.pallas_call(
        body,
        grid=(rows // block,),
        in_specs=[by_row, by_row, by_row, thin, fixed],
        out_specs=[by_row, thin, by_row, fixed],
        out_shape=[
            jax.ShapeDtypeStruct((rows, width), BF),
            jax.ShapeDtypeStruct((rows, 1), F32),
            jax.ShapeDtypeStruct((rows, width), BF),
            jax.ShapeDtypeStruct((8, width), F32),
        ],
        compiler_params=pltpu.CompilerParams(vmem_limit_bytes=12 * MIB),
        cost_estimate=priced(flops=20 * rows * width, bytes_accessed=10 * rows * width, transcendentals=rows),
        name="norm_forward",
    )(part, other, before, live, table)


def norm_rows_backward(terms, unit, inverse, gain, rounded):
    rows, width = unit.shape
    block = min(256, rows)

    def body(*refs):
        refs = list(refs)
        grad = sum([refs.pop(0)[...].astype(F32) for _ in terms])
        unit_ref, inverse_ref, gain_ref = refs[:3]
        low_ref, sums_ref = refs[3:5]
        if rounded:
            refs[5][...] = grad.astype(BF)
            grad = grad.astype(BF).astype(F32)
        unit_rows = unit_ref[...].astype(F32)
        scaled = grad * gain_ref[...]
        result = inverse_ref[...] * (
            scaled
            - jnp.mean(scaled, axis=-1, keepdims=True)
            - unit_rows * jnp.mean(scaled * unit_rows, axis=-1, keepdims=True)
        )
        low = result.astype(BF)
        low_ref[...] = low

        @pl.when(pl.program_id(0) == 0)
        def _():
            sums_ref[...] = jnp.zeros_like(sums_ref)

        sums_ref[0:1, :] += jnp.sum(grad * unit_rows, axis=0, keepdims=True)
        sums_ref[1:2, :] += jnp.sum(grad, axis=0, keepdims=True)
        sums_ref[2:3, :] += jnp.sum(low.astype(F32), axis=0, keepdims=True)

    by_row = pl.BlockSpec((block, width), lambda i: (i, 0))
    thin = pl.BlockSpec((block, 1), lambda i: (i, 0))
    fixed = pl.BlockSpec((8, width), lambda i: (0, 0))
    low_shape = jax.ShapeDtypeStruct((rows, width), BF)
    return pl.pallas_call(
        body,
        grid=(rows // block,),
        in_specs=[by_row] * len(terms) + [by_row, thin, pl.BlockSpec((1, width), lambda i: (0, 0))],
        out_specs=[by_row, fixed] + [by_row] * rounded,
        out_shape=[low_shape, jax.ShapeDtypeStruct((8, width), F32)] + [low_shape] * rounded,
        compiler_params=pltpu.CompilerParams(vmem_limit_bytes=12 * MIB),
        cost_estimate=priced(flops=20 * rows * width, bytes_accessed=10 * rows * width, transcendentals=0),
        name="norm_backward",
    )(*terms, unit, inverse, gain)


def gelu_pair(values):
    cdf = 0.5 * (1.0 + lax.erf(values * (2.0**-0.5)))
    density = jnp.exp(-0.5 * values * values) * ((2.0 * math.pi) ** -0.5)
    return values * cdf, cdf + values * density


class Place:
    def __init__(self):
        self.section = lax.axis_index("section")
        self.ctx = lax.axis_index("ctx")
        fsdp = lax.axis_index("fsdp")
        self.nz = lax.axis_size("ctx")
        self.nf = lax.axis_size("fsdp")
        side = math.isqrt(self.nf)
        self.nx = side if side * side == self.nf else self.nf
        self.ny = self.nf // self.nx
        self.y = fsdp // self.nx
        self.x = fsdp % self.nx

    def from_x(self, value, steps):
        pairs = []
        for f in range(self.nf):
            y, x = divmod(f, self.nx)
            pairs.append((y * self.nx + (x + steps) % self.nx, f))
        return lax.ppermute(value, "fsdp", pairs)

    def from_y(self, value, steps):
        pairs = []
        for f in range(self.nf):
            y, x = divmod(f, self.nx)
            pairs.append((((y + steps) % self.ny) * self.nx + x, f))
        return lax.ppermute(value, "fsdp", pairs)

    def sibling(self, value):
        return lax.ppermute(value, "section", [(0, 1), (1, 0)])

    def in_order(self, own, other, axis):
        first = self.section == 0
        return jnp.concatenate([jnp.where(first, own, other), jnp.where(first, other, own)], axis=axis)


def place_rotated(pieces, first, count):
    out = jnp.zeros((count,) + pieces[0].shape, pieces[0].dtype)
    for r, piece in enumerate(pieces):
        out = lax.dynamic_update_index_in_dim(out, piece, (first + r) % count, 0)
    return out


def tie(*trees):
    return lax.optimization_barrier(trees)


class Gather:
    def __init__(self, place, shard):
        self.place, self.shard = place, shard

    def along_z(self):
        rows, cols = self.shard.shape
        column = lax.all_gather(self.shard, "ctx", axis=0, tiled=True)
        return column.reshape(self.place.nz, rows, cols)

    def first(self, column):
        place = self.place
        from_x = [place.from_x(column, r) for r in range(1, place.nx)]
        from_y = [place.from_y(column, r) for r in range(1, place.ny)]
        return (from_x, from_y)

    def second(self, got):
        place = self.place
        from_x, from_y = got
        half = self.shard.shape[1] // 2
        left = [[place.from_y(piece[..., :half], r) for piece in from_x] for r in range(1, place.ny)]
        right = [[place.from_x(piece[..., half:], r) for r in range(1, place.nx)] for piece in from_y]
        return (left, right)

    def whole(self, column, got, more, split):
        place = self.place
        from_x, from_y = got
        left, right = more
        nz, rows, cols = column.shape
        nx, ny, nf = place.nx, place.ny, place.nf
        half = cols // 2
        diagonal = [(ry, rx) for ry in range(1, ny) for rx in range(1, nx)]
        pieces = [column] + from_x + from_y
        places = [(0, 0)] + [(0, r) for r in range(1, nx)] + [(r, 0) for r in range(1, ny)]
        lefts = [left[ry - 1][rx - 1] for ry, rx in diagonal]
        rights = [right[ry - 1][rx - 1] for ry, rx in diagonal]
        at = jnp.stack([place.y, place.x]).astype(jnp.int32)

        def assemble(at_ref, *refs):
            outs = refs[len(pieces) + 2 * len(diagonal) :]

            def index(ry, rx):
                return ((at_ref[0] + ry) % ny) * nx + (at_ref[1] + rx) % nx

            def put(to, first, value):
                last = first + value.shape[-1]
                if first < split:
                    stop = min(last, split)
                    outs[0][0, to, :, first:stop] = value[:, : stop - first]
                if last > split:
                    start = max(first, split)
                    outs[1][0, to, :, start - split : last - split] = value[:, start - first :]

            for at_piece, ref in zip(places, refs):
                put(index(*at_piece), 0, ref[0])
            for k, at_piece in enumerate(diagonal):
                put(index(*at_piece), 0, refs[len(pieces) + k][0])
                put(index(*at_piece), half, refs[len(pieces) + len(diagonal) + k][0])

        widths = [split] + [cols - split] * (split < cols)
        out = pl.pallas_call(
            assemble,
            grid_spec=pltpu.PrefetchScalarGridSpec(
                num_scalar_prefetch=1,
                grid=(nz,),
                in_specs=[pl.BlockSpec((1, rows, cols), lambda z, at_ref: (z, 0, 0))] * len(pieces)
                + [pl.BlockSpec((1, rows, half), lambda z, at_ref: (z, 0, 0))] * (2 * len(diagonal)),
                out_specs=[pl.BlockSpec((1, nf, rows, w), lambda z, at_ref: (z, 0, 0, 0)) for w in widths],
            ),
            out_shape=[jax.ShapeDtypeStruct((nz, nf, rows, w), column.dtype) for w in widths],
            compiler_params=pltpu.CompilerParams(vmem_limit_bytes=10 * MIB),
            cost_estimate=priced(flops=0, bytes_accessed=4 * nz * nf * rows * cols, transcendentals=0),
            name="assemble",
        )(at, *pieces, *lefts, *rights)
        return [part.reshape(nz * nf * rows, part.shape[-1]) for part in out]


def scatter_sizes(place):
    return place.nz, place.ny, place.nx


class Scatter:
    def __init__(self, place):
        self.place = place
        self.at = jnp.stack([place.y, place.x, place.section]).astype(jnp.int32)

    def product(self, x, grads, ready=None):
        place = self.place
        nz, ny, nx = scatter_sizes(place)
        tokens = x.shape[0]
        span = x.shape[1] // nz
        rows = span // (ny * nx)
        widths = [g.shape[1] for g in grads]
        extra = [] if ready is None else list(ready)
        cols = sum(widths) + (extra[0].shape[1] if extra else 0)
        half = cols // 2

        def body(at_ref, x_ref, *refs):
            refs = list(refs)
            grad_refs = [refs.pop(0) for _ in grads]
            extra_refs = [refs.pop(0) for _ in extra]
            full_ref = refs.pop()
            left_refs = [refs.pop(0) for _ in range(ny)]
            right_refs = [refs.pop(0) for _ in range(nx)]
            sums_ref = refs.pop(0)
            turned = x_ref[...].T
            first = 0
            for ref, wide in zip(grad_refs, widths):
                for start in range(0, wide, 512):
                    stop = min(wide, start + 512)
                    value = nn_dot(turned, ref[:, start:stop]).astype(BF)
                    full_ref[:, :, :, first + start : first + stop] = value.reshape(ny, nx, rows, stop - start)
                first += wide
            if extra:
                here = (pl.program_id(0) < nz // 2) == (at_ref[2] == 0)
                value = jnp.where(here, extra_refs[0][...], extra_refs[1][...])
                full_ref[:, :, :, first:] = value.reshape(ny, nx, rows, cols - first)
            for r, ref in enumerate(left_refs):
                ref[0] = full_ref[(at_ref[0] + r) % ny, :, :, :half]
            for r, ref in enumerate(right_refs):
                for y in range(ny):
                    ref[0, y] = full_ref[y, (at_ref[1] + r) % nx, :, half:]

            @pl.when(pl.program_id(0) == 0)
            def _():
                ones = jnp.ones((8, tokens), BF)
                first = 0
                for ref, wide in zip(grad_refs, widths):
                    sums_ref[:, first : first + wide] = nn_dot(ones, ref[...])
                    first += wide

        out = pl.pallas_call(
            body,
            grid_spec=pltpu.PrefetchScalarGridSpec(
                num_scalar_prefetch=1,
                grid=(nz,),
                in_specs=[pl.BlockSpec((tokens, span), lambda z, at_ref: (0, z))]
                + [pl.BlockSpec((tokens, wide), lambda z, at_ref: (0, 0)) for wide in widths]
                + [pl.BlockSpec((span, e.shape[1]), lambda z, at_ref: (z % (nz // 2), 0)) for e in extra],
                out_specs=[pl.BlockSpec((1, nx, rows, half), lambda z, at_ref: (z, 0, 0, 0))] * ny
                + [pl.BlockSpec((1, ny, rows, half), lambda z, at_ref: (z, 0, 0, 0))] * nx
                + [pl.BlockSpec((8, sum(widths)), lambda z, at_ref: (0, 0))],
                scratch_shapes=[pltpu.VMEM((ny, nx, rows, cols), BF)],
            ),
            out_shape=[jax.ShapeDtypeStruct((nz, nx, rows, half), BF)] * ny
            + [jax.ShapeDtypeStruct((nz, ny, rows, half), BF)] * nx
            + [jax.ShapeDtypeStruct((8, sum(widths)), F32)],
            compiler_params=pltpu.CompilerParams(vmem_limit_bytes=20 * MIB),
            cost_estimate=priced(
                flops=2 * tokens * x.shape[1] * sum(widths),
                bytes_accessed=2 * (x.size + tokens * cols + x.shape[1] * cols),
                transcendentals=0,
            ),
            name="weight_grad",
        )(self.at, x, *grads, *extra)
        return (out[:ny], out[ny : ny + nx]), out[-1][0]

    def first(self, parts):
        place = self.place
        left, right = parts
        left = [left[0]] + [place.from_y(left[r], -r) for r in range(1, place.ny)]
        right = [right[0]] + [place.from_x(right[r], -r) for r in range(1, place.nx)]
        return (left, right)

    def second(self, parts):
        place = self.place
        nz, ny, nx = scatter_sizes(place)
        left, right = parts
        rows, half = left[0].shape[2:]

        def body(at_ref, *refs):
            left_in, right_in = refs[:ny], refs[ny : ny + nx]
            left_out, right_out = refs[ny + nx : ny + 2 * nx], refs[ny + 2 * nx :]
            for r, ref in enumerate(left_out):
                to = (at_ref[1] + r) % nx
                ref[...] = sum([piece[:, to].astype(F32) for piece in left_in]).astype(BF)
            for r, ref in enumerate(right_out):
                to = (at_ref[0] + r) % ny
                ref[...] = sum([piece[:, to].astype(F32) for piece in right_in]).astype(BF)

        out = pl.pallas_call(
            body,
            grid_spec=pltpu.PrefetchScalarGridSpec(
                num_scalar_prefetch=1,
                grid=(1,),
                in_specs=[pl.BlockSpec((nz, nx, rows, half), lambda z, at_ref: (0, 0, 0, 0))] * ny
                + [pl.BlockSpec((nz, ny, rows, half), lambda z, at_ref: (0, 0, 0, 0))] * nx,
                out_specs=[pl.BlockSpec((nz, rows, half), lambda z, at_ref: (0, 0, 0))] * (nx + ny),
            ),
            out_shape=[jax.ShapeDtypeStruct((nz, rows, half), BF)] * (nx + ny),
            compiler_params=pltpu.CompilerParams(vmem_limit_bytes=20 * MIB),
            cost_estimate=priced(flops=0, bytes_accessed=8 * nz * nx * ny * rows * half, transcendentals=0),
            name="scatter_add",
        )(self.at, *left, *right)
        left, right = out[:nx], out[nx:]
        left = [left[0]] + [place.from_x(left[r], -r) for r in range(1, nx)]
        right = [right[0]] + [place.from_y(right[r], -r) for r in range(1, ny)]
        return (left, right)

    def third(self, parts):
        left, right = parts
        both = [sum([piece.astype(F32) for piece in side]) for side in (left, right)]
        column = jnp.concatenate(both, axis=-1).astype(BF)
        return column.reshape(-1, column.shape[-1])

    def along_z(self, column):
        return lax.psum_scatter(column, "ctx", scatter_dimension=0, tiled=True)


def small_scatter(place, value):
    value = value.reshape(place.nz, place.ny, place.nx, -1)

    def pick(part, axis, index):
        return lax.dynamic_index_in_dim(part, index, axis, False)

    total = pick(value, 1, place.y)
    for r in range(1, place.ny):
        total = total + place.from_y(pick(value, 1, (place.y + r) % place.ny), -r)
    value = total
    total = pick(value, 1, place.x)
    for r in range(1, place.nx):
        total = total + place.from_x(pick(value, 1, (place.x + r) % place.nx), -r)
    value = total
    total = pick(value, 0, place.ctx)
    for r in range(1, place.nz):
        pairs = [(z, (z + r) % place.nz) for z in range(place.nz)]
        total = total + lax.ppermute(pick(value, 0, (place.ctx + r) % place.nz), "ctx", pairs)
    return total


def to_pieces(place, value, steps):
    count = value.shape[0]
    groups = place.nz // count
    piece_at = place.ctx % count
    pieces = []
    for k in steps:
        sent = lax.dynamic_index_in_dim(value, (piece_at + k) % count, 0, False)
        pairs = [(z, ((z % count + k) % count) * groups + z // count) for z in range(place.nz)]
        pieces.append(sent if all(a == b for a, b in pairs) else lax.ppermute(sent, "ctx", pairs))
    return pieces


def in_positions(place, pieces):
    count = len(pieces)
    kept_seq = place.ctx // (place.nz // count)
    return place_rotated([pieces[0]] + pieces[:0:-1], kept_seq, count)


def from_sequences(place, value, steps, section=None):
    count = value.shape[0]
    groups = place.nz // count
    kept_seq = place.ctx // groups
    pieces = []
    for k in steps:
        sent = lax.dynamic_index_in_dim(value, (kept_seq - k) % count, 0, False)
        pairs = [(((z % count + k) % count) * groups + z // count, z) for z in range(place.nz)]
        if any(a != b for a, b in pairs):
            if section is None:
                sent = lax.ppermute(sent, "ctx", pairs)
            else:
                first = section * place.nz
                sent = lax.ppermute(sent, ("section", "ctx"), [(first + a, first + b) for a, b in pairs])
        pieces.append(sent)
    return pieces


def half_rows(place, value):
    half = value.shape[1] // 2
    return lax.dynamic_slice_in_dim(value, place.section * half, half, 1)


def join_pieces(place, pieces):
    count = len(pieces)
    half, width = pieces[0].shape
    mine = jnp.stack(pieces)
    other = place.sibling(mine)
    at = jnp.stack([place.ctx // (place.nz // count), place.section]).astype(jnp.int32)

    def body(at_ref, mine_ref, other_ref, out_ref):
        out_ref[0, at_ref[1]] = mine_ref[0]
        out_ref[0, 1 - at_ref[1]] = other_ref[0]

    piece = pl.BlockSpec((1, half, width), lambda k, at_ref: (k, 0, 0))
    out = pl.pallas_call(
        body,
        grid_spec=pltpu.PrefetchScalarGridSpec(
            num_scalar_prefetch=1,
            grid=(count,),
            in_specs=[piece, piece],
            out_specs=pl.BlockSpec(
                (1, 2, half, width), lambda k, at_ref: ((at_ref[0] + count - k) % count, 0, 0, 0)
            ),
        ),
        out_shape=jax.ShapeDtypeStruct((count, 2, half, width), mine.dtype),
        compiler_params=pltpu.CompilerParams(vmem_limit_bytes=10 * MIB),
        cost_estimate=priced(flops=0, bytes_accessed=8 * mine.size, transcendentals=0),
        name="join_pieces",
    )(at, mine, other)
    return out.reshape(count * 2 * half, width)


def join_halves(place, moved):
    other = place.sibling(moved)
    first = place.section == 0
    both = jnp.stack([jnp.where(first, moved, other), jnp.where(first, other, moved)], axis=1)
    return both.reshape(-1, moved.shape[-1])


def on_device(
    tokens,
    segment_ids,
    valid_mask,
    cotangent,
    qkv_weight,
    out_proj,
    in_weight,
    out_weight,
    norm_gain,
    norm_shift,
    proj_bias,
    ff_bias,
):
    place = Place()
    section = place.section
    first_section = section == 0
    micro, seqs, local, width = tokens.shape
    count = micro * seqs
    groups = place.nz // count
    rows = count * local
    head_dim = width // HEADS
    half = width // 2
    ff_width = in_weight.shape[2]
    ff_half = ff_width // 2
    chips = place.nz * place.nf
    ff_rows = out_weight.shape[1]
    ff_split = ff_rows // 2

    def part_of(which):
        qkv_part = lax.dynamic_slice_in_dim(qkv_weight[0], which * half, half, 2)
        proj_part = lax.dynamic_slice_in_dim(out_proj[0], which * half, half, 1)
        in_part = lax.dynamic_index_in_dim(
            in_weight[0].reshape(-1, chips, 2, ff_split), which, 2, False
        ).reshape(-1, ff_half)
        out_part = lax.dynamic_slice_in_dim(out_weight[0], which * ff_split, ff_split, 0)
        attn_part = jnp.concatenate([qkv_part[0], qkv_part[1], qkv_part[2], proj_part], axis=1)
        return (attn_part, in_part, out_part)

    own_parts = part_of(section)
    sent_parts = part_of(1 - section)
    shards = [[None] * 3, [None] * 3]
    for index in range(3):
        other = place.sibling(sent_parts[index])
        shards[0][index] = jnp.where(first_section, own_parts[index], other)
        shards[1][index] = jnp.where(first_section, other, own_parts[index])
    gathers = [Gather(place, shard) for layer in shards for shard in layer]

    def proj_whole(columns):
        mine = lax.dynamic_slice_in_dim(columns, section * half, half, 0)
        sent = lax.dynamic_slice_in_dim(columns, (1 - section) * half, half, 0)
        return place.in_order(mine, place.sibling(sent), 1)

    small_own = jnp.concatenate([norm_gain[0], norm_shift[0], proj_bias[0], ff_bias[0].reshape(-1, width)], axis=0)
    small_other = place.sibling(small_own)
    small = [
        jnp.where(first_section, small_own, small_other),
        jnp.where(first_section, small_other, small_own),
    ]

    def layer_small(layer):
        table = small[layer]
        gains, shifts, biases = table[0:2], table[2:4], table[4:8]
        ff_all = table[8:].reshape(chips, 2, ff_split)
        ff_part = lax.dynamic_index_in_dim(ff_all, section, 1, False).reshape(-1)
        bias_q = lax.dynamic_slice_in_dim(biases[0], section * half, half, 0)
        bias_v = lax.dynamic_slice_in_dim(biases[1], section * half, half, 0)
        bias_qkv = jnp.concatenate([bias_q, jnp.zeros_like(bias_q), bias_v])
        return gains, shifts, biases, ff_part, bias_qkv

    ids = segment_ids.reshape(count, local) * 2 + (valid_mask.reshape(count, local) == 1).astype(jnp.int32)
    ids = in_positions(place, to_pieces(place, ids, range(count))).reshape(rows)
    seg_own = ids // 2
    valid_own = ids % 2

    def over_groups(value, steps):
        pairs = []
        for z in range(place.nz):
            q, g = divmod(z, groups)
            pairs.append((q * groups + (g + steps) % groups, z))
        return lax.ppermute(value, "ctx", pairs)

    def gather_groups(value):
        return jnp.concatenate([value] + [over_groups(value, r) for r in range(1, groups)], axis=0)

    def scatter_groups(value):
        parts = value.reshape(groups, rows, -1)
        total = parts[0]
        for r in range(1, groups):
            total = total + over_groups(parts[r].astype(BF), -r).astype(F32)
        return total.astype(BF)

    code_k = gather_groups(jnp.where(valid_own == 1, seg_own, -1))[:, None]
    seg_q = seg_own[None, :]
    live = valid_own.astype(F32)[:, None]

    token_half = half_rows(place, tokens.reshape(count, local, width))
    cot_half = half_rows(place, cotangent.reshape(count, local, width))
    smalls = [layer_small(layer) for layer in range(2)]

    def project_in(layer_input, w_qkv, layer):
        return row_product(
            [layer_input],
            w_qkv,
            False,
            [],
            [smalls[layer][4][None]],
            [(half, BF)] * 3,
            lambda total, bias: jnp.split(total + bias, 3, axis=1),
            "project_qkv",
        )

    def attention(q, k, v):
        if groups > 1:
            k, v = gather_groups(k), gather_groups(v)
        mixed, lse = attend_forward(q, k, v, code_k, seg_q, head_dim)
        return q, k, v, mixed, lse

    def norm_table(*given):
        return jnp.concatenate([row[None] for row in given] + [jnp.zeros((8 - len(given), width), F32)], axis=0)

    def to_width(xs, w, transposed, name):
        (low,) = row_product(xs, w, transposed, [], [], [(width, BF)], lambda total: (total,), name)
        return low

    def attention_norm(layer_input, low, layer):
        gains, shifts, biases = smalls[layer][:3]
        table = norm_table(biases[2], gains[0], shifts[0])
        return norm_rows_forward(low, place.sibling(low), layer_input, live, table)

    def feed_in(normed_low, w_in, layer):
        activated, slope = gelu_pair(nn_dot(normed_low, w_in) + smalls[layer][3])
        return activated.astype(BF), slope.astype(BF)

    def feed_norm(normed_low, low, layer):
        gains, shifts, biases = smalls[layer][:3]
        table = norm_table(biases[3], gains[1], shifts[1])
        return norm_rows_forward(low, place.sibling(low), normed_low, live, table)

    columns, got, whole, more = [None] * 6, [None] * 6, [None] * 6, [None] * 6

    def near(at):
        got[at] = gathers[at].first(columns[at])

    def far(at):
        more[at] = gathers[at].second(got[at])

    def along_z(at):
        columns[at] = gathers[at].along_z()

    def arrived(at):
        split = 3 * half if at % 3 == 0 else columns[at].shape[2]
        whole[at] = gathers[at].whole(columns[at], got[at], more[at], split)

    def step_end(state, known):
        later = [gathers[at].shard for at in range(3, 6)]
        held = (got, more, columns[:known], later, state)
        held = tie(*held)
        got[:], more[:], columns[:known] = held[0], held[1], held[2]
        for at in range(3, 6):
            gathers[at].shard = held[3][at - 3]
        return held[4]

    token_pieces = to_pieces(place, token_half, range(2))
    along_z(0)
    token_pieces, token_half, code_k, seg_q, live = step_end((token_pieces, token_half, code_k, seg_q, live), 1)

    near(0)
    token_pieces += to_pieces(place, token_half, range(2, count))
    held = (token_pieces, gathers[1].shard, gathers[2].shard)
    token_pieces, gathers[1].shard, gathers[2].shard = step_end(held, 1)

    far(0)
    along_z(1)
    along_z(2)
    layer_input = join_pieces(place, token_pieces)
    layer_input = step_end(layer_input, 2)
    arrived(0)

    near(1)
    w_qkv, columns_proj = whole[0]
    projs = [proj_whole(columns_proj), None]
    q, k, v = project_in(layer_input, w_qkv, 0)
    along_z(3)
    columns[2], q, projs, got[1] = tie(columns[2], q, projs, got[1])
    near(2)
    attns = [attention(q, k, v), None]
    outs = [to_width([attns[0][3]], projs[0], False, "project_out"), None]
    layer_input, attns, projs, outs = step_end((layer_input, attns, projs, outs), 4)
    inputs = [layer_input, None]

    far(1)
    far(2)
    along_z(4)
    norms = [attention_norm(inputs[0], outs[0], 0), None]
    norms, cot_half = step_end((norms, cot_half), 5)
    arrived(1)
    arrived(2)

    near(3)
    along_z(5)
    feeds = [feed_in(norms[0][2], whole[1][0], 0), None]
    outs[0] = to_width([feeds[0][0]], whole[2][0], False, "feed_out")
    cot_pieces = to_pieces(place, cot_half, range(count))
    feeds, outs, cot_pieces = step_end((feeds, outs, cot_pieces), 5)

    far(3)
    near(4)
    ends = [feed_norm(norms[0][2], outs[0], 0), None]
    ends = step_end(ends, 6)
    inputs[1] = ends[0][2]
    arrived(3)

    far(4)
    near(5)
    w_qkv, columns_proj = whole[3]
    projs[1] = proj_whole(columns_proj)
    q, k, v = project_in(inputs[1], w_qkv, 1)
    attns[1] = attention(q, k, v)
    outs[1] = to_width([attns[1][3]], projs[1], False, "project_out")
    attns, projs, outs, inputs = step_end((attns, projs, outs, inputs), 6)
    arrived(4)

    far(5)
    norms[1] = attention_norm(inputs[1], outs[1], 1)
    feeds[1] = feed_in(norms[1][2], whole[4][0], 1)
    first_back = from_sequences(place, inputs[1].reshape(count, local, width), range(count - 1), 0)
    norms, feeds, first_back, first_out = step_end((norms, feeds, first_back, inputs[1]), 6)
    arrived(5)

    outs[1] = to_width([feeds[1][0]], whole[5][0], False, "feed_out")
    first_back += from_sequences(place, first_out.reshape(count, local, width), [count - 1], 0)
    outs[1], cot_pieces, norms, first_back = tie(outs[1], cot_pieces, norms, first_back)
    ends[1] = feed_norm(norms[1][2], outs[1], 1)
    terms = [join_pieces(place, cot_pieces)]

    scatter = Scatter(place)
    totals = [[None] * 3, [None] * 3]
    small_grads = [None, None]
    last_out = ends[1][2].reshape(count, local, width)
    last_back = from_sequences(place, last_out, range(count), 1)
    attn_parts = back_one = grad_one = None
    for layer in (1, 0):
        gains = smalls[layer][0]
        u = inputs[layer]
        q, k, v, mixed, lse = attns[layer]
        unit_one, inverse_one, normed_low, sums_one = norms[layer]
        activated, slope = feeds[layer]
        unit_two, inverse_two, output, sums_two = ends[layer]
        w_qkv = whole[3 * layer][0]
        w_proj, w_in, w_out = projs[layer], whole[3 * layer + 1][0], whole[3 * layer + 2][0]

        second = norm_rows_backward(terms, unit_two, inverse_two, gains[1:2], layer == 0)
        grad_ff, second_sums = second[:2]
        out_parts, _ = scatter.product(activated, [grad_ff])
        if layer == 1:
            out_parts, grad_ff = tie(out_parts, grad_ff)
        else:
            grad_one = second[2].reshape(count, local, width)
            out_parts, grad_ff, grad_one = tie(out_parts, grad_ff, grad_one)
            back_one = from_sequences(place, grad_one, range(2), 1)

        out_parts = scatter.first(out_parts)
        (grad_hidden,) = row_product(
            [grad_ff],
            w_out,
            True,
            [slope],
            [],
            [(ff_half, BF)],
            lambda total, slope: (total * slope.astype(F32),),
            "feed_out_back",
        )
        low = to_width([grad_hidden], w_in, True, "feed_in_back")
        in_parts, hidden_sums = scatter.product(normed_low, [grad_hidden])
        low, in_parts, out_parts, attn_parts, last_back = tie(low, in_parts, out_parts, attn_parts, last_back)
        other = place.sibling(low)
        if layer == 0:
            attn_parts = scatter.second(attn_parts)

        out_parts = scatter.second(out_parts)
        in_parts = scatter.first(in_parts)
        grad_branch, first_sums = norm_rows_backward(
            [grad_ff, low, other], unit_one, inverse_one, gains[0:1], False
        )
        (grad_mixed,) = row_product(
            [grad_branch], w_proj, True, [], [], [(half, BF)], lambda total: (total,), "project_out_back"
        )
        grad_w_proj = tn_dot(mixed, grad_branch).astype(BF)
        mine = lax.dynamic_slice_in_dim(grad_w_proj, section * half, half, 1)
        sent = lax.dynamic_slice_in_dim(grad_w_proj, (1 - section) * half, half, 1)
        if layer == 0:
            attn_parts, grad_mixed, sent = tie(attn_parts, grad_mixed, sent)
            totals[1][0] = scatter.along_z(scatter.third(attn_parts))

        grad_w_proj = (mine, place.sibling(sent))
        dq, dk, dv = attend_backward(
            q, k, v, grad_mixed, lse, code_k, seg_q, head_dim, BF if groups == 1 else F32
        )
        if groups > 1:
            dk, dv = scatter_groups(dk), scatter_groups(dv)
        out_parts, in_parts, dq, dk, dv, grad_w_proj, back_one, grad_one, totals = tie(
            out_parts, in_parts, dq, dk, dv, grad_w_proj, back_one, grad_one, totals
        )

        totals[layer][2] = scatter.along_z(scatter.third(out_parts))
        in_parts = scatter.second(in_parts)
        if layer == 0:
            back_one += from_sequences(place, grad_one, range(2, count), 1)
        attn_parts, dqkv_rows = scatter.product(u, [dq, dk, dv], grad_w_proj)
        in_parts, attn_parts, dq, dk, dv = tie(in_parts, attn_parts, dq, dk, dv)
        attn_parts = scatter.first(attn_parts)
        in_column = scatter.third(in_parts)
        low = to_width([dq, dk, dv], w_qkv, True, "project_qkv_back")
        low, in_column = tie(low, in_column)
        totals[layer][1] = scatter.along_z(in_column)
        other = place.sibling(low)
        terms = [grad_branch, low, other]

        here = jnp.where(section == layer, 1.0, 0.0)
        spread = jnp.zeros((2, 2, half), F32)
        spread = lax.dynamic_update_slice(spread, dqkv_rows[:half][None, None], (0, section, 0))
        spread = lax.dynamic_update_slice(spread, dqkv_rows[2 * half :][None, None], (1, section, 0))
        ff_spread = lax.dynamic_update_slice(
            jnp.zeros((chips, 2, ff_split), F32), hidden_sums.reshape(chips, 1, ff_split), (0, section, 0)
        )
        rest = jnp.stack(
            [first_sums[0], second_sums[0], first_sums[1], second_sums[1], first_sums[2], second_sums[2]]
        )
        by_chip = jnp.concatenate([here * rest, spread.reshape(2, width)], axis=0).reshape(8, chips, -1)
        by_chip = jnp.moveaxis(by_chip, 1, 0).reshape(chips, -1)
        squares = jnp.concatenate([jnp.sum(sums_one[:2], axis=1), jnp.sum(sums_two[1:3], axis=1)])
        squares = here * jnp.concatenate([squares, jnp.sum(live)[None], jnp.zeros((3,), F32)])
        small_grads[layer] = jnp.concatenate(
            [by_chip, ff_spread.reshape(chips, -1), jnp.broadcast_to(squares, (chips, 8))], axis=1
        )

    grad_zero = sum([term.astype(F32) for term in terms]).astype(BF).reshape(count, local, width)
    back_zero = from_sequences(place, grad_zero, range(count), 0)
    mine = jnp.where(first_section, small_grads[0], small_grads[1])
    sent = jnp.where(first_section, small_grads[1], small_grads[0])
    small_rows = mine + place.sibling(sent)
    attn_parts, small_rows, first_back, last_back, back_one, grad_zero = tie(
        attn_parts, small_rows, first_back, last_back, back_one, grad_zero
    )
    attn_parts = scatter.second(attn_parts)
    small_total = small_scatter(place, small_rows)
    attn_parts, back_zero = tie(attn_parts, back_zero)
    totals[0][0] = scatter.along_z(scatter.third(attn_parts))

    def give_back(pieces):
        return place_rotated(pieces, place.ctx % count, count).reshape(1, micro, seqs, local, width)

    activations = give_back([jnp.where(first_section, a, b) for a, b in zip(first_back, last_back)])
    input_grads = give_back([jnp.where(first_section, a, b) for a, b in zip(back_zero, back_one)])

    def halves(index):
        a, b = totals[0][index], totals[1][index]
        mine = jnp.where(first_section, a, b)
        other = place.sibling(jnp.where(first_section, b, a))
        low, high = jnp.where(first_section, mine, other), jnp.where(first_section, other, mine)
        return low.astype(F32), high.astype(F32)

    attn_rows = width // chips
    low, high = halves(0)
    low = low.reshape(attn_rows, 4, half)
    high = high.reshape(attn_rows, 4, half)
    attn = jnp.concatenate([low, high], axis=2)
    grad_qkv = jnp.moveaxis(attn[:, :3], 1, 0)[None]
    grad_out_proj = attn[:, 3][None]
    low, high = halves(1)
    grad_in_weight = jnp.stack(
        [low.reshape(-1, chips, ff_split), high.reshape(-1, chips, ff_split)], axis=2
    ).reshape(1, -1, ff_width)
    low, high = halves(2)
    grad_out_weight = jnp.concatenate([low, high], axis=0)[None]

    per_chip = width // chips
    table = small_total[: 8 * per_chip].reshape(8, per_chip)
    grad_gain = table[0:2][None]
    grad_shift = table[2:4][None]
    grad_proj_bias = jnp.stack([table[6], table[7], table[4], table[5]])[None]
    grad_ff_bias = small_total[8 * per_chip : 8 * per_chip + ff_rows][None]
    sums = small_total[8 * per_chip + ff_rows :]
    rms = jnp.sqrt(sums[:4] / (sums[4] * width))[None]
    return (
        activations,
        input_grads,
        grad_qkv,
        grad_out_proj,
        grad_in_weight,
        grad_out_weight,
        grad_gain,
        grad_shift,
        grad_proj_bias,
        grad_ff_bias,
        rms,
    )


def solution(mesh):
    placed = (
        P(None, "fsdp", "ctx", None),
        P(None, "fsdp", "ctx"),
        P(None, "fsdp", "ctx"),
        P(None, "fsdp", "ctx", None),
        P("section", None, ("ctx", "fsdp"), None),
        P("section", ("ctx", "fsdp"), None),
        P("section", ("ctx", "fsdp"), None),
        P("section", ("ctx", "fsdp"), None),
        P("section", None, None),
        P("section", None, None),
        P("section", None, None),
        P("section", None),
    )
    return jax.shard_map(
        on_device,
        mesh=mesh,
        in_specs=placed,
        out_specs=(
            P("section", None, "fsdp", "ctx", None),
            P("section", None, "fsdp", "ctx", None),
            P("section", None, ("ctx", "fsdp"), None),
            P("section", ("ctx", "fsdp"), None),
            P("section", ("ctx", "fsdp"), None),
            P("section", ("ctx", "fsdp"), None),
            P("section", None, ("ctx", "fsdp")),
            P("section", None, ("ctx", "fsdp")),
            P("section", None, ("ctx", "fsdp")),
            P("section", ("ctx", "fsdp")),
            P("section", None),
        ),
        check_vma=False,
    )
```

```python
import math

import jax
import jax.numpy as jnp
from jax import lax
from jax.experimental import pallas as pl
from jax.experimental.pallas import tpu as pltpu
from jax.sharding import PartitionSpec as P

HEADS = 16
NORM_EPS = 1e-05
MASKED = -1e30
BF = jnp.bfloat16


def priced(flops, bytes_accessed, transcendentals):
    share = 0.35
    return pl.CostEstimate(
        flops=int(share * flops),
        bytes_accessed=int(share * bytes_accessed),
        transcendentals=int(share * transcendentals),
    )


F32 = jnp.float32
MIB = 1024 * 1024


def nt_dot(a, b):
    return lax.dot_general(a, b, (((1,), (1,)), ((), ())), preferred_element_type=F32)


def nn_dot(a, b):
    return lax.dot_general(a, b, (((1,), (0,)), ((), ())), preferred_element_type=F32)


def tn_dot(a, b):
    return lax.dot_general(a, b, (((0,), (0,)), ((), ())), preferred_element_type=F32)


def mask_bias(code_k, seg_q):
    shape = (code_k.shape[0], seg_q.shape[1])
    key_at = lax.broadcasted_iota(jnp.int32, shape, 0)
    query_at = lax.broadcasted_iota(jnp.int32, shape, 1)
    allowed = (code_k == seg_q) | (key_at == query_at)
    return jnp.where(allowed, 0.0, MASKED)


def head_masked(block, head, head_dim):
    lane = lax.broadcasted_iota(jnp.int32, block.shape, 1)
    inside = (lane >= head * head_dim) & (lane < (head + 1) * head_dim)
    return jnp.where(inside, block, jnp.zeros_like(block))


def attend_forward_kernel(head_dim, q_ref, k_ref, v_ref, code_ref, seg_ref, o_ref, lse_ref, bias_ref):
    per = q_ref.shape[1] // head_dim

    @pl.when(pl.program_id(0) == 0)
    def _():
        bias_ref[...] = mask_bias(code_ref[...], seg_ref[...])

    query = (q_ref[...].astype(F32) * head_dim ** (-0.5)).astype(BF)
    keys = k_ref[...]
    values_t = v_ref[...].T
    outs, tops = [], []
    for head in range(per):
        scores = nt_dot(keys, head_masked(query, head, head_dim)) + bias_ref[...]
        top = jnp.max(scores, axis=0, keepdims=True)
        expo = jnp.exp(scores - top)
        total = jnp.sum(expo, axis=0, keepdims=True)
        part = nn_dot(values_t[head * head_dim : (head + 1) * head_dim], expo.astype(BF))
        outs.append(part / total)
        tops.append(top + jnp.log(total))
    o_ref[...] = jnp.concatenate(outs, axis=0).T.astype(BF)
    lse_ref[0] = jnp.concatenate(tops, axis=0)


def attend_backward_kernel(
    head_dim, q_ref, k_ref, v_ref, do_ref, lse_ref, code_ref, seg_ref, dq_ref, dk_ref, dv_ref, bias_ref
):
    rows = q_ref.shape[0]
    block = min(512, rows)
    per = q_ref.shape[1] // head_dim
    scale = head_dim ** (-0.5)

    @pl.when(pl.program_id(0) == 0)
    def _():
        bias_ref[...] = mask_bias(code_ref[...], seg_ref[...])

    keys = k_ref[...]
    keys_t = keys.T
    values = v_ref[...]
    dk, dv = None, None
    for first in range(0, rows, block):
        span = slice(first, first + block)
        query = (q_ref[span, :].astype(F32) * scale).astype(BF)
        grad_out = do_ref[span, :]
        outs = []
        for head in range(per):
            query_h = head_masked(query, head, head_dim)
            grad_h = head_masked(grad_out, head, head_dim)
            scores = nt_dot(keys, query_h) + bias_ref[:, span]
            probs = jnp.exp(scores - lse_ref[0, head : head + 1, span])
            grad_probs = nt_dot(values, grad_h)
            inner = jnp.sum(probs * grad_probs, axis=0, keepdims=True)
            grad_scores = (probs * (grad_probs - inner)).astype(BF)
            dv_part = nn_dot(probs.astype(BF), grad_h)
            dk_part = nn_dot(grad_scores, query_h)
            dv = dv_part if dv is None else dv + dv_part
            dk = dk_part if dk is None else dk + dk_part
            outs.append(nn_dot(keys_t[head * head_dim : (head + 1) * head_dim], grad_scores) * scale)
        dq_ref[span, :] = jnp.concatenate(outs, axis=0).T.astype(BF)
    dk_ref[...] = dk.astype(dk_ref.dtype)
    dv_ref[...] = dv.astype(dv_ref.dtype)


def attend_forward(q, k, v, code_k, seg_q, head_dim):
    rows, width = q.shape
    keys = k.shape[0]
    pair = 2 * head_dim
    cost = priced(
        flops=16 * rows * keys * width, bytes_accessed=8 * rows * width, transcendentals=rows * keys * width // head_dim
    )
    return pl.pallas_call(
        lambda *refs: attend_forward_kernel(head_dim, *refs),
        grid=(width // pair,),
        in_specs=[
            pl.BlockSpec((rows, pair), lambda h: (0, h)),
            pl.BlockSpec((keys, pair), lambda h: (0, h)),
            pl.BlockSpec((keys, pair), lambda h: (0, h)),
            pl.BlockSpec((keys, 1), lambda h: (0, 0)),
            pl.BlockSpec((1, rows), lambda h: (0, 0)),
        ],
        out_specs=[
            pl.BlockSpec((rows, pair), lambda h: (0, h)),
            pl.BlockSpec((1, 2, rows), lambda h: (h, 0, 0)),
        ],
        out_shape=[
            jax.ShapeDtypeStruct((rows, width), BF),
            jax.ShapeDtypeStruct((width // pair, 2, rows), F32),
        ],
        scratch_shapes=[pltpu.VMEM((keys, rows), F32)],
        compiler_params=pltpu.CompilerParams(vmem_limit_bytes=24 * MIB),
        cost_estimate=cost,
        name="attend_forward",
    )(q, k, v, code_k, seg_q)


def attend_backward(q, k, v, grad_out, lse, code_k, seg_q, head_dim, kv_type):
    rows, width = q.shape
    keys = k.shape[0]
    pair = 2 * head_dim
    cost = priced(
        flops=40 * rows * keys * width, bytes_accessed=16 * rows * width, transcendentals=rows * keys * width // head_dim
    )
    return pl.pallas_call(
        lambda *refs: attend_backward_kernel(head_dim, *refs),
        grid=(width // pair,),
        in_specs=[
            pl.BlockSpec((rows, pair), lambda h: (0, h)),
            pl.BlockSpec((keys, pair), lambda h: (0, h)),
            pl.BlockSpec((keys, pair), lambda h: (0, h)),
            pl.BlockSpec((rows, pair), lambda h: (0, h)),
            pl.BlockSpec((1, 2, rows), lambda h: (h, 0, 0)),
            pl.BlockSpec((keys, 1), lambda h: (0, 0)),
            pl.BlockSpec((1, rows), lambda h: (0, 0)),
        ],
        out_specs=[
            pl.BlockSpec((rows, pair), lambda h: (0, h)),
            pl.BlockSpec((keys, pair), lambda h: (0, h)),
            pl.BlockSpec((keys, pair), lambda h: (0, h)),
        ],
        out_shape=[
            jax.ShapeDtypeStruct((rows, width), BF),
            jax.ShapeDtypeStruct((keys, width), kv_type),
            jax.ShapeDtypeStruct((keys, width), kv_type),
        ],
        scratch_shapes=[pltpu.VMEM((keys, rows), F32)],
        compiler_params=pltpu.CompilerParams(vmem_limit_bytes=24 * MIB),
        cost_estimate=cost,
        name="attend_backward",
    )(q, k, v, grad_out, lse, code_k, seg_q)


def row_product(xs, w, transposed, rows_in, consts, outs, finish, name):
    rows = xs[0].shape[0]
    block = min(256, rows)
    widths = [x.shape[1] for x in xs]
    wide = w.shape[0] if transposed else w.shape[1]

    def body(*refs):
        refs = list(refs)
        x_refs = [refs.pop(0) for _ in xs]
        w_ref = refs.pop(0)
        row_refs = [refs.pop(0) for _ in rows_in]
        const_refs = [refs.pop(0) for _ in consts]
        total, first = None, 0
        for x_ref, depth in zip(x_refs, widths):
            if transposed:
                part = nt_dot(x_ref[...], w_ref[:, first : first + depth])
            else:
                part = nn_dot(x_ref[...], w_ref[first : first + depth, :])
            total = part if total is None else total + part
            first += depth
        results = finish(total, *[r[...] for r in row_refs], *[c[...] for c in const_refs])
        for out_ref, value in zip(refs, results):
            out_ref[...] = value.astype(out_ref.dtype)

    return pl.pallas_call(
        body,
        grid=(rows // block,),
        in_specs=[pl.BlockSpec((block, depth), lambda i: (i, 0)) for depth in widths]
        + [pl.BlockSpec(w.shape, lambda i: (0, 0))]
        + [pl.BlockSpec((block, r.shape[1]), lambda i: (i, 0)) for r in rows_in]
        + [pl.BlockSpec(c.shape, lambda i: (0, 0)) for c in consts],
        out_specs=[pl.BlockSpec((block, columns), lambda i: (i, 0)) for columns, _ in outs],
        out_shape=[jax.ShapeDtypeStruct((rows, columns), kind) for columns, kind in outs],
        compiler_params=pltpu.CompilerParams(vmem_limit_bytes=16 * MIB),
        cost_estimate=priced(
            flops=2 * rows * sum(widths) * wide,
            bytes_accessed=2 * (rows * sum(widths) + w.size) + sum(4 * rows * c for c, _ in outs),
            transcendentals=0,
        ),
        name=name,
    )(*xs, w, *rows_in, *consts)


def norm_rows_forward(part, other, before, live, table):
    rows, width = part.shape
    block = min(256, rows)

    def body(part_ref, other_ref, before_ref, live_ref, table_ref, unit_ref, inverse_ref, low_ref, sums_ref):
        start = before_ref[...].astype(F32)
        branch = part_ref[...].astype(F32) + other_ref[...].astype(F32) + table_ref[0:1, :]
        residual = start + branch
        centred = residual - jnp.mean(residual, axis=-1, keepdims=True)
        spread = jnp.mean(centred * centred, axis=-1, keepdims=True)
        inverse = lax.rsqrt(spread + NORM_EPS)
        unit = centred * inverse
        out = unit * table_ref[1:2, :] + table_ref[2:3, :]
        unit_ref[...] = unit.astype(BF)
        inverse_ref[...] = inverse
        low_ref[...] = out.astype(BF)
        real = live_ref[...]

        @pl.when(pl.program_id(0) == 0)
        def _():
            sums_ref[...] = jnp.zeros_like(sums_ref)

        sums_ref[0:1, :] += jnp.sum(real * start * start, axis=0, keepdims=True)
        sums_ref[1:2, :] += jnp.sum(real * branch * branch, axis=0, keepdims=True)
        sums_ref[2:3, :] += jnp.sum(real * out * out, axis=0, keepdims=True)

    by_row = pl.BlockSpec((block, width), lambda i: (i, 0))
    thin = pl.BlockSpec((block, 1), lambda i: (i, 0))
    fixed = pl.BlockSpec((8, width), lambda i: (0, 0))
    return pl.pallas_call(
        body,
        grid=(rows // block,),
        in_specs=[by_row, by_row, by_row, thin, fixed],
        out_specs=[by_row, thin, by_row, fixed],
        out_shape=[
            jax.ShapeDtypeStruct((rows, width), BF),
            jax.ShapeDtypeStruct((rows, 1), F32),
            jax.ShapeDtypeStruct((rows, width), BF),
            jax.ShapeDtypeStruct((8, width), F32),
        ],
        compiler_params=pltpu.CompilerParams(vmem_limit_bytes=12 * MIB),
        cost_estimate=priced(flops=20 * rows * width, bytes_accessed=10 * rows * width, transcendentals=rows),
        name="norm_forward",
    )(part, other, before, live, table)


def norm_rows_backward(terms, unit, inverse, gain, rounded):
    rows, width = unit.shape
    block = min(256, rows)

    def body(*refs):
        refs = list(refs)
        grad = sum([refs.pop(0)[...].astype(F32) for _ in terms])
        unit_ref, inverse_ref, gain_ref = refs[:3]
        low_ref, sums_ref = refs[3:5]
        if rounded:
            refs[5][...] = grad.astype(BF)
            grad = grad.astype(BF).astype(F32)
        unit_rows = unit_ref[...].astype(F32)
        scaled = grad * gain_ref[...]
        result = inverse_ref[...] * (
            scaled
            - jnp.mean(scaled, axis=-1, keepdims=True)
            - unit_rows * jnp.mean(scaled * unit_rows, axis=-1, keepdims=True)
        )
        low = result.astype(BF)
        low_ref[...] = low

        @pl.when(pl.program_id(0) == 0)
        def _():
            sums_ref[...] = jnp.zeros_like(sums_ref)

        sums_ref[0:1, :] += jnp.sum(grad * unit_rows, axis=0, keepdims=True)
        sums_ref[1:2, :] += jnp.sum(grad, axis=0, keepdims=True)
        sums_ref[2:3, :] += jnp.sum(low.astype(F32), axis=0, keepdims=True)

    by_row = pl.BlockSpec((block, width), lambda i: (i, 0))
    thin = pl.BlockSpec((block, 1), lambda i: (i, 0))
    fixed = pl.BlockSpec((8, width), lambda i: (0, 0))
    low_shape = jax.ShapeDtypeStruct((rows, width), BF)
    return pl.pallas_call(
        body,
        grid=(rows // block,),
        in_specs=[by_row] * len(terms) + [by_row, thin, pl.BlockSpec((1, width), lambda i: (0, 0))],
        out_specs=[by_row, fixed] + [by_row] * rounded,
        out_shape=[low_shape, jax.ShapeDtypeStruct((8, width), F32)] + [low_shape] * rounded,
        compiler_params=pltpu.CompilerParams(vmem_limit_bytes=12 * MIB),
        cost_estimate=priced(flops=20 * rows * width, bytes_accessed=10 * rows * width, transcendentals=0),
        name="norm_backward",
    )(*terms, unit, inverse, gain)


def gelu_pair(values):
    cdf = 0.5 * (1.0 + lax.erf(values * (2.0**-0.5)))
    density = jnp.exp(-0.5 * values * values) * ((2.0 * math.pi) ** -0.5)
    return values * cdf, cdf + values * density


class Place:
    def __init__(self):
        self.section = lax.axis_index("section")
        self.ctx = lax.axis_index("ctx")
        fsdp = lax.axis_index("fsdp")
        self.nz = lax.axis_size("ctx")
        self.nf = lax.axis_size("fsdp")
        side = math.isqrt(self.nf)
        self.nx = side if side * side == self.nf else self.nf
        self.ny = self.nf // self.nx
        self.y = fsdp // self.nx
        self.x = fsdp % self.nx

    def from_x(self, value, steps):
        pairs = []
        for f in range(self.nf):
            y, x = divmod(f, self.nx)
            pairs.append((y * self.nx + (x + steps) % self.nx, f))
        return lax.ppermute(value, "fsdp", pairs)

    def from_y(self, value, steps):
        pairs = []
        for f in range(self.nf):
            y, x = divmod(f, self.nx)
            pairs.append((((y + steps) % self.ny) * self.nx + x, f))
        return lax.ppermute(value, "fsdp", pairs)

    def sibling(self, value):
        return lax.ppermute(value, "section", [(0, 1), (1, 0)])

    def in_order(self, own, other, axis):
        first = self.section == 0
        return jnp.concatenate([jnp.where(first, own, other), jnp.where(first, other, own)], axis=axis)


def place_rotated(pieces, first, count):
    out = jnp.zeros((count,) + pieces[0].shape, pieces[0].dtype)
    for r, piece in enumerate(pieces):
        out = lax.dynamic_update_index_in_dim(out, piece, (first + r) % count, 0)
    return out


def tie(*trees):
    return lax.optimization_barrier(trees)


class Gather:
    def __init__(self, place, shard):
        self.place, self.shard = place, shard

    def along_z(self):
        rows, cols = self.shard.shape
        column = lax.all_gather(self.shard, "ctx", axis=0, tiled=True)
        return column.reshape(self.place.nz, rows, cols)

    def first(self, column):
        place = self.place
        from_x = [place.from_x(column, r) for r in range(1, place.nx)]
        from_y = [place.from_y(column, r) for r in range(1, place.ny)]
        return (from_x, from_y)

    def second(self, got):
        place = self.place
        from_x, from_y = got
        half = self.shard.shape[1] // 2
        left = [[place.from_y(piece[..., :half], r) for piece in from_x] for r in range(1, place.ny)]
        right = [[place.from_x(piece[..., half:], r) for r in range(1, place.nx)] for piece in from_y]
        return (left, right)

    def whole(self, column, got, more, split):
        place = self.place
        from_x, from_y = got
        left, right = more
        nz, rows, cols = column.shape
        nx, ny, nf = place.nx, place.ny, place.nf
        half = cols // 2
        diagonal = [(ry, rx) for ry in range(1, ny) for rx in range(1, nx)]
        pieces = [column] + from_x + from_y
        places = [(0, 0)] + [(0, r) for r in range(1, nx)] + [(r, 0) for r in range(1, ny)]
        lefts = [left[ry - 1][rx - 1] for ry, rx in diagonal]
        rights = [right[ry - 1][rx - 1] for ry, rx in diagonal]
        at = jnp.stack([place.y, place.x]).astype(jnp.int32)

        def assemble(at_ref, *refs):
            outs = refs[len(pieces) + 2 * len(diagonal) :]

            def index(ry, rx):
                return ((at_ref[0] + ry) % ny) * nx + (at_ref[1] + rx) % nx

            def put(to, first, value):
                last = first + value.shape[-1]
                if first < split:
                    stop = min(last, split)
                    outs[0][0, to, :, first:stop] = value[:, : stop - first]
                if last > split:
                    start = max(first, split)
                    outs[1][0, to, :, start - split : last - split] = value[:, start - first :]

            for at_piece, ref in zip(places, refs):
                put(index(*at_piece), 0, ref[0])
            for k, at_piece in enumerate(diagonal):
                put(index(*at_piece), 0, refs[len(pieces) + k][0])
                put(index(*at_piece), half, refs[len(pieces) + len(diagonal) + k][0])

        widths = [split] + [cols - split] * (split < cols)
        out = pl.pallas_call(
            assemble,
            grid_spec=pltpu.PrefetchScalarGridSpec(
                num_scalar_prefetch=1,
                grid=(nz,),
                in_specs=[pl.BlockSpec((1, rows, cols), lambda z, at_ref: (z, 0, 0))] * len(pieces)
                + [pl.BlockSpec((1, rows, half), lambda z, at_ref: (z, 0, 0))] * (2 * len(diagonal)),
                out_specs=[pl.BlockSpec((1, nf, rows, w), lambda z, at_ref: (z, 0, 0, 0)) for w in widths],
            ),
            out_shape=[jax.ShapeDtypeStruct((nz, nf, rows, w), column.dtype) for w in widths],
            compiler_params=pltpu.CompilerParams(vmem_limit_bytes=10 * MIB),
            cost_estimate=priced(flops=0, bytes_accessed=4 * nz * nf * rows * cols, transcendentals=0),
            name="assemble",
        )(at, *pieces, *lefts, *rights)
        return [part.reshape(nz * nf * rows, part.shape[-1]) for part in out]


def scatter_sizes(place):
    return place.nz, place.ny, place.nx


class Scatter:
    def __init__(self, place):
        self.place = place
        self.at = jnp.stack([place.y, place.x, place.section]).astype(jnp.int32)

    def product(self, x, grads, ready=None, sums=True):
        place = self.place
        nz, ny, nx = scatter_sizes(place)
        tokens = x.shape[0]
        span = x.shape[1] // nz
        rows = span // (ny * nx)
        widths = [g.shape[1] for g in grads]
        extra = [] if ready is None else list(ready)
        cols = sum(widths) + (extra[0].shape[1] if extra else 0)
        half = cols // 2

        def body(at_ref, x_ref, *refs):
            refs = list(refs)
            grad_refs = [refs.pop(0) for _ in grads]
            extra_refs = [refs.pop(0) for _ in extra]
            full_ref = refs.pop()
            left_refs = [refs.pop(0) for _ in range(ny)]
            right_refs = [refs.pop(0) for _ in range(nx)]
            sums_ref = refs.pop(0)
            turned = x_ref[...].T
            first = 0
            for ref, wide in zip(grad_refs, widths):
                for start in range(0, wide, 512):
                    stop = min(wide, start + 512)
                    value = nn_dot(turned, ref[:, start:stop]).astype(BF)
                    full_ref[:, :, :, first + start : first + stop] = value.reshape(ny, nx, rows, stop - start)
                first += wide
            if extra:
                here = (pl.program_id(0) < nz // 2) == (at_ref[2] == 0)
                value = jnp.where(here, extra_refs[0][...], extra_refs[1][...])
                full_ref[:, :, :, first:] = value.reshape(ny, nx, rows, cols - first)
            for r, ref in enumerate(left_refs):
                ref[0] = full_ref[(at_ref[0] + r) % ny, :, :, :half]
            for r, ref in enumerate(right_refs):
                for y in range(ny):
                    ref[0, y] = full_ref[y, (at_ref[1] + r) % nx, :, half:]

            @pl.when(pl.program_id(0) == 0)
            def _():
                if not sums:
                    sums_ref[...] = jnp.zeros_like(sums_ref)
                    return
                ones = jnp.ones((8, tokens), BF)
                first = 0
                for ref, wide in zip(grad_refs, widths):
                    sums_ref[:, first : first + wide] = nn_dot(ones, ref[...])
                    first += wide

        out = pl.pallas_call(
            body,
            grid_spec=pltpu.PrefetchScalarGridSpec(
                num_scalar_prefetch=1,
                grid=(nz,),
                in_specs=[pl.BlockSpec((tokens, span), lambda z, at_ref: (0, z))]
                + [pl.BlockSpec((tokens, wide), lambda z, at_ref: (0, 0)) for wide in widths]
                + [pl.BlockSpec((span, e.shape[1]), lambda z, at_ref: (z % (nz // 2), 0)) for e in extra],
                out_specs=[pl.BlockSpec((1, nx, rows, half), lambda z, at_ref: (z, 0, 0, 0))] * ny
                + [pl.BlockSpec((1, ny, rows, half), lambda z, at_ref: (z, 0, 0, 0))] * nx
                + [pl.BlockSpec((8, sum(widths)), lambda z, at_ref: (0, 0))],
                scratch_shapes=[pltpu.VMEM((ny, nx, rows, cols), BF)],
            ),
            out_shape=[jax.ShapeDtypeStruct((nz, nx, rows, half), BF)] * ny
            + [jax.ShapeDtypeStruct((nz, ny, rows, half), BF)] * nx
            + [jax.ShapeDtypeStruct((8, sum(widths)), F32)],
            compiler_params=pltpu.CompilerParams(vmem_limit_bytes=20 * MIB),
            cost_estimate=priced(
                flops=2 * tokens * x.shape[1] * sum(widths),
                bytes_accessed=2 * (x.size + tokens * cols + x.shape[1] * cols),
                transcendentals=0,
            ),
            name="weight_grad",
        )(self.at, x, *grads, *extra)
        return (out[:ny], out[ny : ny + nx]), out[-1][0]

    def first(self, parts):
        place = self.place
        left, right = parts
        left = [left[0]] + [place.from_y(left[r], -r) for r in range(1, place.ny)]
        right = [right[0]] + [place.from_x(right[r], -r) for r in range(1, place.nx)]
        return (left, right)

    def second(self, parts):
        place = self.place
        nz, ny, nx = scatter_sizes(place)
        left, right = parts
        rows, half = left[0].shape[2:]

        def body(at_ref, *refs):
            left_in, right_in = refs[:ny], refs[ny : ny + nx]
            left_out, right_out = refs[ny + nx : ny + 2 * nx], refs[ny + 2 * nx :]
            for r, ref in enumerate(left_out):
                to = (at_ref[1] + r) % nx
                ref[...] = sum([piece[:, to].astype(F32) for piece in left_in]).astype(BF)
            for r, ref in enumerate(right_out):
                to = (at_ref[0] + r) % ny
                ref[...] = sum([piece[:, to].astype(F32) for piece in right_in]).astype(BF)

        out = pl.pallas_call(
            body,
            grid_spec=pltpu.PrefetchScalarGridSpec(
                num_scalar_prefetch=1,
                grid=(1,),
                in_specs=[pl.BlockSpec((nz, nx, rows, half), lambda z, at_ref: (0, 0, 0, 0))] * ny
                + [pl.BlockSpec((nz, ny, rows, half), lambda z, at_ref: (0, 0, 0, 0))] * nx,
                out_specs=[pl.BlockSpec((nz, rows, half), lambda z, at_ref: (0, 0, 0))] * (nx + ny),
            ),
            out_shape=[jax.ShapeDtypeStruct((nz, rows, half), BF)] * (nx + ny),
            compiler_params=pltpu.CompilerParams(vmem_limit_bytes=20 * MIB),
            cost_estimate=priced(flops=0, bytes_accessed=8 * nz * nx * ny * rows * half, transcendentals=0),
            name="scatter_add",
        )(self.at, *left, *right)
        left, right = out[:nx], out[nx:]
        left = [left[0]] + [place.from_x(left[r], -r) for r in range(1, nx)]
        right = [right[0]] + [place.from_y(right[r], -r) for r in range(1, ny)]
        return (left, right)

    def third(self, parts):
        left, right = parts
        both = [sum([piece.astype(F32) for piece in side]) for side in (left, right)]
        column = jnp.concatenate(both, axis=-1).astype(BF)
        return column.reshape(-1, column.shape[-1])

    def along_z(self, column):
        return lax.psum_scatter(column, "ctx", scatter_dimension=0, tiled=True)


def small_scatter(place, value):
    value = value.reshape(place.nz, place.ny, place.nx, -1)

    def pick(part, axis, index):
        return lax.dynamic_index_in_dim(part, index, axis, False)

    total = pick(value, 1, place.y)
    for r in range(1, place.ny):
        total = total + place.from_y(pick(value, 1, (place.y + r) % place.ny), -r)
    value = total
    total = pick(value, 1, place.x)
    for r in range(1, place.nx):
        total = total + place.from_x(pick(value, 1, (place.x + r) % place.nx), -r)
    value = total
    total = pick(value, 0, place.ctx)
    for r in range(1, place.nz):
        pairs = [(z, (z + r) % place.nz) for z in range(place.nz)]
        total = total + lax.ppermute(pick(value, 0, (place.ctx + r) % place.nz), "ctx", pairs)
    return total


def to_pieces(place, value, steps):
    count = value.shape[0]
    groups = place.nz // count
    piece_at = place.ctx % count
    pieces = []
    for k in steps:
        sent = lax.dynamic_index_in_dim(value, (piece_at + k) % count, 0, False)
        pairs = [(z, ((z % count + k) % count) * groups + z // count) for z in range(place.nz)]
        pieces.append(sent if all(a == b for a, b in pairs) else lax.ppermute(sent, "ctx", pairs))
    return pieces


def in_positions(place, pieces):
    count = len(pieces)
    kept_seq = place.ctx // (place.nz // count)
    return place_rotated([pieces[0]] + pieces[:0:-1], kept_seq, count)


def from_sequences(place, value, steps, section=None):
    count = value.shape[0]
    groups = place.nz // count
    kept_seq = place.ctx // groups
    pieces = []
    for k in steps:
        sent = lax.dynamic_index_in_dim(value, (kept_seq - k) % count, 0, False)
        pairs = [(((z % count + k) % count) * groups + z // count, z) for z in range(place.nz)]
        if any(a != b for a, b in pairs):
            if section is None:
                sent = lax.ppermute(sent, "ctx", pairs)
            else:
                first = section * place.nz
                sent = lax.ppermute(sent, ("section", "ctx"), [(first + a, first + b) for a, b in pairs])
        pieces.append(sent)
    return pieces


def half_rows(place, value):
    half = value.shape[1] // 2
    return lax.dynamic_slice_in_dim(value, place.section * half, half, 1)


def join_pieces(place, pieces):
    count = len(pieces)
    half, width = pieces[0].shape
    mine = jnp.stack(pieces)
    other = place.sibling(mine)
    at = jnp.stack([place.ctx // (place.nz // count), place.section]).astype(jnp.int32)

    def body(at_ref, mine_ref, other_ref, out_ref):
        out_ref[0, at_ref[1]] = mine_ref[0]
        out_ref[0, 1 - at_ref[1]] = other_ref[0]

    piece = pl.BlockSpec((1, half, width), lambda k, at_ref: (k, 0, 0))
    out = pl.pallas_call(
        body,
        grid_spec=pltpu.PrefetchScalarGridSpec(
            num_scalar_prefetch=1,
            grid=(count,),
            in_specs=[piece, piece],
            out_specs=pl.BlockSpec(
                (1, 2, half, width), lambda k, at_ref: ((at_ref[0] + count - k) % count, 0, 0, 0)
            ),
        ),
        out_shape=jax.ShapeDtypeStruct((count, 2, half, width), mine.dtype),
        compiler_params=pltpu.CompilerParams(vmem_limit_bytes=10 * MIB),
        cost_estimate=priced(flops=0, bytes_accessed=8 * mine.size, transcendentals=0),
        name="join_pieces",
    )(at, mine, other)
    return out.reshape(count * 2 * half, width)


def join_halves(place, moved):
    other = place.sibling(moved)
    first = place.section == 0
    both = jnp.stack([jnp.where(first, moved, other), jnp.where(first, other, moved)], axis=1)
    return both.reshape(-1, moved.shape[-1])


def on_device(
    tokens,
    segment_ids,
    valid_mask,
    cotangent,
    qkv_weight,
    out_proj,
    in_weight,
    out_weight,
    norm_gain,
    norm_shift,
    proj_bias,
    ff_bias,
):
    place = Place()
    section = place.section
    first_section = section == 0
    micro, seqs, local, width = tokens.shape
    count = micro * seqs
    groups = place.nz // count
    rows = count * local
    head_dim = width // HEADS
    half = width // 2
    ff_width = in_weight.shape[2]
    ff_half = ff_width // 2
    chips = place.nz * place.nf
    ff_rows = out_weight.shape[1]
    ff_split = ff_rows // 2

    def part_of(which):
        qkv_part = lax.dynamic_slice_in_dim(qkv_weight[0], which * half, half, 2)
        proj_part = lax.dynamic_slice_in_dim(out_proj[0], which * half, half, 1)
        in_part = lax.dynamic_index_in_dim(
            in_weight[0].reshape(-1, chips, 2, ff_split), which, 2, False
        ).reshape(-1, ff_half)
        out_part = lax.dynamic_slice_in_dim(out_weight[0], which * ff_split, ff_split, 0)
        attn_part = jnp.concatenate([qkv_part[0], qkv_part[1], qkv_part[2], proj_part], axis=1)
        return (attn_part, in_part, out_part)

    own_parts = part_of(section)
    sent_parts = part_of(1 - section)
    shards = [[None] * 3, [None] * 3]
    for index in range(3):
        other = place.sibling(sent_parts[index])
        shards[0][index] = jnp.where(first_section, own_parts[index], other)
        shards[1][index] = jnp.where(first_section, other, own_parts[index])
    gathers = [Gather(place, shard) for layer in shards for shard in layer]

    def proj_whole(columns):
        mine = lax.dynamic_slice_in_dim(columns, section * half, half, 0)
        sent = lax.dynamic_slice_in_dim(columns, (1 - section) * half, half, 0)
        return place.in_order(mine, place.sibling(sent), 1)

    small_own = jnp.concatenate([norm_gain[0], norm_shift[0], proj_bias[0], ff_bias[0].reshape(-1, width)], axis=0)
    small_other = place.sibling(small_own)
    small = [
        jnp.where(first_section, small_own, small_other),
        jnp.where(first_section, small_other, small_own),
    ]

    def layer_small(layer):
        table = small[layer]
        gains, shifts, biases = table[0:2], table[2:4], table[4:8]
        ff_all = table[8:].reshape(chips, 2, ff_split)
        ff_part = lax.dynamic_index_in_dim(ff_all, section, 1, False).reshape(-1)
        bias_q = lax.dynamic_slice_in_dim(biases[0], section * half, half, 0)
        bias_v = lax.dynamic_slice_in_dim(biases[1], section * half, half, 0)
        bias_qkv = jnp.concatenate([bias_q, jnp.zeros_like(bias_q), bias_v])
        return gains, shifts, biases, ff_part, bias_qkv

    ids = segment_ids.reshape(count, local) * 2 + (valid_mask.reshape(count, local) == 1).astype(jnp.int32)
    ids = in_positions(place, to_pieces(place, ids, range(count))).reshape(rows)
    seg_own = ids // 2
    valid_own = ids % 2

    def over_groups(value, steps):
        pairs = []
        for z in range(place.nz):
            q, g = divmod(z, groups)
            pairs.append((q * groups + (g + steps) % groups, z))
        return lax.ppermute(value, "ctx", pairs)

    def gather_groups(value):
        return jnp.concatenate([value] + [over_groups(value, r) for r in range(1, groups)], axis=0)

    def scatter_groups(value):
        parts = value.reshape(groups, rows, -1)
        total = parts[0]
        for r in range(1, groups):
            total = total + over_groups(parts[r].astype(BF), -r).astype(F32)
        return total.astype(BF)

    code_k = gather_groups(jnp.where(valid_own == 1, seg_own, -1))[:, None]
    seg_q = seg_own[None, :]
    live = valid_own.astype(F32)[:, None]

    token_half = half_rows(place, tokens.reshape(count, local, width))
    cot_half = half_rows(place, cotangent.reshape(count, local, width))
    smalls = [layer_small(layer) for layer in range(2)]

    def project_in(layer_input, w_qkv, layer):
        return row_product(
            [layer_input],
            w_qkv,
            False,
            [],
            [smalls[layer][4][None]],
            [(half, BF)] * 3,
            lambda total, bias: jnp.split(total + bias, 3, axis=1),
            "project_qkv",
        )

    def attention(q, k, v):
        if groups > 1:
            k, v = gather_groups(k), gather_groups(v)
        mixed, lse = attend_forward(q, k, v, code_k, seg_q, head_dim)
        return q, k, v, mixed, lse

    def norm_table(*given):
        return jnp.concatenate([row[None] for row in given] + [jnp.zeros((8 - len(given), width), F32)], axis=0)

    def to_width(xs, w, transposed, name):
        (low,) = row_product(xs, w, transposed, [], [], [(width, BF)], lambda total: (total,), name)
        return low

    def attention_norm(layer_input, low, layer):
        gains, shifts, biases = smalls[layer][:3]
        table = norm_table(biases[2], gains[0], shifts[0])
        return norm_rows_forward(low, place.sibling(low), layer_input, live, table)

    def feed_in(normed_low, w_in, layer):
        activated, slope = gelu_pair(nn_dot(normed_low, w_in) + smalls[layer][3])
        return activated.astype(BF), slope.astype(BF)

    def feed_norm(normed_low, low, layer):
        gains, shifts, biases = smalls[layer][:3]
        table = norm_table(biases[3], gains[1], shifts[1])
        return norm_rows_forward(low, place.sibling(low), normed_low, live, table)

    columns, got, whole, more = [None] * 6, [None] * 6, [None] * 6, [None] * 6

    def near(at):
        got[at] = gathers[at].first(columns[at])

    def far(at):
        more[at] = gathers[at].second(got[at])

    def along_z(at):
        columns[at] = gathers[at].along_z()

    def arrived(at):
        split = 3 * half if at % 3 == 0 else columns[at].shape[2]
        whole[at] = gathers[at].whole(columns[at], got[at], more[at], split)

    def step_end(state, known):
        later = [gathers[at].shard for at in range(3, 6)]
        held = (got, more, columns[:known], later, state)
        held = tie(*held)
        got[:], more[:], columns[:known] = held[0], held[1], held[2]
        for at in range(3, 6):
            gathers[at].shard = held[3][at - 3]
        return held[4]

    token_pieces = to_pieces(place, token_half, range(2))
    along_z(0)
    token_pieces, token_half, code_k, seg_q, live = step_end((token_pieces, token_half, code_k, seg_q, live), 1)

    near(0)
    token_pieces += to_pieces(place, token_half, range(2, count))
    held = (token_pieces, gathers[1].shard, gathers[2].shard)
    token_pieces, gathers[1].shard, gathers[2].shard = step_end(held, 1)

    far(0)
    along_z(1)
    along_z(2)
    layer_input = join_pieces(place, token_pieces)
    layer_input = step_end(layer_input, 2)
    arrived(0)

    near(1)
    w_qkv, columns_proj = whole[0]
    projs = [proj_whole(columns_proj), None]
    q, k, v = project_in(layer_input, w_qkv, 0)
    along_z(3)
    columns[2], q, projs, got[1] = tie(columns[2], q, projs, got[1])
    near(2)
    attns = [attention(q, k, v), None]
    outs = [to_width([attns[0][3]], projs[0], False, "project_out"), None]
    layer_input, attns, projs, outs = step_end((layer_input, attns, projs, outs), 4)
    inputs = [layer_input, None]

    far(1)
    far(2)
    along_z(4)
    norms = [attention_norm(inputs[0], outs[0], 0), None]
    norms, cot_half = step_end((norms, cot_half), 5)
    arrived(1)
    arrived(2)

    near(3)
    along_z(5)
    feeds = [feed_in(norms[0][2], whole[1][0], 0), None]
    outs[0] = to_width([feeds[0][0]], whole[2][0], False, "feed_out")
    cot_pieces = to_pieces(place, cot_half, range(count))
    feeds, outs, cot_pieces = step_end((feeds, outs, cot_pieces), 5)

    far(3)
    near(4)
    ends = [feed_norm(norms[0][2], outs[0], 0), None]
    ends = step_end(ends, 6)
    inputs[1] = ends[0][2]
    arrived(3)

    far(4)
    near(5)
    w_qkv, columns_proj = whole[3]
    projs[1] = proj_whole(columns_proj)
    q, k, v = project_in(inputs[1], w_qkv, 1)
    attns[1] = attention(q, k, v)
    outs[1] = to_width([attns[1][3]], projs[1], False, "project_out")
    attns, projs, outs, inputs = step_end((attns, projs, outs, inputs), 6)
    arrived(4)

    far(5)
    norms[1] = attention_norm(inputs[1], outs[1], 1)
    feeds[1] = feed_in(norms[1][2], whole[4][0], 1)
    first_back = from_sequences(place, inputs[1].reshape(count, local, width), range(count - 1), 0)
    norms, feeds, first_back, first_out = step_end((norms, feeds, first_back, inputs[1]), 6)
    arrived(5)

    outs[1] = to_width([feeds[1][0]], whole[5][0], False, "feed_out")
    first_back += from_sequences(place, first_out.reshape(count, local, width), [count - 1], 0)
    outs[1], cot_pieces, norms, first_back = tie(outs[1], cot_pieces, norms, first_back)
    ends[1] = feed_norm(norms[1][2], outs[1], 1)
    terms = [join_pieces(place, cot_pieces)]

    scatter = Scatter(place)
    totals = [[None] * 3, [None] * 3]
    small_grads = [None, None]
    last_out = ends[1][2].reshape(count, local, width)
    last_back = from_sequences(place, last_out, range(count), 1)
    attn_parts = back_one = grad_one = None
    for layer in (1, 0):
        gains = smalls[layer][0]
        u = inputs[layer]
        q, k, v, mixed, lse = attns[layer]
        unit_one, inverse_one, normed_low, sums_one = norms[layer]
        activated, slope = feeds[layer]
        unit_two, inverse_two, output, sums_two = ends[layer]
        w_qkv = whole[3 * layer][0]
        w_proj, w_in, w_out = projs[layer], whole[3 * layer + 1][0], whole[3 * layer + 2][0]

        second = norm_rows_backward(terms, unit_two, inverse_two, gains[1:2], layer == 0)
        grad_ff, second_sums = second[:2]
        out_parts, _ = scatter.product(activated, [grad_ff], sums=False)
        if layer == 1:
            out_parts, grad_ff = tie(out_parts, grad_ff)
        else:
            grad_one = second[2].reshape(count, local, width)
            out_parts, grad_ff, grad_one = tie(out_parts, grad_ff, grad_one)
            back_one = from_sequences(place, grad_one, range(2), 1)

        out_parts = scatter.first(out_parts)
        (grad_hidden,) = row_product(
            [grad_ff],
            w_out,
            True,
            [slope],
            [],
            [(ff_half, BF)],
            lambda total, slope: (total * slope.astype(F32),),
            "feed_out_back",
        )
        low = to_width([grad_hidden], w_in, True, "feed_in_back")
        in_parts, hidden_sums = scatter.product(normed_low, [grad_hidden])
        low, in_parts, out_parts, attn_parts, last_back = tie(low, in_parts, out_parts, attn_parts, last_back)
        other = place.sibling(low)
        if layer == 0:
            attn_parts = scatter.second(attn_parts)

        out_parts = scatter.second(out_parts)
        in_parts = scatter.first(in_parts)
        grad_branch, first_sums = norm_rows_backward(
            [grad_ff, low, other], unit_one, inverse_one, gains[0:1], False
        )
        (grad_mixed,) = row_product(
            [grad_branch], w_proj, True, [], [], [(half, BF)], lambda total: (total,), "project_out_back"
        )
        grad_w_proj = tn_dot(mixed, grad_branch).astype(BF)
        mine = lax.dynamic_slice_in_dim(grad_w_proj, section * half, half, 1)
        sent = lax.dynamic_slice_in_dim(grad_w_proj, (1 - section) * half, half, 1)
        if layer == 0:
            attn_parts, grad_mixed, sent = tie(attn_parts, grad_mixed, sent)
            totals[1][0] = scatter.along_z(scatter.third(attn_parts))

        grad_w_proj = (mine, place.sibling(sent))
        dq, dk, dv = attend_backward(
            q, k, v, grad_mixed, lse, code_k, seg_q, head_dim, BF if groups == 1 else F32
        )
        if groups > 1:
            dk, dv = scatter_groups(dk), scatter_groups(dv)
        out_parts, in_parts, dq, dk, dv, grad_w_proj, back_one, grad_one, totals = tie(
            out_parts, in_parts, dq, dk, dv, grad_w_proj, back_one, grad_one, totals
        )

        totals[layer][2] = scatter.along_z(scatter.third(out_parts))
        in_parts = scatter.second(in_parts)
        if layer == 0:
            back_one += from_sequences(place, grad_one, range(2, count), 1)
        attn_parts, dqkv_rows = scatter.product(u, [dq, dk, dv], grad_w_proj)
        in_parts, attn_parts, dq, dk, dv = tie(in_parts, attn_parts, dq, dk, dv)
        attn_parts = scatter.first(attn_parts)
        in_column = scatter.third(in_parts)
        low = to_width([dq, dk, dv], w_qkv, True, "project_qkv_back")
        low, in_column = tie(low, in_column)
        totals[layer][1] = scatter.along_z(in_column)
        other = place.sibling(low)
        terms = [grad_branch, low, other]

        here = jnp.where(section == layer, 1.0, 0.0)
        spread = jnp.zeros((2, 2, half), F32)
        spread = lax.dynamic_update_slice(spread, dqkv_rows[:half][None, None], (0, section, 0))
        spread = lax.dynamic_update_slice(spread, dqkv_rows[2 * half :][None, None], (1, section, 0))
        ff_spread = lax.dynamic_update_slice(
            jnp.zeros((chips, 2, ff_split), F32), hidden_sums.reshape(chips, 1, ff_split), (0, section, 0)
        )
        rest = jnp.stack(
            [first_sums[0], second_sums[0], first_sums[1], second_sums[1], first_sums[2], second_sums[2]]
        )
        by_chip = jnp.concatenate([here * rest, spread.reshape(2, width)], axis=0).reshape(8, chips, -1)
        by_chip = jnp.moveaxis(by_chip, 1, 0).reshape(chips, -1)
        squares = jnp.concatenate([jnp.sum(sums_one[:2], axis=1), jnp.sum(sums_two[1:3], axis=1)])
        squares = here * jnp.concatenate([squares, jnp.sum(live)[None], jnp.zeros((3,), F32)])
        small_grads[layer] = jnp.concatenate(
            [by_chip, ff_spread.reshape(chips, -1), jnp.broadcast_to(squares, (chips, 8))], axis=1
        )

    grad_zero = sum([term.astype(F32) for term in terms]).astype(BF).reshape(count, local, width)
    back_zero = from_sequences(place, grad_zero, range(count), 0)
    mine = jnp.where(first_section, small_grads[0], small_grads[1])
    sent = jnp.where(first_section, small_grads[1], small_grads[0])
    small_rows = mine + place.sibling(sent)
    attn_parts, small_rows, first_back, last_back, back_one, grad_zero = tie(
        attn_parts, small_rows, first_back, last_back, back_one, grad_zero
    )
    attn_parts = scatter.second(attn_parts)
    small_total = small_scatter(place, small_rows)
    attn_parts, back_zero = tie(attn_parts, back_zero)
    totals[0][0] = scatter.along_z(scatter.third(attn_parts))

    def give_back(pieces):
        return place_rotated(pieces, place.ctx % count, count).reshape(1, micro, seqs, local, width)

    activations = give_back([jnp.where(first_section, a, b) for a, b in zip(first_back, last_back)])
    input_grads = give_back([jnp.where(first_section, a, b) for a, b in zip(back_zero, back_one)])

    def halves(index):
        a, b = totals[0][index], totals[1][index]
        mine = jnp.where(first_section, a, b)
        other = place.sibling(jnp.where(first_section, b, a))
        low, high = jnp.where(first_section, mine, other), jnp.where(first_section, other, mine)
        return low.astype(F32), high.astype(F32)

    attn_rows = width // chips
    low, high = halves(0)
    low = low.reshape(attn_rows, 4, half)
    high = high.reshape(attn_rows, 4, half)
    attn = jnp.concatenate([low, high], axis=2)
    grad_qkv = jnp.moveaxis(attn[:, :3], 1, 0)[None]
    grad_out_proj = attn[:, 3][None]
    low, high = halves(1)
    grad_in_weight = jnp.stack(
        [low.reshape(-1, chips, ff_split), high.reshape(-1, chips, ff_split)], axis=2
    ).reshape(1, -1, ff_width)
    low, high = halves(2)
    grad_out_weight = jnp.concatenate([low, high], axis=0)[None]

    per_chip = width // chips
    table = small_total[: 8 * per_chip].reshape(8, per_chip)
    grad_gain = table[0:2][None]
    grad_shift = table[2:4][None]
    grad_proj_bias = jnp.stack([table[6], table[7], table[4], table[5]])[None]
    grad_ff_bias = small_total[8 * per_chip : 8 * per_chip + ff_rows][None]
    sums = small_total[8 * per_chip + ff_rows :]
    rms = jnp.sqrt(sums[:4] / (sums[4] * width))[None]
    return (
        activations,
        input_grads,
        grad_qkv,
        grad_out_proj,
        grad_in_weight,
        grad_out_weight,
        grad_gain,
        grad_shift,
        grad_proj_bias,
        grad_ff_bias,
        rms,
    )


def solution(mesh):
    placed = (
        P(None, "fsdp", "ctx", None),
        P(None, "fsdp", "ctx"),
        P(None, "fsdp", "ctx"),
        P(None, "fsdp", "ctx", None),
        P("section", None, ("ctx", "fsdp"), None),
        P("section", ("ctx", "fsdp"), None),
        P("section", ("ctx", "fsdp"), None),
        P("section", ("ctx", "fsdp"), None),
        P("section", None, None),
        P("section", None, None),
        P("section", None, None),
        P("section", None),
    )
    return jax.shard_map(
        on_device,
        mesh=mesh,
        in_specs=placed,
        out_specs=(
            P("section", None, "fsdp", "ctx", None),
            P("section", None, "fsdp", "ctx", None),
            P("section", None, ("ctx", "fsdp"), None),
            P("section", ("ctx", "fsdp"), None),
            P("section", ("ctx", "fsdp"), None),
            P("section", ("ctx", "fsdp"), None),
            P("section", None, ("ctx", "fsdp")),
            P("section", None, ("ctx", "fsdp")),
            P("section", None, ("ctx", "fsdp")),
            P("section", ("ctx", "fsdp")),
            P("section", None),
        ),
        check_vma=False,
    )
```
